32 devices in a mesh: dp: 8 (over z, x), img: 4 (over y, core).
Axes of the slice: x: 2, y: 2, z: 4, core: 2. Of those that a mesh axis runs over, the one named last changes fastest.
Arguments:
- image: bfloat16 [8, 16, 64, 512], P('dp', 'img'), may hold values from -6 to 6
- cond: bfloat16 [8, 2048], P('dp'), may hold values from -6 to 6
- context: bfloat16 [8, 81, 2048], P('dp'), may hold values from -6 to 6
- w_conv1: bfloat16 [4608, 512], P(('dp', 'img')), may hold values from -0.09375 to 0.09375
- w_conv2: bfloat16 [4608, 512], P(('dp', 'img')), may hold values from -0.09375 to 0.09375
- w_embed: bfloat16 [2048, 1024], P(('dp', 'img')), may hold values from -0.125 to 0.125
- w_qkv: bfloat16 [512, 1536], P(('dp', 'img')), may hold values from -0.25 to 0.25
- w_context: bfloat16 [2048, 1024], P(('dp', 'img')), may hold values from -0.125 to 0.125
- w_out: bfloat16 [512, 512], P(('dp', 'img')), may hold values from -6 to 6
- vectors: bfloat16 [16, 512], P(None, ('dp', 'img')), may hold values from -1.5 to 1.75, as said below
- cotangent: bfloat16 [8, 16, 64, 512], P('dp', 'img'), may hold values from -6 to 6
Outputs:
- output: bfloat16 [8, 16, 64, 512], P('dp', 'img')
- in_grad: bfloat16 [8, 16, 64, 512], P('dp', 'img')
- g_conv1: float32 [4608, 512], P(('dp', 'img'))
- g_conv2: float32 [4608, 512], P(('dp', 'img'))
- g_embed: float32 [2048, 1024], P(('dp', 'img'))
- g_qkv: float32 [512, 1536], P(('dp', 'img'))
- g_context: float32 [2048, 1024], P(('dp', 'img'))
- g_out: float32 [512, 512], P(('dp', 'img'))
- g_vectors: float32 [16, 512], P(None, ('dp', 'img'))
The draws below stay inside these ranges and needn't reach their ends.
Inputs may be any that keep to these rules, and one draw needn't show every extreme that they name: `vectors`: rows 0, 3 and 6 lie between 0.25 and 1.75, the others between -1.5 and 1.5.
All inputs are finite; a program needn't handle non-finite values.
Results may differ from the reference program's by a relative error of at most 0.014.
Values may be sent and summed in bfloat16 or wider, within the bound.
A program may use at most 192 MiB of HBM per device.

```python
import jax
import jax.numpy as jnp
from jax import lax

C = 512
HEADS = 8
HEAD = 64
GROUPS = 32
EMB = 2048
XF = 2048
CTXT = 81
COLS = 64
HEIGHT = 16
IMAGES = 8


def draw_vectors(key, part):
    noise = jax.random.normal(key, (16, C), jnp.float32)
    rows = jnp.arange(16)[:, None]
    gain_rows = (rows == 0) | (rows == 3) | (rows == 6)
    gains = 1.0 + 0.3 * jnp.clip(noise, -2.5, 2.5)
    biases = 0.5 * jnp.clip(noise, -3.0, 3.0)
    return jnp.where(gain_rows, gains, biases).astype(jnp.bfloat16)


def levels(key, shape, pieces, least, high):
    def one(axis_at, shards_of):
        draws = jax.random.uniform(jax.random.fold_in(jax.random.fold_in(key, 6), axis_at), (shards_of,), jnp.float32, least / len(pieces), high / len(pieces))
        return jnp.repeat(jnp.exp(draws), shape[axis_at] // shards_of).reshape((-1,) + (1,) * (len(shape) - axis_at - 1))

    gain = one(*pieces[0])
    for cut in pieces[1:]:
        gain = gain * one(*cut)
    return gain


def bell_draw(stream_key, extent, scale, bound, cuts=(), dtype=jnp.bfloat16):
    values = scale * jax.random.normal(stream_key, extent, jnp.float32)
    if cuts:
        values = values * levels(stream_key, extent, cuts, -0.22, 0.18)
    return jnp.clip(values, -bound, bound).astype(dtype)


def setup_inputs(seed: int = 0) -> dict:
    seeds = jax.random.split(jax.random.key(seed), 12)
    return {
        "image": bell_draw(seeds[0], (IMAGES, HEIGHT, COLS, C), 1.0, 6.0, ((0, 8), (1, 4))),
        "cond": bell_draw(seeds[1], (IMAGES, EMB), 1.0, 6.0, ((0, 8),)),
        "context": bell_draw(seeds[2], (IMAGES, CTXT, XF), 1.0, 6.0, ((0, 8),)),
        "w_conv1": bell_draw(seeds[3], (9 * C, C), (9 * C) ** -0.5, 0.09375, ((0, 32),)),
        "w_conv2": bell_draw(seeds[4], (9 * C, C), (9 * C) ** -0.5, 0.09375, ((0, 32),)),
        "w_embed": bell_draw(seeds[5], (EMB, 2 * C), EMB ** -0.5, 0.125, ((0, 32),)),
        "w_qkv": bell_draw(seeds[6], (C, 3 * C), C ** -0.5, 0.25, ((0, 32),)),
        "w_context": bell_draw(seeds[7], (XF, 2 * C), XF ** -0.5, 0.125, ((0, 32),)),
        "w_out": bell_draw(seeds[8], (C, C), (max(C // 512, 1)) ** -0.5, 6.0, ((0, 32),)),
        "vectors": draw_vectors(jax.random.fold_in(seeds[11], 71), 0),
        "cotangent": bell_draw(seeds[10], (IMAGES, HEIGHT, COLS, C), 1.0, 6.0, ((0, 8), (1, 4))),
    }


highest = lax.Precision.HIGHEST

@jax.custom_vjp
def low(v):
    return lax.optimization_barrier(v.astype(jnp.bfloat16)).astype(jnp.float32)

@jax.custom_vjp
def low_back(v):
    return v

def low_keep(v):
    return (low(v), None)

def low_pass(kept, grad):
    return (grad,)

def back_keep(v):
    return (v, None)

def back_low(kept, grad):
    return (low(grad),)
low.defvjp(low_keep, low_pass)
low_back.defvjp(back_keep, back_low)

def product(left, right):
    return jnp.dot(left, right, precision=highest, preferred_element_type=jnp.float32)

def group_norm(flat):
    pixels, chans = flat.shape
    part = flat.reshape(pixels, GROUPS, chans // GROUPS)
    mean = lax.optimization_barrier(jnp.mean(part, axis=(0, 2), keepdims=True))
    spread = lax.optimization_barrier(jnp.mean(jnp.square(part - mean), axis=(0, 2), keepdims=True))
    return ((part - mean) * lax.rsqrt(spread + 1e-05)).reshape(pixels, chans)

def convolve(field, kernel):
    chans = field.shape[-1]
    kernel4 = kernel.reshape(3, 3, chans, kernel.shape[-1])
    result = lax.conv_general_dilated(field[None], kernel4, (1, 1), 'SAME', dimension_numbers=('NHWC', 'HWIO', 'NHWC'), precision=highest)
    return result[0]

def forward(params, image, cond, context):
    w_conv1, w_conv2, w_embed, w_qkv, w_context, w_out, vec = params
    rows, cols, chans = image.shape
    pixels = rows * cols
    flat = image.reshape(pixels, chans)
    pre1 = group_norm(flat) * vec[0] + vec[1]
    act1 = low(jax.nn.silu(pre1))
    hid1 = low_back(convolve(act1.reshape(rows, cols, chans), w_conv1).reshape(pixels, chans) + vec[2])
    cond_act = low(jax.nn.silu(cond))
    embed = product(cond_act[None], w_embed)[0]
    scale = embed[:chans] + vec[14]
    shift = embed[chans:] + vec[15]
    normed2 = group_norm(hid1) * vec[3] + vec[4]
    act2 = low(jax.nn.silu(normed2 * (1.0 + scale) + shift))
    hid2 = low_back(convolve(act2.reshape(rows, cols, chans), w_conv2).reshape(pixels, chans) + vec[5])
    resid = flat + hid2
    normed3 = low(group_norm(resid) * vec[6] + vec[7])
    qkv = low(low_back(product(normed3, w_qkv) + jnp.concatenate([vec[9], vec[10], vec[11]])))
    ctx = low(product(context, w_context) + jnp.concatenate([vec[12], vec[13]]))
    query = qkv[:, :chans].reshape(pixels, HEADS, HEAD)
    keys = jnp.concatenate([ctx[:, :chans], qkv[:, chans:2 * chans]], 0).reshape(-1, HEADS, HEAD)
    values = jnp.concatenate([ctx[:, chans:], qkv[:, 2 * chans:]], 0).reshape(-1, HEADS, HEAD)
    scores = low_back(jnp.einsum('phd,khd->hpk', query, keys, precision=highest) * HEAD ** (-0.5))
    probs = jax.nn.softmax(scores, axis=-1)
    mixed = jnp.einsum('hpk,khd->phd', low(probs), values, precision=highest)
    mixed = low(low_back(mixed.reshape(pixels, chans)))
    return (resid + product(mixed, w_out) + vec[8]).reshape(rows, cols, chans)

def reference(image, cond, context, w_conv1, w_conv2, w_embed, w_qkv, w_context, w_out, vectors, cotangent):
    params = tuple((w.astype(jnp.float32) for w in (w_conv1, w_conv2, w_embed, w_qkv, w_context, w_out, vectors)))

    def one_image(carry, item):
        picture, embedding, tokens, grad_out = item
        embedding = embedding.astype(jnp.float32)
        tokens = tokens.astype(jnp.float32)

        def local(weights, field):
            return forward(weights, field, embedding, tokens)
        result, pull = jax.vjp(local, params, picture.astype(jnp.float32))
        grad_params, grad_field = pull(grad_out.astype(jnp.float32))
        carry = tuple((total + part for total, part in zip(carry, grad_params)))
        return (carry, (result.astype(jnp.bfloat16), grad_field.astype(jnp.bfloat16)))
    zeros = tuple((jnp.zeros_like(w) for w in params))
    grads, (outputs, in_grads) = lax.scan(one_image, zeros, (image, cond, context, cotangent))
    return (outputs, in_grads, grads[0], grads[1], grads[2], grads[3], grads[4], grads[5], grads[6])
```

```python
import jax
import jax.numpy as jnp
from jax import lax
from jax.sharding import PartitionSpec as P

HEADS = 8
HEAD = 64
GROUPS = 32

f32 = jnp.float32
bf16 = jnp.bfloat16
highest = lax.Precision.HIGHEST


def dot(a, b):
    return jnp.dot(a, b, preferred_element_type=f32)


def silu_slope(value):
    sigma = jax.nn.sigmoid(value)
    return sigma * (1.0 + value * (1.0 - sigma))


def group_norm(flat, size):
    pixels, chans = flat.shape
    part = flat.reshape(pixels, chans // size, size)
    mean = jnp.mean(part, axis=(0, 2), keepdims=True)
    spread = jnp.mean(jnp.square(part - mean), axis=(0, 2), keepdims=True)
    inverse = lax.rsqrt(spread + 1e-05)
    return ((part - mean) * inverse).reshape(pixels, chans), inverse


def group_back(grad, normed, inverse, size):
    pixels, chans = grad.shape
    upper = grad.reshape(pixels, chans // size, size)
    lower = normed.reshape(pixels, chans // size, size)
    first = jnp.mean(upper, axis=(0, 2), keepdims=True)
    second = jnp.mean(upper * lower, axis=(0, 2), keepdims=True)
    return ((upper - first - lower * second) * inverse).reshape(pixels, chans)


def taps_of(flat, rows, cols, flipped):
    chans = flat.shape[-1]
    padded = jnp.pad(flat.reshape(rows, cols, chans), ((1, 1), (1, 1), (0, 0)))
    pieces = []
    for r in range(3):
        for c in range(3):
            top, left = (2 - r, 2 - c) if flipped else (r, c)
            pieces.append(padded[top : top + rows, left : left + cols].reshape(rows * cols, chans))
    return jnp.concatenate(pieces, 1)


def columns(weight, parts):
    rows, chans = weight.shape
    return weight.reshape(rows, chans // (parts * 128), parts, 128).transpose(2, 1, 0, 3).reshape(parts, -1, 128)


def on_device(
    image, cond, context, w_conv1, w_conv2, w_embed, w_qkv, w_context, w_out, vectors, cotangent
):
    parts = lax.axis_size("img")
    place = lax.axis_index("img")
    images = lax.axis_size("dp")
    rows, cols, chans = image.shape[1] * parts, image.shape[2], image.shape[3]
    pixels = rows * cols
    width = chans // parts
    size = chans // GROUPS
    count = images * parts

    def own(full):
        return lax.dynamic_slice_in_dim(full, place * width, width, full.ndim - 1)

    shards = (w_conv1, w_conv2, w_qkv, w_context, w_embed, w_out)
    lengths = [w.shape[0] * (w.shape[1] // chans) for w in shards]
    packed = jnp.concatenate([columns(w, parts) for w in shards], 1)
    packed = lax.all_to_all(packed, "img", 0, 0, tiled=True)
    packed = lax.all_gather(packed, "dp", axis=0, tiled=True)
    full = []
    start = 0
    for w, length in zip(shards, lengths):
        wide = w.shape[1] // chans
        piece = packed[:, start : start + length].reshape(count, wide, w.shape[0], width)
        full.append(piece.transpose(0, 2, 1, 3).reshape(count * w.shape[0], wide * width))
        start += length
    k1, k2, kq, kc, ke, ko = full
    vec_all = lax.all_gather(vectors, ("dp", "img"), axis=1, tiled=True).astype(f32)
    vec = own(vec_all)

    x_low = lax.all_gather(image[0].reshape(-1, chans), "img", axis=0, tiled=True)
    x_all = x_low.astype(f32)
    normed1_all, inverse1_all = group_norm(x_all, size)
    act1 = jax.nn.silu(normed1_all * vec_all[0] + vec_all[1]).astype(bf16)
    normed1 = own(normed1_all)
    inverse1 = lax.dynamic_slice_in_dim(inverse1_all, place * (GROUPS // parts), GROUPS // parts, 1)
    pre1 = normed1 * vec[0] + vec[1]
    hidden1 = dot(taps_of(act1, rows, cols, False), k1) + vec[2]
    cond_act = jax.nn.silu(cond.astype(f32)).astype(bf16)
    embed = dot(cond_act, ke)[0]
    scale = embed[:width] + vec[14]
    shift = embed[width:] + vec[15]
    normed2, inverse2 = group_norm(hidden1, size)
    affine2 = normed2 * vec[3] + vec[4]
    pre2 = affine2 * (1.0 + scale) + shift
    act2_own = jax.nn.silu(pre2).astype(bf16)
    act2 = lax.all_gather(act2_own, "img", axis=1, tiled=True)
    resid = own(x_all) + dot(taps_of(act2, rows, cols, False), k2) + vec[5]
    normed3, inverse3 = group_norm(resid, size)
    affine3_own = (normed3 * vec[6] + vec[7]).astype(bf16)
    affine3 = lax.all_gather(affine3_own, "img", axis=1, tiled=True)
    qkv = (dot(affine3, kq) + jnp.concatenate([vec[9], vec[10], vec[11]])).astype(bf16)
    ctx = (dot(context[0], kc) + jnp.concatenate([vec[12], vec[13]])).astype(bf16)
    tokens = ctx.shape[0]

    out_full = lax.all_gather(ko, "img", axis=1, tiled=True)
    dy_px = cotangent[0].reshape(-1, chans)
    do_px = lax.dot_general(dy_px, out_full, (((1,), (1,)), ((), ())), preferred_element_type=f32).astype(bf16)
    both = jnp.stack([do_px, dy_px])
    both = lax.all_to_all(both, "img", 2, 1, tiled=True)
    do, dy = both[0], both[1]
    dy_wide = dy.astype(f32)

    keys = jnp.concatenate([ctx[:, :width], qkv[:, width : 2 * width]], 0)
    values = jnp.concatenate([ctx[:, width:], qkv[:, 2 * width :]], 0)
    factor = HEAD ** (-0.5)
    mixed, dq, dk, dv = [], [], [], []
    for h in range(width // HEAD):
        at = slice(h * HEAD, (h + 1) * HEAD)
        q_h, k_h, v_h, do_h = qkv[:, at], keys[:, at], values[:, at], do[:, at]
        scores = dot(k_h, q_h.T) * factor
        top = jnp.max(scores, 0, keepdims=True)
        weights = jnp.exp(scores - top)
        probs = weights / jnp.sum(weights, 0, keepdims=True)
        low = probs.astype(bf16)
        mixed.append(dot(v_h.T, low).T)
        dv.append(dot(low, do_h))
        dp = dot(v_h, do_h.T)
        ds = (probs * (dp - jnp.sum(dp * probs, 0, keepdims=True))).astype(bf16)
        dq.append(dot(k_h.T, ds).T * factor)
        dk.append(dot(ds, q_h) * factor)
    mixed = jnp.concatenate(mixed, 1).astype(bf16)
    dq, dk, dv = (jnp.concatenate(v, 1) for v in (dq, dk, dv))
    mixed_all = lax.all_gather(mixed, "img", axis=1, tiled=True)
    output = (resid + dot(mixed_all, ko) + vec[8]).astype(bf16)

    dqkv = jnp.concatenate([dq, dk[tokens:], dv[tokens:]], 1).astype(bf16)
    dctx = jnp.concatenate([dk[:tokens], dv[:tokens]], 1)
    dn_part = lax.dot_general(dqkv, kq, (((1,), (1,)), ((), ())), preferred_element_type=f32)
    dn = lax.psum_scatter(dn_part.astype(bf16), "img", scatter_dimension=1, tiled=True).astype(f32)
    dy1 = dy_wide + group_back(dn * vec[6], normed3, inverse3, size)
    dh2 = dy1.astype(bf16)

    def turned(kernel):
        return kernel.reshape(9, chans, width).transpose(0, 2, 1).reshape(9 * width, chans)

    def conv_back(dh, kernel, act):
        field = taps_of(dh, rows, cols, True)
        part = dot(field, turned(kernel)).astype(bf16)
        grad = lax.psum_scatter(part, "img", scatter_dimension=1, tiled=True).astype(f32)
        kernel_grad = lax.dot_general(act, field, (((0,), (0,)), ((), ())), preferred_element_type=f32)
        return grad, kernel_grad.reshape(chans, 9, width).transpose(1, 0, 2).reshape(9 * chans, width)

    da2, gk2 = conv_back(dh2, k2, act2)
    du = da2 * silu_slope(pre2)
    dscale = jnp.sum(du * affine2, 0)
    dshift = jnp.sum(du, 0)
    dz = du * (1.0 + scale)
    dh1 = group_back(dz * vec[3], normed2, inverse2, size).astype(bf16)
    da1, gk1 = conv_back(dh1, k1, act1)
    dt1 = da1 * silu_slope(pre1)
    in_grad = (dy1 + group_back(dt1 * vec[0], normed1, inverse1, size)).astype(bf16)

    tops = lax.all_to_all(jnp.stack([output, in_grad]), "img", 1, 2, tiled=True)
    gkq = lax.dot_general(affine3, dqkv, (((0,), (0,)), ((), ())), preferred_element_type=f32)
    gkc = lax.dot_general(context[0], dctx.astype(bf16), (((0,), (0,)), ((), ())), preferred_element_type=f32)
    gko = lax.dot_general(mixed_all, dy, (((0,), (0,)), ((), ())), preferred_element_type=f32)
    gke = cond_act[0].astype(f32)[:, None] * jnp.concatenate([dscale, dshift])[None, :]
    grad_vec = jnp.stack(
        [
            jnp.sum(dt1 * normed1, 0),
            jnp.sum(dt1, 0),
            jnp.sum(dh1.astype(f32), 0),
            jnp.sum(dz * normed2, 0),
            jnp.sum(dz, 0),
            jnp.sum(dh2.astype(f32), 0),
            jnp.sum(dn * normed3, 0),
            jnp.sum(dn, 0),
            jnp.sum(dy_wide, 0),
        ]
        + [jnp.sum(v.astype(f32), 0) for v in jnp.split(dqkv, 3, 1)]
        + [jnp.sum(v, 0) for v in jnp.split(dctx, 2, 1)]
        + [dscale, dshift],
        0,
    )
    grads = (gk1, gk2, gkq, gkc, gke, gko)
    pieces = []
    for w, g in zip(shards, grads):
        wide = w.shape[1] // chans
        piece = g.reshape(count, w.shape[0], wide, width).transpose(0, 2, 1, 3)
        pieces.append(piece.reshape(count, wide * w.shape[0], width))
    packed = jnp.concatenate(pieces, 1).astype(bf16)
    packed = lax.psum_scatter(packed, "dp", scatter_dimension=0, tiled=True).astype(f32)
    packed = lax.all_to_all(packed.astype(bf16), "img", 0, 0, tiled=True).astype(f32)
    outs = []
    start = 0
    for w, length in zip(shards, lengths):
        wide = w.shape[1] // chans
        piece = packed[:, start : start + length].reshape(parts, wide, w.shape[0], width)
        outs.append(piece.transpose(2, 1, 0, 3).reshape(w.shape))
        start += length
    vec_sum = lax.all_gather(lax.psum(grad_vec, "dp"), "img", axis=1, tiled=True)
    each = chans // count
    g_vec = lax.dynamic_slice_in_dim(
        vec_sum, (lax.axis_index("dp") * parts + place) * each, each, 1
    )
    g1, g2, gq, gc, ge, go = outs
    return (tops[0].reshape(image.shape), tops[1].reshape(image.shape), g1, g2, ge, gq, gc, go, g_vec)


def solution(mesh):
    whole = P(("dp", "img"), None)
    field = P("dp", "img", None, None)
    in_specs = (
        field, P("dp", None), P("dp", None, None), whole, whole, whole, whole, whole, whole,
        P(None, ("dp", "img")), field,
    )
    out_specs = (field, field, whole, whole, whole, whole, whole, whole, P(None, ("dp", "img")))
    return jax.shard_map(
        on_device, mesh=mesh, in_specs=in_specs, out_specs=out_specs, check_vma=False
    )
```

```python
import functools
import types

import jax
import jax.numpy as jnp
from jax import lax
from jax.experimental import pallas as pl
from jax.experimental.pallas import tpu as pltpu
from jax.sharding import PartitionSpec as P

HEADS = 8
HEAD = 64
GROUPS = 32

f32 = jnp.float32
bf16 = jnp.bfloat16
highest = lax.Precision.HIGHEST


def dot(a, b):
    return jnp.dot(a, b, preferred_element_type=f32)


def silu_slope(value):
    sigma = jax.nn.sigmoid(value)
    return sigma * (1.0 + value * (1.0 - sigma))


def group_norm(flat, size):
    pixels, chans = flat.shape
    part = flat.reshape(pixels, chans // size, size)
    mean = jnp.mean(part, axis=(0, 2), keepdims=True)
    spread = jnp.mean(jnp.square(part - mean), axis=(0, 2), keepdims=True)
    inverse = lax.rsqrt(spread + 1e-05)
    return ((part - mean) * inverse).reshape(pixels, chans), inverse


def group_back(grad, normed, inverse, size):
    pixels, chans = grad.shape
    upper = grad.reshape(pixels, chans // size, size)
    lower = normed.reshape(pixels, chans // size, size)
    first = jnp.mean(upper, axis=(0, 2), keepdims=True)
    second = jnp.mean(upper * lower, axis=(0, 2), keepdims=True)
    return ((upper - first - lower * second) * inverse).reshape(pixels, chans)


def taps_of(flat, rows, cols, flipped):
    chans = flat.shape[-1]
    padded = jnp.pad(flat.reshape(rows, cols, chans), ((1, 1), (1, 1), (0, 0)))
    pieces = []
    for r in range(3):
        for c in range(3):
            top, left = (2 - r, 2 - c) if flipped else (r, c)
            pieces.append(padded[top : top + rows, left : left + cols].reshape(rows * cols, chans))
    return jnp.concatenate(pieces, 1)


def columns(weight, parts):
    rows, chans = weight.shape
    return weight.reshape(rows, chans // (parts * 128), parts, 128).transpose(2, 1, 0, 3).reshape(parts, -1, 128)


class Wires:
    def __init__(self, sent, landed):
        self.sent, self.landed, self.copies = sent, landed, []

    def send(self, source, target, device):
        at = len(self.copies)
        copy = pltpu.make_async_remote_copy(
            src_ref=source, dst_ref=target, send_sem=self.sent.at[at], recv_sem=self.landed.at[at],
            device_id=device, device_id_type=pl.DeviceIdType.MESH,
        )
        copy.start()
        self.copies.append(copy)
        return copy

    def drain(self):
        for copy in self.copies:
            copy.wait_send()


def scratch_plan(g):
    P, Q, C, B, N, J, X = g.P, g.Q, g.C, g.B, g.N, g.J, g.X
    plan = dict(
        X=((J, Q, C), bf16), vown=((16, C), bf16), vs1=((J, 16, C), bf16),
        vsum=((16, C), bf16), vs2=((N, 16, C), bf16), vecs=((J, 16, B), f32),
        eall=((N, 1, g.E), f32), wemb=((2 * g.RE, 2 * C), bf16), epart=((N, 1, 2 * C), f32),
        erx=((N, 1, 2 * C), f32), esum=((J, 1, 2 * C), f32), emb=((1, 2 * C), f32),
        A1=((2, P + 2 * g.COLS, 2 * B), bf16), A2=((2, P + 2 * g.COLS, 2 * B), bf16),
        N3=((2, P, 2 * B), bf16), O=((2, P, 2 * B), bf16),
        A1T=((C, P), bf16), A2T=((C, P), bf16), N3T=((C, P), bf16), OT=((C, P), bf16),
        st1=((J, 8, B), f32), xj=((P, B), bf16),
        h1=((P, B), f32), y1=((P, B), f32), dy1=((P, B), f32), tmp=((P, B), f32),
        W1T=((2, 9 * B, 2 * B), bf16), W2T=((2, 9 * B, 2 * B), bf16), WqT=((2, 3 * B, 2 * B), bf16),
        ctx=((B, X), bf16), ctxT=((X, B), bf16),
        Kb=((P + B, B), bf16), Vb=((P + B, B), bf16), KT=((B, P + B), bf16), VT=((B, P + B), bf16),
        qs=((P, B), bf16), dK=((P + B, B), f32), dV=((P + B, B), f32), dqkv=((3, P, B), bf16),
        WoF=((2, C, 2 * B), bf16), dopx=((Q, C), bf16), doj=((P, B), bf16), dyj=((P, B), bf16),
        outj=((P, B), bf16), inj=((P, B), bf16),
        S=((3, P + 2 * g.COLS, B), bf16),
        dse=((J, 2, B), f32), dsall=((N, J, 2, B), f32), geb=((2 * g.RE, 2 * C), f32),
        gvec=((16, B), f32), gvs=((N, 16, B), f32), gvi=((J, 16, B), f32), gvt=((16, B), f32),
    )
    half = dict(ps=((2, 2, P, B), bf16), rc=((2, P, B), bf16), sy=((P, B), bf16), ry=((P, B), bf16))
    groups = [plan, half, half, half]
    for wide, rows in g.weights:
        depth = rows * J
        groups.append(dict(
            w=((wide, depth * N, B), bf16), g=((wide, depth * N, B), bf16),
            rx=((N // 2, wide, depth, B), bf16), zs=((N // 2, wide, depth, B), bf16),
            zr=((N // 2, wide, depth, B), bf16), fin=((wide, depth, B), bf16), gr=((J, wide, rows, B), bf16),
        ))
    return groups


def body(g, groups, *refs):
    (x_in, cond, ctx_in, w1, w2, w_emb, w_q, w_c, w_o, vec_in, dy_in) = refs[:11]
    (out, in_grad, gc1, gc2, g_emb, g_q, g_c, g_o, g_v) = refs[11:20]
    left = list(refs[20:-2])
    spaces = [types.SimpleNamespace(**{name: left.pop(0) for name in group}) for group in groups]
    s, dn_bufs, da2_bufs, da1_bufs = spaces[:4]
    c1, c2, wq, wc, wo = spaces[4:]
    for weight, shape, ref in zip(spaces[4:], g.weights, (w1, w2, w_q, w_c, w_o)):
        weight.wide, weight.rows, weight.ref = shape[0], shape[1], ref
        weight.depth = weight.rows * g.J
    rest = (wq, wc, wo)
    P, Q, C, B, N, J, COLS, SIZE = g.P, g.Q, g.C, g.B, g.N, g.J, g.COLS, g.SIZE
    T, E, RE = g.T, g.E, g.RE
    Z = N // 2
    STEPS = P // Q
    wires = Wires(refs[-2], refs[-1])
    send = wires.send
    d = lax.axis_index("dp")
    j = lax.axis_index("img")
    flat = d * J + j
    z, xx = lax.div(d, 2), lax.rem(d, 2)
    yy, cc = lax.div(j, 2), lax.rem(j, 2)
    sib = (d, yy * 2 + (1 - cc))
    ypeer = (d, (1 - yy) * 2 + cc)
    diag = (d, (1 - yy) * 2 + (1 - cc))
    img_peers = [ypeer, diag, sib]
    dp_peers = [(lax.rem(d + k, N), j) for k in range(1, N)]
    zdev = [lax.rem(z + k, Z) for k in range(Z)]
    zsrc = [lax.rem(z + Z - k, Z) for k in range(Z)]
    xpeer = (z * 2 + (1 - xx), j)

    def lanes(k):
        return pl.ds(pl.multiple_of(k * B, B), B)

    def rows_at(start, size, unit):
        return pl.ds(pl.multiple_of(start, unit), size)

    def px(i):
        return pl.ds(pl.multiple_of(i * Q, Q), Q)

    def each(fn, init=None):
        if init is None:
            lax.fori_loop(0, STEPS, lambda i, carry: (fn(i), carry)[1], 0)
            return None
        return lax.fori_loop(0, STEPS, fn, init)

    def mm(a, b):
        return jnp.dot(a, b, preferred_element_type=f32)

    def mm_t(a, b):
        return lax.dot_general(a, b, (((1,), (1,)), ((), ())), preferred_element_type=f32)

    lane8 = lax.broadcasted_iota(jnp.int32, (8, B), 1)

    def group_sum(row):
        v = jnp.broadcast_to(row, (8, B))
        step = 1
        while step < SIZE:
            down, up = pltpu.roll(v, B - step, 1), pltpu.roll(v, step, 1)
            v = v + jnp.where((lane8 & step) == 0, down, up)
            step *= 2
        return v[0:1]

    def colsum(v):
        return jnp.sum(v, axis=0, keepdims=True)

    zero_row = jnp.zeros((1, B), f32)
    count = P * SIZE

    def moments(load):
        total = each(lambda i, a: a + colsum(load(i)), zero_row)
        mean = group_sum(total) * (1.0 / count)
        spread = each(lambda i, a: a + colsum(jnp.square(load(i) - mean)), zero_row)
        return mean, lax.rsqrt(group_sum(spread) * (1.0 / count) + 1e-05)

    col = lax.rem(lax.broadcasted_iota(jnp.int32, (Q, B), 0), COLS)

    def from_left(v):
        return jnp.where(col == 0, 0.0, pltpu.roll(v, 1, 0))

    def from_right(v):
        return jnp.where(col == COLS - 1, 0.0, pltpu.roll(v, Q - 1, 0))

    hot = lax.broadcasted_iota(jnp.int32, (16, C), 1) == (
        lax.broadcasted_iota(jnp.int32, (16, C), 0) + flat * g.VW
    )
    hot = jnp.where(hot, 1.0, 0.0).astype(bf16)
    own_vec = mm(vec_in[...], hot).astype(bf16)
    s.vown[...] = own_vec
    s.vs1[j] = own_vec
    e_own = cond[...].astype(f32)
    e_own = (e_own * jax.nn.sigmoid(e_own)).astype(bf16).astype(f32)
    s.eall[d] = e_own

    barrier = pltpu.get_barrier_semaphore()
    for device in img_peers + dp_peers:
        pl.semaphore_signal(barrier, inc=1, device_id=device, device_id_type=pl.DeviceIdType.MESH)
    pl.semaphore_wait(barrier, len(img_peers) + len(dp_peers))

    def stage_img(W):
        start = d * W.depth + j * W.rows
        W.img = []
        for device in img_peers:
            for t in range(W.wide):
                source = W.ref.at[:, rows_at(t * C + device[1] * B, B, B)]
                W.img.append(send(source, W.w.at[t, rows_at(start, W.rows, 16), :], device))

    def own_img(W):
        start = d * W.depth + j * W.rows
        for t in range(W.wide):
            W.w[t, rows_at(start, W.rows, 16), :] = W.ref[:, rows_at(t * C + j * B, B, B)]

    def block(W, ref, owner):
        return ref.at[:, rows_at(owner * W.depth, W.depth, 16), :]

    def stage_z(W):
        for copy in W.img:
            copy.wait_recv()
        mine = block(W, W.w, d)
        W.z = [send(mine, mine, (zdev[k] * 2 + xx, j)) for k in range(1, Z)]
        W.x = [send(mine, mine, xpeer)]

    def forward(W):
        for k, copy in enumerate(W.z, 1):
            copy.wait_recv()
            here = block(W, W.w, zsrc[k] * 2 + xx)
            W.x.append(send(here, here, xpeer))

    def arrive(W):
        for copy in W.x:
            copy.wait_recv()

    def gather_start(mine):
        return types.SimpleNamespace(y=send(mine, mine, ypeer), c=send(mine, mine, sib))

    def gather_near(state):
        state.c.wait_recv()

    def gather_far(state, theirs):
        state.y.wait_recv()
        state.f = send(theirs, theirs, sib)

    def gather_end(state):
        state.f.wait_recv()

    stage_img(c1)
    v_stage1 = [send(s.vown, s.vs1.at[j], device) for device in img_peers]
    x_own = s.X.at[j]
    x_state = types.SimpleNamespace(y=send(x_in, x_own, ypeer), c=send(x_in, x_own, sib))
    e_stage1 = [send(s.eall.at[d], s.eall.at[d], device) for device in dp_peers]
    own_img(c1)
    s.X[j] = x_in[...]
    for W in (c2, *rest):
        own_img(W)
    for buf in (s.A1, s.A2):
        for h in range(2):
            buf[h, 0:COLS, :] = jnp.zeros((COLS, 2 * B), bf16)
            buf[h, P + COLS : P + 2 * COLS, :] = jnp.zeros((COLS, 2 * B), bf16)
    for c in range(3):
        s.S[c, 0:COLS, :] = jnp.zeros((COLS, B), bf16)
        s.S[c, P + COLS : P + 2 * COLS, :] = jnp.zeros((COLS, B), bf16)
    s.ctx[...] = jnp.zeros((B, g.X), bf16)
    s.ctx[0:T, :] = ctx_in[...]
    stage_z(c1)
    for copy in v_stage1:
        copy.wait_recv()
    total = s.vs1[0].astype(f32)
    for k in range(1, J):
        total = total + s.vs1[k].astype(f32)
    s.vsum[...] = total.astype(bf16)
    s.vs2[d] = total.astype(bf16)
    v_stage2 = [send(s.vsum, s.vs2.at[d], device) for device in dp_peers]

    x_state.y.wait_recv()
    far = s.X.at[(1 - yy) * 2 + cc]
    x_state.f = send(far, far, sib)
    for W in (c2, *rest):
        stage_img(W)
    dy_copies = [
        send(dy_in.at[:, lanes(device[1])], s.dyj.at[rows_at(j * Q, Q, Q), :], device) for device in img_peers
    ]
    s.dyj[rows_at(j * Q, Q, Q), :] = dy_in[:, lanes(j)]

    for copy in e_stage1:
        copy.wait_recv()
    s.wemb[...] = jnp.zeros((2 * RE, 2 * C), bf16)
    s.wemb[rows_at(lax.rem(flat, 2) * RE, RE, 16), :] = w_emb[...]
    e_at = rows_at(lax.div(flat, 2) * (2 * RE), 2 * RE, B)
    e_rows = jnp.concatenate([s.eall[k, :, e_at] for k in range(N)], axis=0)
    part = mm(e_rows.astype(bf16), s.wemb[...])
    for k in range(N):
        s.epart[k] = part[k : k + 1]
    s.erx[d] = s.epart[d]
    e_stage2 = [send(s.epart.at[device[0]], s.erx.at[d], device) for device in dp_peers]

    x_state.c.wait_recv()
    x_state.f.wait_recv()

    def load_x(k):
        return lambda i: s.X[i, :, k * B : (k + 1) * B].astype(f32)

    for k in range(J):
        mean, inverse = moments(load_x(k))
        s.st1[k, 0:1, :] = mean
        s.st1[k, 1:2, :] = inverse
    for copy in e_stage2:
        copy.wait_recv()
    total = s.erx[0]
    for k in range(1, N):
        total = total + s.erx[k]
    s.esum[j] = total
    e_stage3 = [send(s.esum.at[j], s.esum.at[j], device) for device in img_peers]
    for copy in v_stage2:
        copy.wait_recv()
    total = s.vs2[0].astype(f32)
    for k in range(1, N):
        total = total + s.vs2[k].astype(f32)
    for k in range(J):
        s.vecs[k] = total[:, k * B : (k + 1) * B]

    def vec(row):
        return s.vecs[j, row : row + 1, :]

    forward(c1)
    for k in range(J):
        mean, inverse = s.st1[k, 0:1, :], s.st1[k, 1:2, :]
        gain, bias = s.vecs[k, 0:1, :], s.vecs[k, 1:2, :]
        load = load_x(k)

        def act(i):
            t1 = (load(i) - mean) * inverse * gain + bias
            a1 = t1 * jax.nn.sigmoid(t1)
            s.A1[k // 2, rows_at(i * Q + COLS, Q, COLS), (k % 2) * B : (k % 2 + 1) * B] = a1.astype(bf16)

        each(act)

    def turn(source, target, offset):
        def one(i):
            for h in range(2):
                v = source[h, rows_at(i * Q + offset, Q, 16), :]
                target[h * 2 * B : (h + 1) * 2 * B, px(i)] = v.T
        each(one)

    each(lambda i: s.xj.__setitem__((px(i), slice(None)), s.X[i, :, lanes(j)]))
    turn(s.A1, s.A1T, COLS)
    for copy in e_stage3:
        copy.wait_recv()
    total = s.esum[0]
    for k in range(1, J):
        total = total + s.esum[k]
    s.emb[...] = total
    scale = 1.0 + (s.emb[:, lanes(j)] + vec(14))
    shift = s.emb[:, lanes(j + J)] + vec(15)
    stage_z(c2)
    arrive(c1)

    def convolve(A, W, emit):
        def one(i):
            left = jnp.concatenate(
                [A[h, rows_at(i * Q + r * COLS, Q, COLS), :] for r in range(3) for h in range(2)], axis=1
            )
            right = jnp.concatenate(
                [
                    jnp.concatenate([W[0, (3 * r + c) * C : (3 * r + c + 1) * C, :] for r in range(3)], axis=0)
                    for c in range(3)
                ],
                axis=1,
            )
            p = mm(left, right)
            emit(i, p[:, B : 2 * B] + from_left(p[:, :B]) + from_right(p[:, 2 * B :]))
        each(one)

    def save_h1(i, v):
        s.h1[px(i), :] = v + vec(2)

    convolve(s.A1, c1.w, save_h1)
    mean2, inv2 = moments(lambda i: s.h1[px(i), :])

    def xh2(i):
        return (s.h1[px(i), :] - mean2) * inv2

    def u_of(i):
        return (xh2(i) * vec(3) + vec(4)) * scale + shift

    def act2(i):
        u = u_of(i)
        s.A2[yy, rows_at(i * Q + COLS, Q, COLS), lanes(cc)] = (u * jax.nn.sigmoid(u)).astype(bf16)

    each(act2)
    inside = pl.ds(COLS, P)
    a2_state = gather_start(s.A2.at[yy, inside, lanes(cc)])
    forward(c2)
    for W in rest:
        stage_z(W)
    gather_far(a2_state, s.A2.at[1 - yy, inside, lanes(cc)])
    gather_near(a2_state)
    gather_end(a2_state)
    arrive(c2)

    def save_y1(i, v):
        s.y1[px(i), :] = s.xj[px(i), :].astype(f32) + v + vec(5)

    convolve(s.A2, c2.w, save_y1)
    mean3, inv3 = moments(lambda i: s.y1[px(i), :])

    def xh3(i):
        return (s.y1[px(i), :] - mean3) * inv3

    def act3(i):
        s.N3[yy, px(i), lanes(cc)] = (xh3(i) * vec(6) + vec(7)).astype(bf16)

    each(act3)
    n_state = gather_start(s.N3.at[yy, :, lanes(cc)])
    for W in rest:
        forward(W)
    turn(s.A2, s.A2T, COLS)

    def turn_weights(W, target, taps, stride):
        for h in range(2):
            for t in range(taps):
                v = W(t)[rows_at(h * 2 * B, 2 * B, 16), :]
                target[h, t * B : (t + 1) * B, :] = v.T

    def conv_tap(W):
        return lambda t: W.w.at[0, pl.ds(t * C, C), :]

    turn_weights(conv_tap(c2), s.W2T, 9, C)
    gather_far(n_state, s.N3.at[1 - yy, :, lanes(cc)])
    turn_weights(conv_tap(c1), s.W1T, 9, C)
    s.ctxT[...] = s.ctx[...].T
    for W in rest:
        arrive(W)
    wo_at = s.WoF.at[yy, :, lanes(cc)]
    s.WoF[yy, :, lanes(cc)] = wo.w[0]
    wo_state = gather_start(wo_at)
    turn_weights(lambda t: wq.w.at[t], s.WqT, 3, C)
    tokens = lax.broadcasted_iota(jnp.int32, (B, B), 0) < T
    for t, target in enumerate((s.Kb, s.Vb)):
        v = mm(s.ctx[...], wc.w[t]) + vec(12 + t)
        target[P : P + B, :] = jnp.where(tokens, v, 0.0).astype(bf16)
    gather_far(wo_state, s.WoF.at[1 - yy, :, lanes(cc)])
    gather_near(wo_state)
    gather_end(wo_state)
    for h in range(2):
        part = mm_t(dy_in[:, 0 : 2 * B], s.WoF[0, h * 2 * B : (h + 1) * 2 * B, :])
        part = part + mm_t(dy_in[:, 2 * B : 4 * B], s.WoF[1, h * 2 * B : (h + 1) * 2 * B, :])
        s.dopx[:, h * 2 * B : (h + 1) * 2 * B] = part.astype(bf16)
    do_copies = [
        send(s.dopx.at[:, lanes(device[1])], s.doj.at[rows_at(j * Q, Q, Q), :], device)
        for device in img_peers
    ]
    s.doj[rows_at(j * Q, Q, Q), :] = s.dopx[:, lanes(j)]
    gather_near(n_state)
    gather_end(n_state)

    def project(i):
        left = jnp.concatenate([s.N3[0, px(i), :], s.N3[1, px(i), :]], axis=1)
        right = jnp.concatenate([wq.w[t] for t in range(3)], axis=1)
        v = mm(left, right)
        q = (v[:, :B] + vec(9)).astype(bf16)
        s.qs[px(i), :] = (q.astype(f32) * g.FACTOR).astype(bf16)
        s.Kb[px(i), :] = (v[:, B : 2 * B] + vec(10)).astype(bf16)
        s.Vb[px(i), :] = (v[:, 2 * B :] + vec(11)).astype(bf16)

    each(project)
    for source, target in ((s.Kb, s.KT), (s.Vb, s.VT)):
        for k in range(0, P + B, B):
            target[:, k : k + B] = source[k : k + B, :].T
    for copy in do_copies + dy_copies:
        copy.wait_recv()
    s.dK[...] = jnp.zeros((P + B, B), f32)
    s.dV[...] = jnp.zeros((P + B, B), f32)

    HEAD_ = g.HEAD
    lane_row = lax.broadcasted_iota(jnp.int32, (1, B), 1)
    known = lax.broadcasted_iota(jnp.int32, (B, Q), 0) < T

    def attend(i):
        q_i, do_i = s.qs[px(i), :], s.doj[px(i), :]
        q_m, do_m, low, slope, mixed, back = [], [], [], [], [], []
        for h in range(B // HEAD_):
            keep = jnp.where(lax.div(lane_row, HEAD_) == h, 1.0, 0.0).astype(bf16)
            qm, dom = q_i * keep, do_i * keep
            scores = mm_t(s.Kb[...], qm)
            scores = jnp.concatenate([scores[:P], jnp.where(known, scores[P:], -1e30)], axis=0)
            top = jnp.max(scores, axis=0, keepdims=True)
            e = jnp.exp(scores - top)
            probs = e * (1.0 / jnp.sum(e, axis=0, keepdims=True))
            pb = probs.astype(bf16)
            mixed.append(mm(s.VT[h * HEAD_ : (h + 1) * HEAD_, :], pb))
            dp = mm_t(s.Vb[...], dom)
            inner = jnp.sum(dp * probs, axis=0, keepdims=True)
            ds = (probs * (dp - inner)).astype(bf16)
            back.append(mm(s.KT[h * HEAD_ : (h + 1) * HEAD_, :], ds))
            q_m.append(qm)
            do_m.append(dom)
            low.append(pb)
            slope.append(ds)
        s.dV[...] += mm(jnp.concatenate(low, axis=1), jnp.concatenate(do_m, axis=0))
        s.dK[...] += mm(jnp.concatenate(slope, axis=1), jnp.concatenate(q_m, axis=0))
        s.O[yy, px(i), lanes(cc)] = jnp.concatenate(mixed, axis=0).T.astype(bf16)
        s.dqkv[0, px(i), :] = (jnp.concatenate(back, axis=0).T * g.FACTOR).astype(bf16)

    each(attend)
    o_state = gather_start(s.O.at[yy, :, lanes(cc)])

    def grads_kv(i):
        s.dqkv[1, px(i), :] = s.dK[px(i), :].astype(bf16)
        s.dqkv[2, px(i), :] = s.dV[px(i), :].astype(bf16)

    each(grads_kv)

    def scatter(bufs, left, right):
        ps, rc, sy, ry = bufs.ps, bufs.rc, bufs.sy, bufs.ry
        near = []
        for slot in range(2):
            half = 1 - yy if slot == 0 else yy

            def one(i):
                v = mm(left(i), right[half]).astype(bf16)
                ps[slot, 0, px(i), :] = v[:, :B]
                ps[slot, 1, px(i), :] = v[:, B:]

            each(one)
            near.append(send(ps.at[slot, 1 - cc], rc.at[slot], sib))
            if slot == 0:
                near[0].wait_recv()

                def add(i):
                    v = ps[0, cc, px(i), :].astype(f32) + rc[0, px(i), :].astype(f32)
                    sy[px(i), :] = v.astype(bf16)

                each(add)
                across = send(sy, ry, ypeer)

        def done():
            near[1].wait_recv()
            across.wait_recv()

        def load(i):
            v = ps[1, cc, px(i), :].astype(f32) + rc[1, px(i), :].astype(f32)
            return v + ry[px(i), :].astype(f32)

        return done, load

    order = list(range(1, Z)) + [0]

    def sum_start(W):
        W.sx = {}
        for k in order:
            W.sx[k] = send(block(W, W.g, zdev[k] * 2 + (1 - xx)), W.rx.at[k], xpeer)

    def sum_z(W):
        W.sz = {}
        for k in order:
            W.sx[k].wait_recv()
            at = rows_at((zdev[k] * 2 + xx) * W.depth, W.depth, 16)
            v = W.g[:, at, :].astype(f32) + W.rx[k].astype(f32)
            W.zs[k] = v.astype(bf16)
            if k:
                W.sz[k] = send(W.zs.at[k], W.zr.at[k], (zdev[k] * 2 + xx, j))

    def sum_img(W):
        v = W.zs[0].astype(f32)
        for k in range(1, Z):
            W.sz[k].wait_recv()
            v = v + W.zr[k].astype(f32)
        W.fin[...] = v.astype(bf16)
        W.simg = [
            send(W.fin.at[:, rows_at(device[1] * W.rows, W.rows, 16), :], W.gr.at[j], device)
            for device in img_peers
        ]
        W.gr[j] = W.fin[:, rows_at(j * W.rows, W.rows, 16), :]

    def sum_end(W, target):
        for copy in W.simg:
            copy.wait_recv()
        for k in range(J):
            for t in range(W.wide):
                target[:, t * C + k * B : t * C + (k + 1) * B] = W.gr[k, t].astype(f32)

    dn_done, dn_at = scatter(
        dn_bufs, lambda i: jnp.concatenate([s.dqkv[t, px(i), :] for t in range(3)], axis=1), s.WqT
    )
    turn(s.N3, s.N3T, 0)
    for h in range(2):
        at = slice(h * 2 * B, (h + 1) * 2 * B)
        v = mm(s.N3T[at, :], jnp.concatenate([s.dqkv[t] for t in range(3)], axis=1)).astype(bf16)
        for t in range(3):
            wq.g[t, at, :] = v[:, t * B : (t + 1) * B]
    sum_start(wq)
    d_ctx = jnp.concatenate([s.dK[P : P + B, :], s.dV[P : P + B, :]], axis=1).astype(bf16)
    X_ = g.X
    for k in range(0, X_, C):
        v = mm(s.ctxT[k : k + C, :], d_ctx).astype(bf16)
        wc.g[0, k : k + C, :] = v[:, :B]
        wc.g[1, k : k + C, :] = v[:, B:]
    sum_start(wc)
    gather_far(o_state, s.O.at[1 - yy, :, lanes(cc)])
    gather_near(o_state)
    gather_end(o_state)

    def finish(i):
        left = jnp.concatenate([s.O[0, px(i), :], s.O[1, px(i), :]], axis=1)
        s.outj[px(i), :] = (s.y1[px(i), :] + mm(left, wo.w[0]) + vec(8)).astype(bf16)

    each(finish)

    def to_pixels(source, target):
        copies = [
            send(source.at[rows_at(device[1] * Q, Q, Q), :], target.at[:, lanes(j)], device) for device in img_peers
        ]
        target[:, lanes(j)] = source[rows_at(j * Q, Q, Q), :]
        return copies

    out_copies = to_pixels(s.outj, out)
    turn(s.O, s.OT, 0)
    for h in range(2):
        at = slice(h * 2 * B, (h + 1) * 2 * B)
        wo.g[0, at, :] = mm(s.OT[at, :], s.dyj[...]).astype(bf16)
    sum_start(wo)

    def back_sums(grad, normed, factor):
        def one(i, carry):
            v = grad(i)
            return carry[0] + colsum(v), carry[1] + colsum(v * normed(i))
        first, second = each(one, (zero_row, zero_row))
        return first, second, group_sum(first * factor) * (1.0 / count), group_sum(second * factor) * (1.0 / count)

    dn_done()
    dn_sum, dn_hat, m1, m2 = back_sums(dn_at, xh3, vec(6))

    def shifted(i, v):
        at = rows_at(i * Q + COLS, Q, COLS)
        s.S[0, at, :] = from_right(v).astype(bf16)
        s.S[1, at, :] = v.astype(bf16)
        s.S[2, at, :] = from_left(v).astype(bf16)

    def make_dh2(i, carry):
        dy = s.dyj[px(i), :].astype(f32)
        v = dy + (dn_at(i) * vec(6) - m1 - xh3(i) * m2) * inv3
        s.dy1[px(i), :] = v
        low = v.astype(bf16).astype(f32)
        shifted(i, low)
        return carry[0] + colsum(low), carry[1] + colsum(dy)

    dh2_sum, dy_sum = each(make_dh2, (zero_row, zero_row))

    def tap(t, start, size):
        r, c = t // 3, t % 3
        return s.S[c, rows_at(start + (2 - r) * COLS, size, COLS), :]

    def field(i):
        return jnp.concatenate([tap(t, i * Q, Q) for t in range(9)], axis=1)

    def kernel_grad(W, turned):
        for h in range(2):
            at = slice(h * 2 * B, (h + 1) * 2 * B)
            v = mm(turned[at, :], jnp.concatenate([tap(t, 0, P) for t in range(9)], axis=1)).astype(bf16)
            for t in range(9):
                W.g[0, t * C + h * 2 * B : t * C + (h + 1) * 2 * B, :] = v[:, t * B : (t + 1) * B]

    da2_done, da2_at = scatter(da2_bufs, field, s.W2T)
    kernel_grad(c2, s.A2T)
    sum_z(wq)
    sum_z(wc)
    sum_z(wo)
    sum_start(c2)
    da2_done()

    def slope_of(v):
        sigma = jax.nn.sigmoid(v)
        return sigma * (1.0 + v * (1.0 - sigma))

    def make_du(i, carry):
        du = da2_at(i) * slope_of(u_of(i))
        s.tmp[px(i), :] = du
        return carry[0] + colsum(du), carry[1] + colsum(du * xh2(i))

    du_sum, du_hat = each(make_du, (zero_row, zero_row))
    gain2 = scale * vec(3)
    m1b = group_sum(du_sum * gain2) * (1.0 / count)
    m2b = group_sum(du_hat * gain2) * (1.0 / count)

    def make_dh1(i, carry):
        v = (s.tmp[px(i), :] * gain2 - m1b - xh2(i) * m2b) * inv2
        low = v.astype(bf16).astype(f32)
        shifted(i, low)
        return carry + colsum(low)

    dh1_sum = each(make_dh1, zero_row)
    dscale = vec(3) * du_hat + vec(4) * du_sum
    da1_done, da1_at = scatter(da1_bufs, field, s.W1T)
    kernel_grad(c1, s.A1T)
    sum_start(c1)
    s.dse[j] = jnp.concatenate([dscale, du_sum], axis=0)
    ds_copies = [send(s.dse.at[j], s.dse.at[j], device) for device in img_peers]
    for W in rest:
        sum_img(W)
    sum_z(c2)
    for copy in ds_copies:
        copy.wait_recv()
    s.dsall[d] = s.dse[...]
    ds_copies = [send(s.dse, s.dsall.at[d], device) for device in dp_peers]
    da1_done()
    mean1, inv1 = s.st1[j, 0:1, :], s.st1[j, 1:2, :]

    def xh1(i):
        return (s.xj[px(i), :].astype(f32) - mean1) * inv1

    def make_dt1(i, carry):
        n1 = xh1(i)
        dt1 = da1_at(i) * slope_of(n1 * vec(0) + vec(1))
        s.tmp[px(i), :] = dt1
        return carry[0] + colsum(dt1), carry[1] + colsum(dt1 * n1)

    dt1_sum, dt1_hat = each(make_dt1, (zero_row, zero_row))
    m1c = group_sum(dt1_sum * vec(0)) * (1.0 / count)
    m2c = group_sum(dt1_hat * vec(0)) * (1.0 / count)

    def make_in(i):
        v = s.dy1[px(i), :] + (s.tmp[px(i), :] * vec(0) - m1c - xh1(i) * m2c) * inv1
        s.inj[px(i), :] = v.astype(bf16)

    each(make_in)
    in_copies = to_pixels(s.inj, in_grad)

    qkv_sums = [each(lambda i, a, t=t: a + colsum(s.dqkv[t, px(i), :].astype(f32)), zero_row) for t in range(3)]
    s.gvec[...] = jnp.concatenate(
        [dt1_hat, dt1_sum, dh1_sum, scale * du_hat, scale * du_sum, dh2_sum, dn_hat, dn_sum, dy_sum]
        + qkv_sums
        + [colsum(s.dK[P : P + B, :]), colsum(s.dV[P : P + B, :]), dscale, du_sum],
        axis=0,
    )
    gv_copies = [send(s.gvec, s.gvs.at[d], device) for device in dp_peers]
    s.gvs[d] = s.gvec[...]
    sum_z(c1)
    for copy in gv_copies:
        copy.wait_recv()
    total = s.gvs[0]
    for k in range(1, N):
        total = total + s.gvs[k]
    s.gvt[...] = total
    s.gvi[j] = total
    gv_copies = [send(s.gvt, s.gvi.at[j], device) for device in img_peers]
    sum_img(c2)
    sum_end(wq, g_q)
    sum_end(wc, g_c)
    sum_end(wo, g_o)
    for copy in ds_copies:
        copy.wait_recv()
    e_cols = jnp.concatenate([s.eall[k, :, e_at] for k in range(N)], axis=0)
    for t in range(2):
        for k in range(J):
            rows = jnp.concatenate([s.dsall[i, k, t : t + 1, :] for i in range(N)], axis=0)
            v = lax.dot_general(
                e_cols, rows, (((0,), (0,)), ((), ())), precision=highest, preferred_element_type=f32
            )
            s.geb[:, t * C + k * B : t * C + (k + 1) * B] = v
    g_emb[...] = s.geb[rows_at(lax.rem(flat, 2) * RE, RE, 8), :]
    for copy in gv_copies:
        copy.wait_recv()
    VW = g.VW
    each_block = B // VW
    pick = lax.broadcasted_iota(jnp.int32, (B, VW), 0) == (
        lax.broadcasted_iota(jnp.int32, (B, VW), 1) + lax.rem(flat, each_block) * VW
    )
    g_v[...] = jnp.dot(
        s.gvi[lax.div(flat, each_block)], jnp.where(pick, 1.0, 0.0), precision=highest,
        preferred_element_type=f32,
    )
    sum_end(c2, gc2)
    sum_img(c1)
    sum_end(c1, gc1)
    for copy in out_copies + in_copies:
        copy.wait_recv()
    wires.drain()


def fused(
    image, cond, context, w_conv1, w_conv2, w_embed, w_qkv, w_context, w_out, vectors, cotangent
):
    J, N = lax.axis_size("img"), lax.axis_size("dp")
    local, cols, chans = image.shape[1:]
    g = types.SimpleNamespace(
        P=local * cols * J, Q=local * cols, C=chans, B=chans // J, N=N, J=J, COLS=cols, SIZE=chans // GROUPS,
        T=context.shape[1], X=context.shape[2], E=cond.shape[1], RE=w_embed.shape[0], VW=vectors.shape[1],
        HEAD=HEAD, FACTOR=HEAD ** (-0.5),
        weights=[
            (1, w_conv1.shape[0]), (1, w_conv2.shape[0]), (3, w_qkv.shape[0]), (2, w_context.shape[0]),
            (1, w_out.shape[0]),
        ],
    )
    groups = scratch_plan(g)
    rows = local * cols
    shape = jax.ShapeDtypeStruct
    outs = [
        shape((rows, chans), bf16), shape((rows, chans), bf16), shape(w_conv1.shape, f32), shape(w_conv2.shape, f32),
        shape(w_embed.shape, f32), shape(w_qkv.shape, f32), shape(w_context.shape, f32), shape(w_out.shape, f32),
        shape(vectors.shape, f32),
    ]
    copies = 256
    vmem = pl.BlockSpec(memory_space=pltpu.VMEM)
    result = pl.pallas_call(
        functools.partial(body, g, groups),
        out_shape=outs,
        in_specs=[vmem] * 11,
        out_specs=[vmem] * 9,
        scratch_shapes=[pltpu.VMEM(*spec) for group in groups for spec in group.values()]
        + [pltpu.SemaphoreType.DMA((copies,)), pltpu.SemaphoreType.DMA((copies,))],
        compiler_params=pltpu.CompilerParams(
            collective_id=0, has_side_effects=True, vmem_limit_bytes=60 * 1024 * 1024
        ),
    )(
        image.reshape(rows, chans), cond, context[0], w_conv1, w_conv2, w_embed, w_qkv, w_context, w_out, vectors,
        cotangent.reshape(rows, chans),
    )
    return (result[0].reshape(image.shape), result[1].reshape(image.shape), *result[2:])


def on_device(
    image, cond, context, w_conv1, w_conv2, w_embed, w_qkv, w_context, w_out, vectors, cotangent
):
    parts = lax.axis_size("img")
    place = lax.axis_index("img")
    images = lax.axis_size("dp")
    rows, cols, chans = image.shape[1] * parts, image.shape[2], image.shape[3]
    pixels = rows * cols
    width = chans // parts
    size = chans // GROUPS
    count = images * parts

    if parts == 4 and width == 128 and images % 2 == 0 and all(
        w.shape[0] % 16 == 0 for w in (w_conv1, w_conv2, w_embed, w_qkv, w_context, w_out)
    ):
        return fused(
            image, cond, context, w_conv1, w_conv2, w_embed, w_qkv, w_context, w_out, vectors, cotangent
        )

    def own(full):
        return lax.dynamic_slice_in_dim(full, place * width, width, full.ndim - 1)

    shards = (w_conv1, w_conv2, w_qkv, w_context, w_embed, w_out)
    lengths = [w.shape[0] * (w.shape[1] // chans) for w in shards]
    packed = jnp.concatenate([columns(w, parts) for w in shards], 1)
    packed = lax.all_to_all(packed, "img", 0, 0, tiled=True)
    packed = lax.all_gather(packed, "dp", axis=0, tiled=True)
    full = []
    start = 0
    for w, length in zip(shards, lengths):
        wide = w.shape[1] // chans
        piece = packed[:, start : start + length].reshape(count, wide, w.shape[0], width)
        full.append(piece.transpose(0, 2, 1, 3).reshape(count * w.shape[0], wide * width))
        start += length
    k1, k2, kq, kc, ke, ko = full
    vec_all = lax.all_gather(vectors, ("dp", "img"), axis=1, tiled=True).astype(f32)
    vec = own(vec_all)

    x_low = lax.all_gather(image[0].reshape(-1, chans), "img", axis=0, tiled=True)
    x_all = x_low.astype(f32)
    normed1_all, inverse1_all = group_norm(x_all, size)
    act1 = jax.nn.silu(normed1_all * vec_all[0] + vec_all[1]).astype(bf16)
    normed1 = own(normed1_all)
    inverse1 = lax.dynamic_slice_in_dim(inverse1_all, place * (GROUPS // parts), GROUPS // parts, 1)
    pre1 = normed1 * vec[0] + vec[1]
    hidden1 = dot(taps_of(act1, rows, cols, False), k1) + vec[2]
    cond_act = jax.nn.silu(cond.astype(f32)).astype(bf16)
    embed = dot(cond_act, ke)[0]
    scale = embed[:width] + vec[14]
    shift = embed[width:] + vec[15]
    normed2, inverse2 = group_norm(hidden1, size)
    affine2 = normed2 * vec[3] + vec[4]
    pre2 = affine2 * (1.0 + scale) + shift
    act2_own = jax.nn.silu(pre2).astype(bf16)
    act2 = lax.all_gather(act2_own, "img", axis=1, tiled=True)
    resid = own(x_all) + dot(taps_of(act2, rows, cols, False), k2) + vec[5]
    normed3, inverse3 = group_norm(resid, size)
    affine3_own = (normed3 * vec[6] + vec[7]).astype(bf16)
    affine3 = lax.all_gather(affine3_own, "img", axis=1, tiled=True)
    qkv = (dot(affine3, kq) + jnp.concatenate([vec[9], vec[10], vec[11]])).astype(bf16)
    ctx = (dot(context[0], kc) + jnp.concatenate([vec[12], vec[13]])).astype(bf16)
    tokens = ctx.shape[0]

    out_full = lax.all_gather(ko, "img", axis=1, tiled=True)
    dy_px = cotangent[0].reshape(-1, chans)
    do_px = lax.dot_general(dy_px, out_full, (((1,), (1,)), ((), ())), preferred_element_type=f32).astype(bf16)
    both = jnp.stack([do_px, dy_px])
    both = lax.all_to_all(both, "img", 2, 1, tiled=True)
    do, dy = both[0], both[1]
    dy_wide = dy.astype(f32)

    keys = jnp.concatenate([ctx[:, :width], qkv[:, width : 2 * width]], 0)
    values = jnp.concatenate([ctx[:, width:], qkv[:, 2 * width :]], 0)
    factor = HEAD ** (-0.5)
    mixed, dq, dk, dv = [], [], [], []
    for h in range(width // HEAD):
        at = slice(h * HEAD, (h + 1) * HEAD)
        q_h, k_h, v_h, do_h = qkv[:, at], keys[:, at], values[:, at], do[:, at]
        scores = dot(k_h, q_h.T) * factor
        top = jnp.max(scores, 0, keepdims=True)
        weights = jnp.exp(scores - top)
        probs = weights / jnp.sum(weights, 0, keepdims=True)
        low = probs.astype(bf16)
        mixed.append(dot(v_h.T, low).T)
        dv.append(dot(low, do_h))
        dp = dot(v_h, do_h.T)
        ds = (probs * (dp - jnp.sum(dp * probs, 0, keepdims=True))).astype(bf16)
        dq.append(dot(k_h.T, ds).T * factor)
        dk.append(dot(ds, q_h) * factor)
    mixed = jnp.concatenate(mixed, 1).astype(bf16)
    dq, dk, dv = (jnp.concatenate(v, 1) for v in (dq, dk, dv))
    mixed_all = lax.all_gather(mixed, "img", axis=1, tiled=True)
    output = (resid + dot(mixed_all, ko) + vec[8]).astype(bf16)

    dqkv = jnp.concatenate([dq, dk[tokens:], dv[tokens:]], 1).astype(bf16)
    dctx = jnp.concatenate([dk[:tokens], dv[:tokens]], 1)
    dn_part = lax.dot_general(dqkv, kq, (((1,), (1,)), ((), ())), preferred_element_type=f32)
    dn = lax.psum_scatter(dn_part.astype(bf16), "img", scatter_dimension=1, tiled=True).astype(f32)
    dy1 = dy_wide + group_back(dn * vec[6], normed3, inverse3, size)
    dh2 = dy1.astype(bf16)

    def turned(kernel):
        return kernel.reshape(9, chans, width).transpose(0, 2, 1).reshape(9 * width, chans)

    def conv_back(dh, kernel, act):
        field = taps_of(dh, rows, cols, True)
        part = dot(field, turned(kernel)).astype(bf16)
        grad = lax.psum_scatter(part, "img", scatter_dimension=1, tiled=True).astype(f32)
        kernel_grad = lax.dot_general(act, field, (((0,), (0,)), ((), ())), preferred_element_type=f32)
        return grad, kernel_grad.reshape(chans, 9, width).transpose(1, 0, 2).reshape(9 * chans, width)

    da2, gk2 = conv_back(dh2, k2, act2)
    du = da2 * silu_slope(pre2)
    dscale = jnp.sum(du * affine2, 0)
    dshift = jnp.sum(du, 0)
    dz = du * (1.0 + scale)
    dh1 = group_back(dz * vec[3], normed2, inverse2, size).astype(bf16)
    da1, gk1 = conv_back(dh1, k1, act1)
    dt1 = da1 * silu_slope(pre1)
    in_grad = (dy1 + group_back(dt1 * vec[0], normed1, inverse1, size)).astype(bf16)

    tops = lax.all_to_all(jnp.stack([output, in_grad]), "img", 1, 2, tiled=True)
    gkq = lax.dot_general(affine3, dqkv, (((0,), (0,)), ((), ())), preferred_element_type=f32)
    gkc = lax.dot_general(context[0], dctx.astype(bf16), (((0,), (0,)), ((), ())), preferred_element_type=f32)
    gko = lax.dot_general(mixed_all, dy, (((0,), (0,)), ((), ())), preferred_element_type=f32)
    gke = cond_act[0].astype(f32)[:, None] * jnp.concatenate([dscale, dshift])[None, :]
    grad_vec = jnp.stack(
        [
            jnp.sum(dt1 * normed1, 0),
            jnp.sum(dt1, 0),
            jnp.sum(dh1.astype(f32), 0),
            jnp.sum(dz * normed2, 0),
            jnp.sum(dz, 0),
            jnp.sum(dh2.astype(f32), 0),
            jnp.sum(dn * normed3, 0),
            jnp.sum(dn, 0),
            jnp.sum(dy_wide, 0),
        ]
        + [jnp.sum(v.astype(f32), 0) for v in jnp.split(dqkv, 3, 1)]
        + [jnp.sum(v, 0) for v in jnp.split(dctx, 2, 1)]
        + [dscale, dshift],
        0,
    )
    grads = (gk1, gk2, gkq, gkc, gke, gko)
    pieces = []
    for w, g in zip(shards, grads):
        wide = w.shape[1] // chans
        piece = g.reshape(count, w.shape[0], wide, width).transpose(0, 2, 1, 3)
        pieces.append(piece.reshape(count, wide * w.shape[0], width))
    packed = jnp.concatenate(pieces, 1).astype(bf16)
    packed = lax.psum_scatter(packed, "dp", scatter_dimension=0, tiled=True).astype(f32)
    packed = lax.all_to_all(packed.astype(bf16), "img", 0, 0, tiled=True).astype(f32)
    outs = []
    start = 0
    for w, length in zip(shards, lengths):
        wide = w.shape[1] // chans
        piece = packed[:, start : start + length].reshape(parts, wide, w.shape[0], width)
        outs.append(piece.transpose(2, 1, 0, 3).reshape(w.shape))
        start += length
    vec_sum = lax.all_gather(lax.psum(grad_vec, "dp"), "img", axis=1, tiled=True)
    each = chans // count
    g_vec = lax.dynamic_slice_in_dim(
        vec_sum, (lax.axis_index("dp") * parts + place) * each, each, 1
    )
    g1, g2, gq, gc, ge, go = outs
    return (tops[0].reshape(image.shape), tops[1].reshape(image.shape), g1, g2, ge, gq, gc, go, g_vec)


def solution(mesh):
    whole = P(("dp", "img"), None)
    field = P("dp", "img", None, None)
    in_specs = (
        field, P("dp", None), P("dp", None, None), whole, whole, whole, whole, whole, whole,
        P(None, ("dp", "img")), field,
    )
    out_specs = (field, field, whole, whole, whole, whole, whole, whole, P(None, ("dp", "img")))
    return jax.shard_map(
        on_device, mesh=mesh, in_specs=in_specs, out_specs=out_specs, check_vma=False
    )
```

```python
import functools
import types

import jax
import jax.numpy as jnp
from jax import lax
from jax.experimental import pallas as pl
from jax.experimental.pallas import tpu as pltpu
from jax.sharding import PartitionSpec as P

HEADS = 8
HEAD = 64
GROUPS = 32

f32 = jnp.float32
bf16 = jnp.bfloat16
highest = lax.Precision.HIGHEST


def dot(a, b):
    return jnp.dot(a, b, preferred_element_type=f32)


def silu_slope(value):
    sigma = jax.nn.sigmoid(value)
    return sigma * (1.0 + value * (1.0 - sigma))


def group_norm(flat, size):
    pixels, chans = flat.shape
    part = flat.reshape(pixels, chans // size, size)
    mean = jnp.mean(part, axis=(0, 2), keepdims=True)
    spread = jnp.mean(jnp.square(part - mean), axis=(0, 2), keepdims=True)
    inverse = lax.rsqrt(spread + 1e-05)
    return ((part - mean) * inverse).reshape(pixels, chans), inverse


def group_back(grad, normed, inverse, size):
    pixels, chans = grad.shape
    upper = grad.reshape(pixels, chans // size, size)
    lower = normed.reshape(pixels, chans // size, size)
    first = jnp.mean(upper, axis=(0, 2), keepdims=True)
    second = jnp.mean(upper * lower, axis=(0, 2), keepdims=True)
    return ((upper - first - lower * second) * inverse).reshape(pixels, chans)


def taps_of(flat, rows, cols, flipped):
    chans = flat.shape[-1]
    padded = jnp.pad(flat.reshape(rows, cols, chans), ((1, 1), (1, 1), (0, 0)))
    pieces = []
    for r in range(3):
        for c in range(3):
            top, left = (2 - r, 2 - c) if flipped else (r, c)
            pieces.append(padded[top : top + rows, left : left + cols].reshape(rows * cols, chans))
    return jnp.concatenate(pieces, 1)


def columns(weight, parts):
    rows, chans = weight.shape
    return weight.reshape(rows, chans // (parts * 128), parts, 128).transpose(2, 1, 0, 3).reshape(parts, -1, 128)


class Wires:
    def __init__(self, sent, landed):
        self.sent, self.landed, self.used, self.held = sent, landed, [0, 0], []

    def slot(self, kind, count=1):
        self.used[kind] += count
        return self.used[kind] - count

    def copy(self, out, at, source, target, device):
        return pltpu.make_async_remote_copy(
            src_ref=source, dst_ref=target, send_sem=self.sent.at[out], recv_sem=self.landed.at[at],
            device_id=device, device_id_type=pl.DeviceIdType.MESH,
        )

    def send(self, source, target, device, out=None):
        copy = self.copy(self.slot(0) if out is None else out, self.slot(1), source, target, device)
        copy.start()
        if out is None:
            self.held.append(copy.wait_send)
        return copy

    def group(self, triples, whole):
        out, at = self.slot(0), self.slot(1)
        for source, target, device in triples:
            self.copy(out, at, source, target, device).start()
        total = self.copy(out, at, whole, whole, triples[0][2])
        self.held.append(total.wait_send)
        return total

    def drain(self):
        for finish in self.held:
            finish()


def scratch_plan(g):
    P, Q, C, B, N, J, X = g.P, g.Q, g.C, g.B, g.N, g.J, g.X
    plan = dict(
        X=((J, Q, C), bf16), vown=((16, C), bf16), vs1=((J, 16, C), bf16),
        vsum=((16, C), bf16), vs2=((N, 16, C), bf16), vecs=((J, 16, B), f32),
        eall=((N, 1, g.E), f32), wemb=((2 * g.RE, 2 * C), bf16), epart=((N, 1, 2 * C), f32),
        erx=((N, 1, 2 * C), f32), esum=((J, 1, 2 * C), f32), emb=((1, 2 * C), f32),
        A1=((2, P + 2 * g.COLS, 2 * B), bf16), A2=((2, P + 2 * g.COLS, 2 * B), bf16),
        N3=((2, P, 2 * B), bf16), O=((2, P, 2 * B), bf16),
        A1T=((C, P), bf16), A2T=((C, P), bf16), N3T=((C, P), bf16), OT=((C, P), bf16),
        st1=((J, 8, B), f32), xj=((P, B), bf16),
        h1=((P, B), f32), y1=((P, B), f32), dy1=((P, B), f32), tmp=((P, B), f32),
        W1T=((2, 9 * B, 2 * B), bf16), W2T=((2, 9 * B, 2 * B), bf16), WqT=((2, 3 * B, 2 * B), bf16),
        ctx=((B, X), bf16), ctxs=((N, B, X // N), bf16), dcx=((B, 2 * B), bf16), dcxs=((N, B, 2 * B), bf16),
        Kb=((P + B, B), bf16), Vb=((P + B, B), bf16), KT=((B, P + B), bf16), VT=((B, P + B), bf16),
        qs=((P, B), bf16), dK=((P + B, B), f32), dV=((P + B, B), f32), dqkv=((3, P, B), bf16),
        WoF=((2, C, 2 * B), bf16), dopx=((Q, C), bf16), doj=((P, B), bf16), dyj=((P, B), bf16),
        outj=((P, B), bf16), inj=((P, B), bf16),
        S=((3, P + 2 * g.COLS, B), bf16),
        dse=((J, 2, B), f32), dsall=((N, J, 2, B), f32), geb=((2 * g.RE, 2 * C), f32),
        gvec=((16, B), f32), gvs=((N, 16, B), f32), gvi=((J, 16, B), f32), gvt=((16, B), f32),
    )
    half = dict(ps=((2, 2, P, B), bf16), rc=((2, P, B), bf16), sy=((P, B), bf16), ry=((P, B), bf16))
    groups = [plan, half, half, half]
    for wide, rows in g.weights:
        depth = rows * J
        summed = {} if wide == 2 else dict(
            g=((wide, depth * N, B), bf16), rx=((N // 2, wide, depth, B), bf16), zs=((N // 2, wide, depth, B), bf16),
            zr=((N // 2, wide, depth, B), bf16),
        )
        groups.append(dict(
            w=((wide, depth * N, B), bf16), fin=((wide, depth, B), bf16), gr=((J, wide, rows, B), bf16), **summed
        ))
    return groups


def body(g, groups, *refs):
    (x_in, cond, ctx_in, w1, w2, w_emb, w_q, w_c, w_o, vec_in, dy_in) = refs[:11]
    (out, in_grad, gc1, gc2, g_emb, g_q, g_c, g_o, g_v) = refs[11:20]
    left = list(refs[20:-2])
    spaces = [types.SimpleNamespace(**{name: left.pop(0) for name in group}) for group in groups]
    s, dn_bufs, da2_bufs, da1_bufs = spaces[:4]
    c1, c2, wq, wc, wo = spaces[4:]
    for weight, shape, ref in zip(spaces[4:], g.weights, (w1, w2, w_q, w_c, w_o)):
        weight.wide, weight.rows, weight.ref = shape[0], shape[1], ref
        weight.depth = weight.rows * g.J
    rest = (wq, wc, wo)
    P, Q, C, B, N, J, COLS, SIZE = g.P, g.Q, g.C, g.B, g.N, g.J, g.COLS, g.SIZE
    T, E, RE = g.T, g.E, g.RE
    XN, TP = g.X // N, (T + 15) // 16 * 16
    Z = N // 2
    STEPS = P // Q
    wires = Wires(refs[-2], refs[-1])
    send, group = wires.send, wires.group
    d = lax.axis_index("dp")
    j = lax.axis_index("img")
    flat = d * J + j
    z, xx = lax.div(d, 2), lax.rem(d, 2)
    yy, cc = lax.div(j, 2), lax.rem(j, 2)
    sib = (d, yy * 2 + (1 - cc))
    ypeer = (d, (1 - yy) * 2 + cc)
    diag = (d, (1 - yy) * 2 + (1 - cc))
    img_peers = [ypeer, diag, sib]
    dp_peers = [(lax.rem(d + k, N), j) for k in range(1, N)]
    zdev = [lax.rem(z + k, Z) for k in range(Z)]
    zsrc = [lax.rem(z + Z - k, Z) for k in range(Z)]
    xpeer = (z * 2 + (1 - xx), j)

    def lanes(k):
        return pl.ds(pl.multiple_of(k * B, B), B)

    def rows_at(start, size, unit):
        return pl.ds(pl.multiple_of(start, unit), size)

    def px(i):
        return pl.ds(pl.multiple_of(i * Q, Q), Q)

    def each(fn, init=None):
        if init is None:
            lax.fori_loop(0, STEPS, lambda i, carry: (fn(i), carry)[1], 0)
            return None
        return lax.fori_loop(0, STEPS, fn, init)

    def mm(a, b):
        return jnp.dot(a, b, preferred_element_type=f32)

    def mm_t(a, b):
        return lax.dot_general(a, b, (((1,), (1,)), ((), ())), preferred_element_type=f32)

    lane8 = lax.broadcasted_iota(jnp.int32, (8, B), 1)

    def group_sum(row):
        v = jnp.broadcast_to(row, (8, B))
        step = 1
        while step < SIZE:
            down, up = pltpu.roll(v, B - step, 1), pltpu.roll(v, step, 1)
            v = v + jnp.where((lane8 & step) == 0, down, up)
            step *= 2
        return v[0:1]

    def colsum(v):
        while v.shape[0] % 32 == 0:
            half = v.shape[0] // 2
            v = v[:half] + v[half:]
        return jnp.sum(v, axis=0, keepdims=True)

    zero_row = jnp.zeros((1, B), f32)
    count = P * SIZE

    def moments(load):
        total = each(lambda i, a: a + colsum(load(i)), zero_row)
        mean = group_sum(total) * (1.0 / count)
        spread = each(lambda i, a: a + colsum(jnp.square(load(i) - mean)), zero_row)
        return mean, lax.rsqrt(group_sum(spread) * (1.0 / count) + 1e-05)

    col = lax.rem(lax.broadcasted_iota(jnp.int32, (Q, B), 0), COLS)

    def from_left(v):
        return jnp.where(col == 0, 0.0, pltpu.roll(v, 1, 0))

    def from_right(v):
        return jnp.where(col == COLS - 1, 0.0, pltpu.roll(v, Q - 1, 0))

    hot = lax.broadcasted_iota(jnp.int32, (16, C), 1) == (
        lax.broadcasted_iota(jnp.int32, (16, C), 0) + flat * g.VW
    )
    hot = jnp.where(hot, 1.0, 0.0).astype(bf16)
    own_vec = mm(vec_in[...], hot).astype(bf16)
    s.vown[...] = own_vec
    s.vs1[j] = own_vec
    e_own = cond[...].astype(f32)
    e_own = (e_own * jax.nn.sigmoid(e_own)).astype(bf16).astype(f32)
    s.eall[d] = e_own

    barrier = pltpu.get_barrier_semaphore()
    for device in img_peers + dp_peers:
        pl.semaphore_signal(barrier, inc=1, device_id=device, device_id_type=pl.DeviceIdType.MESH)
    pl.semaphore_wait(barrier, len(img_peers) + len(dp_peers))

    def stage_img(W):
        start = d * W.depth + j * W.rows
        W.img = group(
            [
                (W.ref.at[:, rows_at(t * C + device[1] * B, B, B)], W.w.at[t, rows_at(start, W.rows, 16), :], device)
                for device in img_peers
                for t in range(W.wide)
            ],
            W.w.at[:, 0 : (J - 1) * W.rows, :],
        )

    def own_img(W):
        start = d * W.depth + j * W.rows
        for t in range(W.wide):
            W.w[t, rows_at(start, W.rows, 16), :] = W.ref[:, rows_at(t * C + j * B, B, B)]

    def block(W, ref, owner):
        return ref.at[:, rows_at(owner * W.depth, W.depth, 16), :]

    def img_done(W):
        W.img.wait_recv()

    above, below = z < Z - 1, z > 0
    up, down = ((z + 1) * 2 + xx, j), ((z - 1) * 2 + xx, j)

    def piece(W, start, size):
        p = types.SimpleNamespace(W=W, start=start, size=size)
        p.zr, p.xr, p.zs, p.xs = wires.slot(1, Z), wires.slot(1), wires.slot(0), wires.slot(0)
        p.at = lambda owner: W.w.at[:, rows_at(owner * W.depth + start, size, 16), :]
        p.first = lambda count: W.w.at[:, 0 : count * size, :]

        def finish():
            wires.copy(p.xs, p.xr, p.first(Z), p.first(Z), xpeer).wait_send()
            for count, gate in ((Z + 1, above & below), (1, (z == 0) | (z == Z - 1))):
                pl.when(gate)(
                    lambda: wires.copy(p.zs, p.xr, p.first(count), p.first(count), xpeer).wait_send()
                )

        wires.held.append(finish)
        return p

    def move(p, owner, device):
        here = p.at(owner * 2 + xx)
        wires.copy(p.zs, p.zr + owner, here, here, device).start()

    def across(p, owner):
        here = p.at(owner * 2 + xx)
        wires.copy(p.xs, p.xr, here, here, xpeer).start()

    def z_start(pieces):
        for p in pieces:
            pl.when(above)(lambda: move(p, z, up))
            pl.when(below)(lambda: move(p, z, down))
        for p in pieces:
            across(p, z)

    def z_step(pieces, step):
        def take(owner, onward, device):
            for p in pieces:
                here = p.at(owner * 2 + xx)
                wires.copy(p.zs, p.zr + owner, here, here, xpeer).wait_recv()
                if step < Z - 1:
                    pl.when(onward)(lambda: move(p, owner, device))
                across(p, owner)

        pl.when(z >= step)(lambda: take(z - step, above, up))
        pl.when(z + step < Z)(lambda: take(z + step, below, down))

    def arrive(pieces):
        for p in pieces:
            wires.copy(p.xs, p.xr, p.first(Z), p.first(Z), xpeer).wait_recv()

    def halves(W):
        half = W.depth // 32 * 16
        return [piece(W, 0, half), piece(W, half, W.depth - half)]

    p1, p2 = halves(c1), halves(c2)
    pq, pc, po = ([piece(W, 0, W.depth)] for W in rest)

    def gather_start(mine):
        return types.SimpleNamespace(y=send(mine, mine, ypeer), c=send(mine, mine, sib))

    def gather_near(state):
        state.c.wait_recv()

    def gather_far(state, theirs):
        state.y.wait_recv()
        state.f = send(theirs, theirs, sib)

    def gather_end(state):
        state.f.wait_recv()

    stage_img(c1)
    stage_img(wo)
    v_stage1 = group([(s.vown, s.vs1.at[j], device) for device in img_peers], s.vs1.at[0 : J - 1])
    x_own = s.X.at[j]
    x_state = types.SimpleNamespace(y=send(x_in, x_own, ypeer), c=send(x_in, x_own, sib))
    e_stage1 = group([(s.eall.at[d], s.eall.at[d], device) for device in dp_peers], s.eall.at[0 : N - 1])
    own_img(c1)
    s.X[j] = x_in[...]
    for W in (c2, *rest):
        own_img(W)
    for buf in (s.A1, s.A2):
        for h in range(2):
            buf[h, 0:COLS, :] = jnp.zeros((COLS, 2 * B), bf16)
            buf[h, P + COLS : P + 2 * COLS, :] = jnp.zeros((COLS, 2 * B), bf16)
    for c in range(3):
        s.S[c, 0:COLS, :] = jnp.zeros((COLS, B), bf16)
        s.S[c, P + COLS : P + 2 * COLS, :] = jnp.zeros((COLS, B), bf16)
    s.ctx[...] = jnp.zeros((B, g.X), bf16)
    s.ctx[0:T, :] = ctx_in[...]
    if TP < B:
        s.ctxs[:, TP:B, :] = jnp.zeros((N, B - TP, XN), bf16)
        s.dcxs[:, TP:B, :] = jnp.zeros((N, B - TP, 2 * B), bf16)
    img_done(c1)
    z_start(p1[:1])
    z_start(p1[1:])
    img_done(wo)
    z_start(po)
    v_stage1.wait_recv()
    total = s.vs1[0].astype(f32)
    for k in range(1, J):
        total = total + s.vs1[k].astype(f32)
    s.vsum[...] = total.astype(bf16)
    s.vs2[d] = total.astype(bf16)
    v_stage2 = group([(s.vsum, s.vs2.at[d], device) for device in dp_peers], s.vs2.at[0 : N - 1])
    stage_img(c2)

    x_state.y.wait_recv()
    far = s.X.at[(1 - yy) * 2 + cc]
    x_state.f = send(far, far, sib)
    stage_img(wq)
    stage_img(wc)
    dy_copies = group(
        [(dy_in.at[:, lanes(device[1])], s.dyj.at[rows_at(j * Q, Q, Q), :], device) for device in img_peers],
        s.dyj.at[0 : P - Q, :],
    )
    s.dyj[rows_at(j * Q, Q, Q), :] = dy_in[:, lanes(j)]
    z_step(p1[:1], 1)
    z_step(p1[1:] + po, 1)

    e_stage1.wait_recv()
    s.wemb[...] = jnp.zeros((2 * RE, 2 * C), bf16)
    s.wemb[rows_at(lax.rem(flat, 2) * RE, RE, 16), :] = w_emb[...]
    e_at = rows_at(lax.div(flat, 2) * (2 * RE), 2 * RE, B)
    e_rows = jnp.concatenate([s.eall[k, :, e_at] for k in range(N)], axis=0)
    part = mm(e_rows.astype(bf16), s.wemb[...])
    for k in range(N):
        s.epart[k] = part[k : k + 1]
    s.erx[d] = s.epart[d]
    e_stage2 = group([(s.epart.at[device[0]], s.erx.at[d], device) for device in dp_peers], s.erx.at[0 : N - 1])

    x_state.c.wait_recv()
    x_state.f.wait_recv()

    def load_x(k):
        return lambda i: s.X[i, :, k * B : (k + 1) * B].astype(f32)

    def stats(k):
        mean, inverse = moments(load_x(k))
        s.st1[k, 0:1, :] = mean
        s.st1[k, 1:2, :] = inverse

    stats(0)
    stats(1)
    z_step(p1[:1], 2)
    z_step(p1[1:] + po, 2)
    img_done(c2)
    z_start(p2[:1])
    z_start(p2[1:])
    stats(2)
    stats(3)
    e_stage2.wait_recv()
    total = s.erx[0]
    for k in range(1, N):
        total = total + s.erx[k]
    s.esum[j] = total
    e_stage3 = group([(s.esum.at[j], s.esum.at[j], device) for device in img_peers], s.esum.at[0 : J - 1])
    v_stage2.wait_recv()
    total = s.vs2[0].astype(f32)
    for k in range(1, N):
        total = total + s.vs2[k].astype(f32)
    for k in range(J):
        s.vecs[k] = total[:, k * B : (k + 1) * B]

    def vec(row):
        return s.vecs[j, row : row + 1, :]

    z_step(p1[:1], 3)
    z_step(p1[1:] + po, 3)
    for k in range(J):
        mean, inverse = s.st1[k, 0:1, :], s.st1[k, 1:2, :]
        gain, bias = s.vecs[k, 0:1, :], s.vecs[k, 1:2, :]
        load = load_x(k)

        def act(i):
            t1 = (load(i) - mean) * inverse * gain + bias
            a1 = t1 * jax.nn.sigmoid(t1)
            s.A1[k // 2, rows_at(i * Q + COLS, Q, COLS), (k % 2) * B : (k % 2 + 1) * B] = a1.astype(bf16)

        each(act)

    def turn(source, target, offset):
        def one(i):
            for h in range(2):
                v = source[h, rows_at(i * Q + offset, Q, 16), :]
                target[h * 2 * B : (h + 1) * 2 * B, px(i)] = v.T
        each(one)

    each(lambda i: s.xj.__setitem__((px(i), slice(None)), s.X[i, :, lanes(j)]))
    z_step(p2[:1], 1)
    z_step(p2[1:], 1)
    e_stage3.wait_recv()
    total = s.esum[0]
    for k in range(1, J):
        total = total + s.esum[k]
    s.emb[...] = total
    scale = 1.0 + (s.emb[:, lanes(j)] + vec(14))
    shift = s.emb[:, lanes(j + J)] + vec(15)
    arrive(po)
    wo_at = s.WoF.at[yy, :, lanes(cc)]
    s.WoF[yy, :, lanes(cc)] = wo.w[0]
    wo_state = gather_start(wo_at)
    arrive(p1)

    def convolve(A, W, emit):
        def one(i):
            left = jnp.concatenate(
                [A[h, rows_at(i * Q + r * COLS, Q, COLS), :] for r in range(3) for h in range(2)], axis=1
            )
            right = jnp.concatenate(
                [
                    jnp.concatenate([W[0, (3 * r + c) * C : (3 * r + c + 1) * C, :] for r in range(3)], axis=0)
                    for c in range(3)
                ],
                axis=1,
            )
            p = mm(left, right)
            emit(i, p[:, B : 2 * B] + from_left(p[:, :B]) + from_right(p[:, 2 * B :]))
        each(one)

    def save_h1(i, v):
        s.h1[px(i), :] = v + vec(2)

    convolve(s.A1, c1.w, save_h1)
    mean2, inv2 = moments(lambda i: s.h1[px(i), :])
    gather_far(wo_state, s.WoF.at[1 - yy, :, lanes(cc)])
    gather_near(wo_state)
    gather_end(wo_state)

    def xh2(i):
        return (s.h1[px(i), :] - mean2) * inv2

    def u_of(i):
        return (xh2(i) * vec(3) + vec(4)) * scale + shift

    def act2(i):
        u = u_of(i)
        s.A2[yy, rows_at(i * Q + COLS, Q, COLS), lanes(cc)] = (u * jax.nn.sigmoid(u)).astype(bf16)

    each(act2)
    inside = pl.ds(COLS, P)
    a2_state = gather_start(s.A2.at[yy, inside, lanes(cc)])
    for h in range(2):
        part = mm_t(dy_in[:, 0 : 2 * B], s.WoF[0, h * 2 * B : (h + 1) * 2 * B, :])
        part = part + mm_t(dy_in[:, 2 * B : 4 * B], s.WoF[1, h * 2 * B : (h + 1) * 2 * B, :])
        s.dopx[:, h * 2 * B : (h + 1) * 2 * B] = part.astype(bf16)
    do_copies = group(
        [(s.dopx.at[:, lanes(device[1])], s.doj.at[rows_at(j * Q, Q, Q), :], device) for device in img_peers],
        s.doj.at[0 : P - Q, :],
    )
    s.doj[rows_at(j * Q, Q, Q), :] = s.dopx[:, lanes(j)]
    z_step(p2[:1], 2)
    z_step(p2[1:], 2)
    img_done(wq)
    img_done(wc)
    z_start(pq)
    z_start(pc)
    z_step(p2[:1], 3)
    z_step(p2[1:], 3)
    gather_far(a2_state, s.A2.at[1 - yy, inside, lanes(cc)])
    turn(s.A1, s.A1T, COLS)
    z_step(pq, 1)
    z_step(pc, 1)
    gather_near(a2_state)
    gather_end(a2_state)
    arrive(p2)

    def save_y1(i, v):
        s.y1[px(i), :] = s.xj[px(i), :].astype(f32) + v + vec(5)

    convolve(s.A2, c2.w, save_y1)
    mean3, inv3 = moments(lambda i: s.y1[px(i), :])

    def xh3(i):
        return (s.y1[px(i), :] - mean3) * inv3

    def act3(i):
        s.N3[yy, px(i), lanes(cc)] = (xh3(i) * vec(6) + vec(7)).astype(bf16)

    each(act3)
    n_state = gather_start(s.N3.at[yy, :, lanes(cc)])
    z_step(pq, 2)
    z_step(pc, 2)
    turn(s.A2, s.A2T, COLS)

    def turn_weights(W, target, taps, stride):
        for h in range(2):
            for t in range(taps):
                v = W(t)[rows_at(h * 2 * B, 2 * B, 16), :]
                target[h, t * B : (t + 1) * B, :] = v.T

    def conv_tap(W):
        return lambda t: W.w.at[0, pl.ds(t * C, C), :]

    turn_weights(conv_tap(c2), s.W2T, 9, C)
    gather_far(n_state, s.N3.at[1 - yy, :, lanes(cc)])
    z_step(pq, 3)
    z_step(pc, 3)
    turn_weights(conv_tap(c1), s.W1T, 9, C)
    arrive(pq)
    arrive(pc)
    turn_weights(lambda t: wq.w.at[t], s.WqT, 3, C)
    tokens = lax.broadcasted_iota(jnp.int32, (B, B), 0) < T
    for t, target in enumerate((s.Kb, s.Vb)):
        v = mm(s.ctx[...], wc.w[t]) + vec(12 + t)
        target[P : P + B, :] = jnp.where(tokens, v, 0.0).astype(bf16)
    gather_near(n_state)
    gather_end(n_state)

    def tokens_of(owner):
        return s.ctx.at[0:TP, rows_at(owner * XN, XN, B)]

    ctx_copies = group(
        [(tokens_of(device[0]), s.ctxs.at[d, 0:TP, :], device) for device in dp_peers],
        s.ctxs.at[0 : N - 1, 0:TP, :],
    )
    s.ctxs[d, 0:TP, :] = tokens_of(d)[...]

    def project(i):
        left = jnp.concatenate([s.N3[0, px(i), :], s.N3[1, px(i), :]], axis=1)
        right = jnp.concatenate([wq.w[t] for t in range(3)], axis=1)
        v = mm(left, right)
        q = (v[:, :B] + vec(9)).astype(bf16)
        s.qs[px(i), :] = (q.astype(f32) * g.FACTOR).astype(bf16)
        s.Kb[px(i), :] = (v[:, B : 2 * B] + vec(10)).astype(bf16)
        s.Vb[px(i), :] = (v[:, 2 * B :] + vec(11)).astype(bf16)

    each(project)
    for source, target in ((s.Kb, s.KT), (s.Vb, s.VT)):
        for k in range(0, P + B, B):
            target[:, k : k + B] = source[k : k + B, :].T
    do_copies.wait_recv()
    dy_copies.wait_recv()
    s.dK[...] = jnp.zeros((P + B, B), f32)
    s.dV[...] = jnp.zeros((P + B, B), f32)

    HEAD_ = g.HEAD
    lane_row = lax.broadcasted_iota(jnp.int32, (1, B), 1)
    known = lax.broadcasted_iota(jnp.int32, (B, Q), 0) < T

    def attend(i):
        q_i, do_i = s.qs[px(i), :], s.doj[px(i), :]
        q_m, do_m, low, slope, mixed, back = [], [], [], [], [], []
        for h in range(B // HEAD_):
            keep = jnp.where(lax.div(lane_row, HEAD_) == h, 1.0, 0.0).astype(bf16)
            qm, dom = q_i * keep, do_i * keep
            scores = mm_t(s.Kb[...], qm)
            scores = jnp.concatenate([scores[:P], jnp.where(known, scores[P:], -1e30)], axis=0)
            top = jnp.max(scores, axis=0, keepdims=True)
            e = jnp.exp(scores - top)
            probs = e * (1.0 / jnp.sum(e, axis=0, keepdims=True))
            pb = probs.astype(bf16)
            mixed.append(mm(s.VT[h * HEAD_ : (h + 1) * HEAD_, :], pb))
            dp = mm_t(s.Vb[...], dom)
            inner = jnp.sum(dp * probs, axis=0, keepdims=True)
            ds = (probs * (dp - inner)).astype(bf16)
            back.append(mm(s.KT[h * HEAD_ : (h + 1) * HEAD_, :], ds))
            q_m.append(qm)
            do_m.append(dom)
            low.append(pb)
            slope.append(ds)
        s.dV[...] += mm(jnp.concatenate(low, axis=1), jnp.concatenate(do_m, axis=0))
        s.dK[...] += mm(jnp.concatenate(slope, axis=1), jnp.concatenate(q_m, axis=0))
        s.O[yy, px(i), lanes(cc)] = jnp.concatenate(mixed, axis=0).T.astype(bf16)
        s.dqkv[0, px(i), :] = (jnp.concatenate(back, axis=0).T * g.FACTOR).astype(bf16)

    each(attend)
    o_state = gather_start(s.O.at[yy, :, lanes(cc)])

    def grads_kv(i):
        s.dqkv[1, px(i), :] = s.dK[px(i), :].astype(bf16)
        s.dqkv[2, px(i), :] = s.dV[px(i), :].astype(bf16)

    each(grads_kv)

    def scatter(bufs, left, right):
        ps, rc, sy, ry = bufs.ps, bufs.rc, bufs.sy, bufs.ry
        near = []
        for slot in range(2):
            half = 1 - yy if slot == 0 else yy

            def one(i):
                v = mm(left(i), right[half]).astype(bf16)
                ps[slot, 0, px(i), :] = v[:, :B]
                ps[slot, 1, px(i), :] = v[:, B:]

            each(one)
            near.append(send(ps.at[slot, 1 - cc], rc.at[slot], sib))
            if slot == 0:
                near[0].wait_recv()

                def add(i):
                    v = ps[0, cc, px(i), :].astype(f32) + rc[0, px(i), :].astype(f32)
                    sy[px(i), :] = v.astype(bf16)

                each(add)
                across = send(sy, ry, ypeer)

        def done():
            near[1].wait_recv()
            across.wait_recv()

        def load(i):
            v = ps[1, cc, px(i), :].astype(f32) + rc[1, px(i), :].astype(f32)
            return v + ry[px(i), :].astype(f32)

        return done, load

    order = list(range(1, Z)) + [0]

    def sum_start(W):
        W.sx, W.zout, W.zin = {}, wires.slot(0), wires.slot(1)
        out = wires.slot(0)
        for k in order:
            W.sx[k] = send(block(W, W.g, zdev[k] * 2 + (1 - xx)), W.rx.at[k], xpeer, out)
        wires.held.append(wires.copy(out, W.zin, W.rx, W.rx, xpeer).wait_send)

    def sum_block(W, k):
        W.sx[k].wait_recv()
        at = rows_at((zdev[k] * 2 + xx) * W.depth, W.depth, 16)
        v = W.g[:, at, :].astype(f32) + W.rx[k].astype(f32)
        W.zs[k] = v.astype(bf16)
        if k:
            wires.copy(W.zout, W.zin, W.zs.at[k], W.zr.at[k], (zdev[k] * 2 + xx, j)).start()

    def sum_z(W):
        for k in order:
            sum_block(W, k)

    def sum_img(W):
        total = wires.copy(W.zout, W.zin, W.zr.at[0 : Z - 1], W.zr.at[0 : Z - 1], xpeer)
        total.wait_recv()
        wires.held.append(total.wait_send)
        v = W.zs[0].astype(f32)
        for k in range(1, Z):
            v = v + W.zr[k].astype(f32)
        to_rows(W, jnp.concatenate([v[t] for t in range(W.wide)], axis=1))

    def to_rows(W, v):
        for t in range(W.wide):
            W.fin[t] = v[:, t * B : (t + 1) * B].astype(bf16)
        W.simg = group(
            [
                (W.fin.at[:, rows_at(device[1] * W.rows, W.rows, 16), :], W.gr.at[j], device)
                for device in img_peers
            ],
            W.gr.at[0 : J - 1],
        )
        W.gr[j] = W.fin[:, rows_at(j * W.rows, W.rows, 16), :]

    def sum_end(W, target):
        W.simg.wait_recv()
        for k in range(J):
            for t in range(W.wide):
                target[:, t * C + k * B : t * C + (k + 1) * B] = W.gr[k, t].astype(f32)

    dn_done, dn_at = scatter(
        dn_bufs, lambda i: jnp.concatenate([s.dqkv[t, px(i), :] for t in range(3)], axis=1), s.WqT
    )
    turn(s.N3, s.N3T, 0)
    for h in range(2):
        at = slice(h * 2 * B, (h + 1) * 2 * B)
        v = mm(s.N3T[at, :], jnp.concatenate([s.dqkv[t] for t in range(3)], axis=1)).astype(bf16)
        for t in range(3):
            wq.g[t, at, :] = v[:, t * B : (t + 1) * B]
    sum_start(wq)
    s.dcx[...] = jnp.concatenate([s.dK[P : P + B, :], s.dV[P : P + B, :]], axis=1).astype(bf16)
    s.dcxs[d] = s.dcx[...]
    dcx_copies = group(
        [(s.dcx.at[0:TP, :], s.dcxs.at[d, 0:TP, :], device) for device in dp_peers],
        s.dcxs.at[0 : N - 1, 0:TP, :],
    )
    gather_far(o_state, s.O.at[1 - yy, :, lanes(cc)])
    gather_near(o_state)
    gather_end(o_state)

    def finish(i):
        left = jnp.concatenate([s.O[0, px(i), :], s.O[1, px(i), :]], axis=1)
        s.outj[px(i), :] = (s.y1[px(i), :] + mm(left, wo.w[0]) + vec(8)).astype(bf16)

    each(finish)

    def to_pixels(source, target):
        copies = group(
            [(source.at[rows_at(device[1] * Q, Q, Q), :], target.at[:, lanes(j)], device) for device in img_peers],
            source.at[0 : P - Q, :],
        )
        target[:, lanes(j)] = source[rows_at(j * Q, Q, Q), :]
        return copies

    out_copies = to_pixels(s.outj, out)
    turn(s.O, s.OT, 0)
    for h in range(2):
        at = slice(h * 2 * B, (h + 1) * 2 * B)
        wo.g[0, at, :] = mm(s.OT[at, :], s.dyj[...]).astype(bf16)
    sum_start(wo)

    def back_sums(grad, normed, factor):
        def one(i, carry):
            v = grad(i)
            return carry[0] + colsum(v), carry[1] + colsum(v * normed(i))
        first, second = each(one, (zero_row, zero_row))
        return first, second, group_sum(first * factor) * (1.0 / count), group_sum(second * factor) * (1.0 / count)

    dn_done()
    sum_z(wq)
    dn_sum, dn_hat, m1, m2 = back_sums(dn_at, xh3, vec(6))

    def shifted(i, v):
        at = rows_at(i * Q + COLS, Q, COLS)
        s.S[0, at, :] = from_right(v).astype(bf16)
        s.S[1, at, :] = v.astype(bf16)
        s.S[2, at, :] = from_left(v).astype(bf16)

    def make_dh2(i, carry):
        dy = s.dyj[px(i), :].astype(f32)
        v = dy + (dn_at(i) * vec(6) - m1 - xh3(i) * m2) * inv3
        s.dy1[px(i), :] = v
        low = v.astype(bf16).astype(f32)
        shifted(i, low)
        return carry[0] + colsum(low), carry[1] + colsum(dy)

    dh2_sum, dy_sum = each(make_dh2, (zero_row, zero_row))

    def tap(t, start, size):
        r, c = t // 3, t % 3
        return s.S[c, rows_at(start + (2 - r) * COLS, size, COLS), :]

    def field(i):
        return jnp.concatenate([tap(t, i * Q, Q) for t in range(9)], axis=1)

    def kernel_grad(W, turned):
        for h in range(2):
            at = slice(h * 2 * B, (h + 1) * 2 * B)
            v = mm(turned[at, :], jnp.concatenate([tap(t, 0, P) for t in range(9)], axis=1)).astype(bf16)
            for t in range(9):
                W.g[0, t * C + h * 2 * B : t * C + (h + 1) * 2 * B, :] = v[:, t * B : (t + 1) * B]

    da2_done, da2_at = scatter(da2_bufs, field, s.W2T)
    kernel_grad(c2, s.A2T)
    sum_start(c2)
    sum_z(wo)
    ctx_copies.wait_recv()
    dcx_copies.wait_recv()
    v = lax.dot_general(
        s.ctxs[...].reshape(N * B, XN), s.dcxs[...].reshape(N * B, 2 * B), (((0,), (0,)), ((), ())),
        preferred_element_type=f32,
    )
    to_rows(wc, v)
    da2_done()

    def slope_of(v):
        sigma = jax.nn.sigmoid(v)
        return sigma * (1.0 + v * (1.0 - sigma))

    def make_du(i, carry):
        du = da2_at(i) * slope_of(u_of(i))
        s.tmp[px(i), :] = du
        return carry[0] + colsum(du), carry[1] + colsum(du * xh2(i))

    du_sum, du_hat = each(make_du, (zero_row, zero_row))
    gain2 = scale * vec(3)
    m1b = group_sum(du_sum * gain2) * (1.0 / count)
    m2b = group_sum(du_hat * gain2) * (1.0 / count)

    def make_dh1(i, carry):
        v = (s.tmp[px(i), :] * gain2 - m1b - xh2(i) * m2b) * inv2
        low = v.astype(bf16).astype(f32)
        shifted(i, low)
        return carry + colsum(low)

    dh1_sum = each(make_dh1, zero_row)
    dscale = vec(3) * du_hat + vec(4) * du_sum
    kernel_grad(c1, s.A1T)
    sum_start(c1)
    da1_done, da1_at = scatter(da1_bufs, field, s.W1T)
    s.dse[j] = jnp.concatenate([dscale, du_sum], axis=0)
    ds_copies = group([(s.dse.at[j], s.dse.at[j], device) for device in img_peers], s.dse.at[0 : J - 1])
    sum_img(wq)
    sum_img(wo)
    sum_z(c2)
    ds_copies.wait_recv()
    s.dsall[d] = s.dse[...]
    ds_copies = group([(s.dse, s.dsall.at[d], device) for device in dp_peers], s.dsall.at[0 : N - 1])
    da1_done()
    mean1, inv1 = s.st1[j, 0:1, :], s.st1[j, 1:2, :]

    def xh1(i):
        return (s.xj[px(i), :].astype(f32) - mean1) * inv1

    def make_dt1(i, carry):
        n1 = xh1(i)
        dt1 = da1_at(i) * slope_of(n1 * vec(0) + vec(1))
        s.tmp[px(i), :] = dt1
        return carry[0] + colsum(dt1), carry[1] + colsum(dt1 * n1)

    dt1_sum, dt1_hat = each(make_dt1, (zero_row, zero_row))
    m1c = group_sum(dt1_sum * vec(0)) * (1.0 / count)
    m2c = group_sum(dt1_hat * vec(0)) * (1.0 / count)

    def make_in(i):
        v = s.dy1[px(i), :] + (s.tmp[px(i), :] * vec(0) - m1c - xh1(i) * m2c) * inv1
        s.inj[px(i), :] = v.astype(bf16)

    each(make_in)
    in_copies = to_pixels(s.inj, in_grad)

    qkv_sums = [each(lambda i, a, t=t: a + colsum(s.dqkv[t, px(i), :].astype(f32)), zero_row) for t in range(3)]
    s.gvec[...] = jnp.concatenate(
        [dt1_hat, dt1_sum, dh1_sum, scale * du_hat, scale * du_sum, dh2_sum, dn_hat, dn_sum, dy_sum]
        + qkv_sums
        + [colsum(s.dK[P : P + B, :]), colsum(s.dV[P : P + B, :]), dscale, du_sum],
        axis=0,
    )
    gv_copies = group([(s.gvec, s.gvs.at[d], device) for device in dp_peers], s.gvs.at[0 : N - 1])
    s.gvs[d] = s.gvec[...]
    sum_z(c1)
    gv_copies.wait_recv()
    total = s.gvs[0]
    for k in range(1, N):
        total = total + s.gvs[k]
    s.gvt[...] = total
    s.gvi[j] = total
    gv_copies = group([(s.gvt, s.gvi.at[j], device) for device in img_peers], s.gvi.at[0 : J - 1])
    sum_img(c2)
    sum_end(wq, g_q)
    sum_end(wc, g_c)
    sum_end(wo, g_o)
    ds_copies.wait_recv()
    e_cols = jnp.concatenate([s.eall[k, :, e_at] for k in range(N)], axis=0)
    for t in range(2):
        for k in range(J):
            rows = jnp.concatenate([s.dsall[i, k, t : t + 1, :] for i in range(N)], axis=0)
            v = lax.dot_general(
                e_cols, rows, (((0,), (0,)), ((), ())), precision=highest, preferred_element_type=f32
            )
            s.geb[:, t * C + k * B : t * C + (k + 1) * B] = v
    g_emb[...] = s.geb[rows_at(lax.rem(flat, 2) * RE, RE, 8), :]
    gv_copies.wait_recv()
    VW = g.VW
    each_block = B // VW
    pick = lax.broadcasted_iota(jnp.int32, (B, VW), 0) == (
        lax.broadcasted_iota(jnp.int32, (B, VW), 1) + lax.rem(flat, each_block) * VW
    )
    g_v[...] = jnp.dot(
        s.gvi[lax.div(flat, each_block)], jnp.where(pick, 1.0, 0.0), precision=highest,
        preferred_element_type=f32,
    )
    sum_end(c2, gc2)
    sum_img(c1)
    sum_end(c1, gc1)
    out_copies.wait_recv()
    in_copies.wait_recv()
    wires.drain()
    assert wires.used[0] <= g.copies[0] and wires.used[1] <= g.copies[1], wires.used


def fused(
    image, cond, context, w_conv1, w_conv2, w_embed, w_qkv, w_context, w_out, vectors, cotangent
):
    J, N = lax.axis_size("img"), lax.axis_size("dp")
    local, cols, chans = image.shape[1:]
    g = types.SimpleNamespace(
        P=local * cols * J, Q=local * cols, C=chans, B=chans // J, N=N, J=J, COLS=cols, SIZE=chans // GROUPS,
        T=context.shape[1], X=context.shape[2], E=cond.shape[1], RE=w_embed.shape[0], VW=vectors.shape[1],
        HEAD=HEAD, FACTOR=HEAD ** (-0.5),
        weights=[
            (1, w_conv1.shape[0]), (1, w_conv2.shape[0]), (3, w_qkv.shape[0]), (2, w_context.shape[0]),
            (1, w_out.shape[0]),
        ],
    )
    groups = scratch_plan(g)
    rows = local * cols
    shape = jax.ShapeDtypeStruct
    outs = [
        shape((rows, chans), bf16), shape((rows, chans), bf16), shape(w_conv1.shape, f32), shape(w_conv2.shape, f32),
        shape(w_embed.shape, f32), shape(w_qkv.shape, f32), shape(w_context.shape, f32), shape(w_out.shape, f32),
        shape(vectors.shape, f32),
    ]
    g.copies = (71, 49 + 11 * (N // 2 + 1))
    vmem = pl.BlockSpec(memory_space=pltpu.VMEM)
    result = pl.pallas_call(
        functools.partial(body, g, groups),
        out_shape=outs,
        in_specs=[vmem] * 11,
        out_specs=[vmem] * 9,
        scratch_shapes=[pltpu.VMEM(*spec) for group in groups for spec in group.values()]
        + [pltpu.SemaphoreType.DMA((count,)) for count in g.copies],
        compiler_params=pltpu.CompilerParams(
            collective_id=0, has_side_effects=True, vmem_limit_bytes=60 * 1024 * 1024
        ),
    )(
        image.reshape(rows, chans), cond, context[0], w_conv1, w_conv2, w_embed, w_qkv, w_context, w_out, vectors,
        cotangent.reshape(rows, chans),
    )
    return (result[0].reshape(image.shape), result[1].reshape(image.shape), *result[2:])


def on_device(
    image, cond, context, w_conv1, w_conv2, w_embed, w_qkv, w_context, w_out, vectors, cotangent
):
    parts = lax.axis_size("img")
    place = lax.axis_index("img")
    images = lax.axis_size("dp")
    rows, cols, chans = image.shape[1] * parts, image.shape[2], image.shape[3]
    pixels = rows * cols
    width = chans // parts
    size = chans // GROUPS
    count = images * parts

    if parts == 4 and width == 128 and images % 2 == 0 and all(
        w.shape[0] % 16 == 0 for w in (w_conv1, w_conv2, w_embed, w_qkv, w_context, w_out)
    ):
        return fused(
            image, cond, context, w_conv1, w_conv2, w_embed, w_qkv, w_context, w_out, vectors, cotangent
        )

    def own(full):
        return lax.dynamic_slice_in_dim(full, place * width, width, full.ndim - 1)

    shards = (w_conv1, w_conv2, w_qkv, w_context, w_embed, w_out)
    lengths = [w.shape[0] * (w.shape[1] // chans) for w in shards]
    packed = jnp.concatenate([columns(w, parts) for w in shards], 1)
    packed = lax.all_to_all(packed, "img", 0, 0, tiled=True)
    packed = lax.all_gather(packed, "dp", axis=0, tiled=True)
    full = []
    start = 0
    for w, length in zip(shards, lengths):
        wide = w.shape[1] // chans
        piece = packed[:, start : start + length].reshape(count, wide, w.shape[0], width)
        full.append(piece.transpose(0, 2, 1, 3).reshape(count * w.shape[0], wide * width))
        start += length
    k1, k2, kq, kc, ke, ko = full
    vec_all = lax.all_gather(vectors, ("dp", "img"), axis=1, tiled=True).astype(f32)
    vec = own(vec_all)

    x_low = lax.all_gather(image[0].reshape(-1, chans), "img", axis=0, tiled=True)
    x_all = x_low.astype(f32)
    normed1_all, inverse1_all = group_norm(x_all, size)
    act1 = jax.nn.silu(normed1_all * vec_all[0] + vec_all[1]).astype(bf16)
    normed1 = own(normed1_all)
    inverse1 = lax.dynamic_slice_in_dim(inverse1_all, place * (GROUPS // parts), GROUPS // parts, 1)
    pre1 = normed1 * vec[0] + vec[1]
    hidden1 = dot(taps_of(act1, rows, cols, False), k1) + vec[2]
    cond_act = jax.nn.silu(cond.astype(f32)).astype(bf16)
    embed = dot(cond_act, ke)[0]
    scale = embed[:width] + vec[14]
    shift = embed[width:] + vec[15]
    normed2, inverse2 = group_norm(hidden1, size)
    affine2 = normed2 * vec[3] + vec[4]
    pre2 = affine2 * (1.0 + scale) + shift
    act2_own = jax.nn.silu(pre2).astype(bf16)
    act2 = lax.all_gather(act2_own, "img", axis=1, tiled=True)
    resid = own(x_all) + dot(taps_of(act2, rows, cols, False), k2) + vec[5]
    normed3, inverse3 = group_norm(resid, size)
    affine3_own = (normed3 * vec[6] + vec[7]).astype(bf16)
    affine3 = lax.all_gather(affine3_own, "img", axis=1, tiled=True)
    qkv = (dot(affine3, kq) + jnp.concatenate([vec[9], vec[10], vec[11]])).astype(bf16)
    ctx = (dot(context[0], kc) + jnp.concatenate([vec[12], vec[13]])).astype(bf16)
    tokens = ctx.shape[0]

    out_full = lax.all_gather(ko, "img", axis=1, tiled=True)
    dy_px = cotangent[0].reshape(-1, chans)
    do_px = lax.dot_general(dy_px, out_full, (((1,), (1,)), ((), ())), preferred_element_type=f32).astype(bf16)
    both = jnp.stack([do_px, dy_px])
    both = lax.all_to_all(both, "img", 2, 1, tiled=True)
    do, dy = both[0], both[1]
    dy_wide = dy.astype(f32)

    keys = jnp.concatenate([ctx[:, :width], qkv[:, width : 2 * width]], 0)
    values = jnp.concatenate([ctx[:, width:], qkv[:, 2 * width :]], 0)
    factor = HEAD ** (-0.5)
    mixed, dq, dk, dv = [], [], [], []
    for h in range(width // HEAD):
        at = slice(h * HEAD, (h + 1) * HEAD)
        q_h, k_h, v_h, do_h = qkv[:, at], keys[:, at], values[:, at], do[:, at]
        scores = dot(k_h, q_h.T) * factor
        top = jnp.max(scores, 0, keepdims=True)
        weights = jnp.exp(scores - top)
        probs = weights / jnp.sum(weights, 0, keepdims=True)
        low = probs.astype(bf16)
        mixed.append(dot(v_h.T, low).T)
        dv.append(dot(low, do_h))
        dp = dot(v_h, do_h.T)
        ds = (probs * (dp - jnp.sum(dp * probs, 0, keepdims=True))).astype(bf16)
        dq.append(dot(k_h.T, ds).T * factor)
        dk.append(dot(ds, q_h) * factor)
    mixed = jnp.concatenate(mixed, 1).astype(bf16)
    dq, dk, dv = (jnp.concatenate(v, 1) for v in (dq, dk, dv))
    mixed_all = lax.all_gather(mixed, "img", axis=1, tiled=True)
    output = (resid + dot(mixed_all, ko) + vec[8]).astype(bf16)

    dqkv = jnp.concatenate([dq, dk[tokens:], dv[tokens:]], 1).astype(bf16)
    dctx = jnp.concatenate([dk[:tokens], dv[:tokens]], 1)
    dn_part = lax.dot_general(dqkv, kq, (((1,), (1,)), ((), ())), preferred_element_type=f32)
    dn = lax.psum_scatter(dn_part.astype(bf16), "img", scatter_dimension=1, tiled=True).astype(f32)
    dy1 = dy_wide + group_back(dn * vec[6], normed3, inverse3, size)
    dh2 = dy1.astype(bf16)

    def turned(kernel):
        return kernel.reshape(9, chans, width).transpose(0, 2, 1).reshape(9 * width, chans)

    def conv_back(dh, kernel, act):
        field = taps_of(dh, rows, cols, True)
        part = dot(field, turned(kernel)).astype(bf16)
        grad = lax.psum_scatter(part, "img", scatter_dimension=1, tiled=True).astype(f32)
        kernel_grad = lax.dot_general(act, field, (((0,), (0,)), ((), ())), preferred_element_type=f32)
        return grad, kernel_grad.reshape(chans, 9, width).transpose(1, 0, 2).reshape(9 * chans, width)

    da2, gk2 = conv_back(dh2, k2, act2)
    du = da2 * silu_slope(pre2)
    dscale = jnp.sum(du * affine2, 0)
    dshift = jnp.sum(du, 0)
    dz = du * (1.0 + scale)
    dh1 = group_back(dz * vec[3], normed2, inverse2, size).astype(bf16)
    da1, gk1 = conv_back(dh1, k1, act1)
    dt1 = da1 * silu_slope(pre1)
    in_grad = (dy1 + group_back(dt1 * vec[0], normed1, inverse1, size)).astype(bf16)

    tops = lax.all_to_all(jnp.stack([output, in_grad]), "img", 1, 2, tiled=True)
    gkq = lax.dot_general(affine3, dqkv, (((0,), (0,)), ((), ())), preferred_element_type=f32)
    gkc = lax.dot_general(context[0], dctx.astype(bf16), (((0,), (0,)), ((), ())), preferred_element_type=f32)
    gko = lax.dot_general(mixed_all, dy, (((0,), (0,)), ((), ())), preferred_element_type=f32)
    gke = cond_act[0].astype(f32)[:, None] * jnp.concatenate([dscale, dshift])[None, :]
    grad_vec = jnp.stack(
        [
            jnp.sum(dt1 * normed1, 0),
            jnp.sum(dt1, 0),
            jnp.sum(dh1.astype(f32), 0),
            jnp.sum(dz * normed2, 0),
            jnp.sum(dz, 0),
            jnp.sum(dh2.astype(f32), 0),
            jnp.sum(dn * normed3, 0),
            jnp.sum(dn, 0),
            jnp.sum(dy_wide, 0),
        ]
        + [jnp.sum(v.astype(f32), 0) for v in jnp.split(dqkv, 3, 1)]
        + [jnp.sum(v, 0) for v in jnp.split(dctx, 2, 1)]
        + [dscale, dshift],
        0,
    )
    grads = (gk1, gk2, gkq, gkc, gke, gko)
    pieces = []
    for w, g in zip(shards, grads):
        wide = w.shape[1] // chans
        piece = g.reshape(count, w.shape[0], wide, width).transpose(0, 2, 1, 3)
        pieces.append(piece.reshape(count, wide * w.shape[0], width))
    packed = jnp.concatenate(pieces, 1).astype(bf16)
    packed = lax.psum_scatter(packed, "dp", scatter_dimension=0, tiled=True).astype(f32)
    packed = lax.all_to_all(packed.astype(bf16), "img", 0, 0, tiled=True).astype(f32)
    outs = []
    start = 0
    for w, length in zip(shards, lengths):
        wide = w.shape[1] // chans
        piece = packed[:, start : start + length].reshape(parts, wide, w.shape[0], width)
        outs.append(piece.transpose(2, 1, 0, 3).reshape(w.shape))
        start += length
    vec_sum = lax.all_gather(lax.psum(grad_vec, "dp"), "img", axis=1, tiled=True)
    each = chans // count
    g_vec = lax.dynamic_slice_in_dim(
        vec_sum, (lax.axis_index("dp") * parts + place) * each, each, 1
    )
    g1, g2, gq, gc, ge, go = outs
    return (tops[0].reshape(image.shape), tops[1].reshape(image.shape), g1, g2, ge, gq, gc, go, g_vec)


def solution(mesh):
    whole = P(("dp", "img"), None)
    field = P("dp", "img", None, None)
    in_specs = (
        field, P("dp", None), P("dp", None, None), whole, whole, whole, whole, whole, whole,
        P(None, ("dp", "img")), field,
    )
    out_specs = (field, field, whole, whole, whole, whole, whole, whole, P(None, ("dp", "img")))
    return jax.shard_map(
        on_device, mesh=mesh, in_specs=in_specs, out_specs=out_specs, check_vma=False
    )
```

```python
import functools
import types

import jax
import jax.numpy as jnp
from jax import lax
from jax.experimental import pallas as pl
from jax.experimental.pallas import tpu as pltpu
from jax.sharding import PartitionSpec as P

HEADS = 8
HEAD = 64
GROUPS = 32

f32 = jnp.float32
bf16 = jnp.bfloat16
highest = lax.Precision.HIGHEST


def dot(a, b):
    return jnp.dot(a, b, preferred_element_type=f32)


def silu_slope(value):
    sigma = jax.nn.sigmoid(value)
    return sigma * (1.0 + value * (1.0 - sigma))


def group_norm(flat, size):
    pixels, chans = flat.shape
    part = flat.reshape(pixels, chans // size, size)
    mean = jnp.mean(part, axis=(0, 2), keepdims=True)
    spread = jnp.mean(jnp.square(part - mean), axis=(0, 2), keepdims=True)
    inverse = lax.rsqrt(spread + 1e-05)
    return ((part - mean) * inverse).reshape(pixels, chans), inverse


def group_back(grad, normed, inverse, size):
    pixels, chans = grad.shape
    upper = grad.reshape(pixels, chans // size, size)
    lower = normed.reshape(pixels, chans // size, size)
    first = jnp.mean(upper, axis=(0, 2), keepdims=True)
    second = jnp.mean(upper * lower, axis=(0, 2), keepdims=True)
    return ((upper - first - lower * second) * inverse).reshape(pixels, chans)


def taps_of(flat, rows, cols, flipped):
    chans = flat.shape[-1]
    padded = jnp.pad(flat.reshape(rows, cols, chans), ((1, 1), (1, 1), (0, 0)))
    pieces = []
    for r in range(3):
        for c in range(3):
            top, left = (2 - r, 2 - c) if flipped else (r, c)
            pieces.append(padded[top : top + rows, left : left + cols].reshape(rows * cols, chans))
    return jnp.concatenate(pieces, 1)


def columns(weight, parts):
    rows, chans = weight.shape
    return weight.reshape(rows, chans // (parts * 128), parts, 128).transpose(2, 1, 0, 3).reshape(parts, -1, 128)


class Wires:
    def __init__(self, sent, landed):
        self.sent, self.landed, self.used, self.held = sent, landed, [0, 0], []

    def slot(self, kind, count=1):
        self.used[kind] += count
        return self.used[kind] - count

    def copy(self, out, at, source, target, device):
        return pltpu.make_async_remote_copy(
            src_ref=source, dst_ref=target, send_sem=self.sent.at[out], recv_sem=self.landed.at[at],
            device_id=device, device_id_type=pl.DeviceIdType.MESH,
        )

    def send(self, source, target, device, out=None):
        copy = self.copy(self.slot(0) if out is None else out, self.slot(1), source, target, device)
        copy.start()
        if out is None:
            self.held.append(copy.wait_send)
        return copy

    def group(self, triples, whole):
        out, at = self.slot(0), self.slot(1)
        for source, target, device in triples:
            self.copy(out, at, source, target, device).start()
        total = self.copy(out, at, whole, whole, triples[0][2])
        self.held.append(total.wait_send)
        return total

    def drain(self):
        for finish in self.held:
            finish()


def scratch_plan(g):
    P, Q, C, B, N, J, X = g.P, g.Q, g.C, g.B, g.N, g.J, g.X
    plan = dict(
        X=((J, Q, C), bf16), vown=((16, C), bf16), vs1=((J, 16, C), bf16),
        vsum=((16, C), bf16), vs2=((N, 16, C), bf16), vecs=((J, 16, B), f32),
        eall=((N, 1, g.E), f32), wemb=((2 * g.RE, 2 * C), bf16), epart=((N, 1, 2 * C), f32),
        erx=((N, 1, 2 * C), f32), esum=((J, 1, 2 * C), f32), emb=((1, 2 * C), f32),
        A1=((2, P + 2 * g.COLS, 2 * B), bf16), A2=((2, P + 2 * g.COLS, 2 * B), bf16),
        N3=((2, P, 2 * B), bf16), O=((2, P, 2 * B), bf16),
        A1T=((C, P), bf16), A2T=((C, P), bf16), N3T=((C, P), bf16), OT=((C, P), bf16),
        st1=((J, 8, B), f32), xj=((P, B), bf16),
        h1=((P, B), f32), y1=((P, B), f32), dy1=((P, B), f32), tmp=((P, B), f32),
        W1T=((2, 9 * B, 2 * B), bf16), W2T=((2, 9 * B, 2 * B), bf16), WqT=((2, 3 * B, 2 * B), bf16),
        ctx=((B, X), bf16), ctxs=((N, B, X // N), bf16), dcx=((B, 2 * B), bf16), dcxs=((N, B, 2 * B), bf16),
        Kb=((P + B, B), bf16), Vb=((P + B, B), bf16), KT=((B, P + B), bf16), VT=((B, P + B), bf16),
        qs=((P, B), bf16), dK=((P + B, B), f32), dV=((P + B, B), f32), dqkv=((3, P, B), bf16),
        WoF=((2, C, 2 * B), bf16), dopx=((Q, C), bf16), doj=((P, B), bf16), dyj=((P, B), bf16),
        outj=((P, B), bf16), inj=((P, B), bf16),
        S=((3, P + 2 * g.COLS, B), bf16),
        dse=((J, 2, B), f32), dsall=((N, J, 2, B), f32), geb=((2 * g.RE, 2 * C), f32),
        gvec=((16, B), f32), gvs=((N, 16, B), f32), gvi=((J, 16, B), f32), gvt=((16, B), f32),
    )
    half = dict(ps=((2, 2, P, B), bf16), rc=((2, P, B), bf16), sy=((P, B), bf16), ry=((P, B), bf16))
    groups = [plan, half, half, half]
    for wide, rows in g.weights:
        depth = rows * J
        summed = {} if wide == 2 else dict(
            g=((wide, depth * N, B), bf16), rx=((N // 2, wide, depth, B), bf16), zs=((N // 2, wide, depth, B), bf16),
            zr=((N // 2, wide, depth, B), bf16),
        )
        groups.append(dict(
            w=((wide, depth * N, B), bf16), fin=((wide, depth, B), bf16), gr=((J, wide, rows, B), bf16), **summed
        ))
    return groups


def body(g, groups, *refs):
    (x_in, cond, ctx_in, w1, w2, w_emb, w_q, w_c, w_o, vec_in, dy_in) = refs[:11]
    (out, in_grad, gc1, gc2, g_emb, g_q, g_c, g_o, g_v) = refs[11:20]
    left = list(refs[20:-2])
    spaces = [types.SimpleNamespace(**{name: left.pop(0) for name in group}) for group in groups]
    s, dn_bufs, da2_bufs, da1_bufs = spaces[:4]
    c1, c2, wq, wc, wo = spaces[4:]
    for weight, shape, ref in zip(spaces[4:], g.weights, (w1, w2, w_q, w_c, w_o)):
        weight.wide, weight.rows, weight.ref = shape[0], shape[1], ref
        weight.depth = weight.rows * g.J
    rest = (wq, wc, wo)
    P, Q, C, B, N, J, COLS, SIZE = g.P, g.Q, g.C, g.B, g.N, g.J, g.COLS, g.SIZE
    T, E, RE = g.T, g.E, g.RE
    XN, TP = g.X // N, (T + 15) // 16 * 16
    Z = N // 2
    STEPS = P // Q
    wires = Wires(refs[-2], refs[-1])
    send, group = wires.send, wires.group
    d = lax.axis_index("dp")
    j = lax.axis_index("img")
    flat = d * J + j
    z, xx = lax.div(d, 2), lax.rem(d, 2)
    yy, cc = lax.div(j, 2), lax.rem(j, 2)
    sib = (d, yy * 2 + (1 - cc))
    ypeer = (d, (1 - yy) * 2 + cc)
    diag = (d, (1 - yy) * 2 + (1 - cc))
    img_peers = [ypeer, diag, sib]
    dp_peers = [(lax.rem(d + k, N), j) for k in range(1, N)]
    zdev = [lax.rem(z + k, Z) for k in range(Z)]
    zsrc = [lax.rem(z + Z - k, Z) for k in range(Z)]
    xpeer = (z * 2 + (1 - xx), j)

    def lanes(k):
        return pl.ds(pl.multiple_of(k * B, B), B)

    def rows_at(start, size, unit):
        return pl.ds(pl.multiple_of(start, unit), size)

    def px(i):
        return pl.ds(pl.multiple_of(i * Q, Q), Q)

    def each(fn, init=None):
        if init is None:
            lax.fori_loop(0, STEPS, lambda i, carry: (fn(i), carry)[1], 0)
            return None
        return lax.fori_loop(0, STEPS, fn, init)

    def mm(a, b):
        return jnp.dot(a, b, preferred_element_type=f32)

    def mm_t(a, b):
        return lax.dot_general(a, b, (((1,), (1,)), ((), ())), preferred_element_type=f32)

    lane8 = lax.broadcasted_iota(jnp.int32, (8, B), 1)

    def group_sum(row):
        v = jnp.broadcast_to(row, (8, B))
        step = 1
        while step < SIZE:
            down, up = pltpu.roll(v, B - step, 1), pltpu.roll(v, step, 1)
            v = v + jnp.where((lane8 & step) == 0, down, up)
            step *= 2
        return v[0:1]

    def colsum(v):
        while v.shape[0] % 32 == 0:
            half = v.shape[0] // 2
            v = v[:half] + v[half:]
        return jnp.sum(v, axis=0, keepdims=True)

    zero_row = jnp.zeros((1, B), f32)
    count = P * SIZE

    def moments(load):
        total = each(lambda i, a: a + colsum(load(i)), zero_row)
        mean = group_sum(total) * (1.0 / count)
        spread = each(lambda i, a: a + colsum(jnp.square(load(i) - mean)), zero_row)
        return mean, lax.rsqrt(group_sum(spread) * (1.0 / count) + 1e-05)

    col = lax.rem(lax.broadcasted_iota(jnp.int32, (Q, B), 0), COLS)

    def from_left(v):
        return jnp.where(col == 0, 0.0, pltpu.roll(v, 1, 0))

    def from_right(v):
        return jnp.where(col == COLS - 1, 0.0, pltpu.roll(v, Q - 1, 0))

    hot = lax.broadcasted_iota(jnp.int32, (16, C), 1) == (
        lax.broadcasted_iota(jnp.int32, (16, C), 0) + flat * g.VW
    )
    hot = jnp.where(hot, 1.0, 0.0).astype(bf16)
    own_vec = mm(vec_in[...], hot).astype(bf16)
    s.vown[...] = own_vec
    s.vs1[j] = own_vec
    e_own = cond[...].astype(f32)
    e_own = (e_own * jax.nn.sigmoid(e_own)).astype(bf16).astype(f32)
    s.eall[d] = e_own

    barrier = pltpu.get_barrier_semaphore()
    for device in img_peers + dp_peers:
        pl.semaphore_signal(barrier, inc=1, device_id=device, device_id_type=pl.DeviceIdType.MESH)
    pl.semaphore_wait(barrier, len(img_peers) + len(dp_peers))

    def stage_img(W):
        start = d * W.depth + j * W.rows
        W.img = group(
            [
                (W.ref.at[:, rows_at(t * C + device[1] * B, B, B)], W.w.at[t, rows_at(start, W.rows, 16), :], device)
                for device in img_peers
                for t in range(W.wide)
            ],
            W.w.at[:, 0 : (J - 1) * W.rows, :],
        )

    def own_img(W):
        start = d * W.depth + j * W.rows
        for t in range(W.wide):
            W.w[t, rows_at(start, W.rows, 16), :] = W.ref[:, rows_at(t * C + j * B, B, B)]

    def block(W, ref, owner):
        return ref.at[:, rows_at(owner * W.depth, W.depth, 16), :]

    def img_done(W):
        W.img.wait_recv()

    above, below = z < Z - 1, z > 0
    up, down = ((z + 1) * 2 + xx, j), ((z - 1) * 2 + xx, j)

    def piece(W, start, size):
        p = types.SimpleNamespace(W=W, start=start, size=size)
        p.zr, p.xr, p.zs, p.xs = wires.slot(1, Z), wires.slot(1), wires.slot(0), wires.slot(0)
        p.at = lambda owner: W.w.at[:, rows_at(owner * W.depth + start, size, 16), :]
        p.first = lambda count: W.w.at[:, 0 : count * size, :]

        def finish():
            wires.copy(p.xs, p.xr, p.first(Z), p.first(Z), xpeer).wait_send()
            for count, gate in ((Z + 1, above & below), (1, (z == 0) | (z == Z - 1))):
                pl.when(gate)(
                    lambda: wires.copy(p.zs, p.xr, p.first(count), p.first(count), xpeer).wait_send()
                )

        wires.held.append(finish)
        return p

    def move(p, owner, device):
        here = p.at(owner * 2 + xx)
        wires.copy(p.zs, p.zr + owner, here, here, device).start()

    def across(p, owner):
        here = p.at(owner * 2 + xx)
        wires.copy(p.xs, p.xr, here, here, xpeer).start()

    def z_start(pieces):
        for p in pieces:
            pl.when(above)(lambda: move(p, z, up))
            pl.when(below)(lambda: move(p, z, down))
        for p in pieces:
            across(p, z)

    def z_step(pieces, step):
        def take(owner, onward, device):
            for p in pieces:
                here = p.at(owner * 2 + xx)
                wires.copy(p.zs, p.zr + owner, here, here, xpeer).wait_recv()
                if step < Z - 1:
                    pl.when(onward)(lambda: move(p, owner, device))
                across(p, owner)

        pl.when(z >= step)(lambda: take(z - step, above, up))
        pl.when(z + step < Z)(lambda: take(z + step, below, down))

    def arrive(pieces):
        for p in pieces:
            wires.copy(p.xs, p.xr, p.first(Z), p.first(Z), xpeer).wait_recv()

    def halves(W):
        half = W.depth // 32 * 16
        return [piece(W, 0, half), piece(W, half, W.depth - half)]

    p1, p2 = halves(c1), halves(c2)
    pq, pc, po = ([piece(W, 0, W.depth)] for W in rest)

    def gather_start(mine):
        return types.SimpleNamespace(y=send(mine, mine, ypeer), c=send(mine, mine, sib))

    def gather_near(state):
        state.c.wait_recv()

    def gather_far(state, theirs):
        state.y.wait_recv()
        state.f = send(theirs, theirs, sib)

    def gather_end(state):
        state.f.wait_recv()

    stage_img(c1)
    stage_img(wo)
    v_stage1 = group([(s.vown, s.vs1.at[j], device) for device in img_peers], s.vs1.at[0 : J - 1])
    x_own = s.X.at[j]
    x_state = types.SimpleNamespace(y=send(x_in, x_own, ypeer), c=send(x_in, x_own, sib))
    e_stage1 = group([(s.eall.at[d], s.eall.at[d], device) for device in dp_peers], s.eall.at[0 : N - 1])
    own_img(c1)
    s.X[j] = x_in[...]
    for W in (c2, *rest):
        own_img(W)
    for buf in (s.A1, s.A2):
        for h in range(2):
            buf[h, 0:COLS, :] = jnp.zeros((COLS, 2 * B), bf16)
            buf[h, P + COLS : P + 2 * COLS, :] = jnp.zeros((COLS, 2 * B), bf16)
    for c in range(3):
        s.S[c, 0:COLS, :] = jnp.zeros((COLS, B), bf16)
        s.S[c, P + COLS : P + 2 * COLS, :] = jnp.zeros((COLS, B), bf16)
    s.ctx[...] = jnp.zeros((B, g.X), bf16)
    s.ctx[0:T, :] = ctx_in[...]
    if TP < B:
        s.ctxs[:, TP:B, :] = jnp.zeros((N, B - TP, XN), bf16)
        s.dcxs[:, TP:B, :] = jnp.zeros((N, B - TP, 2 * B), bf16)
    img_done(c1)
    z_start(p1[:1])
    z_start(p1[1:])
    img_done(wo)
    z_start(po)
    v_stage1.wait_recv()
    total = s.vs1[0].astype(f32)
    for k in range(1, J):
        total = total + s.vs1[k].astype(f32)
    s.vsum[...] = total.astype(bf16)
    s.vs2[d] = total.astype(bf16)
    v_stage2 = group([(s.vsum, s.vs2.at[d], device) for device in dp_peers], s.vs2.at[0 : N - 1])
    stage_img(c2)

    x_state.y.wait_recv()
    far = s.X.at[(1 - yy) * 2 + cc]
    x_state.f = send(far, far, sib)
    stage_img(wq)
    stage_img(wc)
    dy_copies = group(
        [(dy_in.at[:, lanes(device[1])], s.dyj.at[rows_at(j * Q, Q, Q), :], device) for device in img_peers],
        s.dyj.at[0 : P - Q, :],
    )
    s.dyj[rows_at(j * Q, Q, Q), :] = dy_in[:, lanes(j)]
    z_step(p1[:1], 1)
    z_step(p1[1:] + po, 1)

    e_stage1.wait_recv()
    s.wemb[...] = jnp.zeros((2 * RE, 2 * C), bf16)
    s.wemb[rows_at(lax.rem(flat, 2) * RE, RE, 16), :] = w_emb[...]
    e_at = rows_at(lax.div(flat, 2) * (2 * RE), 2 * RE, B)
    e_rows = jnp.concatenate([s.eall[k, :, e_at] for k in range(N)], axis=0)
    part = mm(e_rows.astype(bf16), s.wemb[...])
    for k in range(N):
        s.epart[k] = part[k : k + 1]
    s.erx[d] = s.epart[d]
    e_stage2 = group([(s.epart.at[device[0]], s.erx.at[d], device) for device in dp_peers], s.erx.at[0 : N - 1])

    x_state.c.wait_recv()
    x_state.f.wait_recv()

    def load_x(k):
        return lambda i: s.X[i, :, k * B : (k + 1) * B].astype(f32)

    def stats(k):
        mean, inverse = moments(load_x(k))
        s.st1[k, 0:1, :] = mean
        s.st1[k, 1:2, :] = inverse

    stats(0)
    stats(1)
    z_step(p1[:1], 2)
    z_step(p1[1:] + po, 2)
    img_done(c2)
    z_start(p2[:1])
    z_start(p2[1:])
    stats(2)
    stats(3)
    e_stage2.wait_recv()
    total = s.erx[0]
    for k in range(1, N):
        total = total + s.erx[k]
    s.esum[j] = total
    e_stage3 = group([(s.esum.at[j], s.esum.at[j], device) for device in img_peers], s.esum.at[0 : J - 1])
    v_stage2.wait_recv()
    total = s.vs2[0].astype(f32)
    for k in range(1, N):
        total = total + s.vs2[k].astype(f32)
    for k in range(J):
        s.vecs[k] = total[:, k * B : (k + 1) * B]

    def vec(row):
        return s.vecs[j, row : row + 1, :]

    z_step(p1[:1], 3)
    z_step(p1[1:] + po, 3)
    for k in range(J):
        mean, inverse = s.st1[k, 0:1, :], s.st1[k, 1:2, :]
        gain, bias = s.vecs[k, 0:1, :], s.vecs[k, 1:2, :]
        load = load_x(k)

        def act(i):
            t1 = (load(i) - mean) * inverse * gain + bias
            a1 = t1 * jax.nn.sigmoid(t1)
            s.A1[k // 2, rows_at(i * Q + COLS, Q, COLS), (k % 2) * B : (k % 2 + 1) * B] = a1.astype(bf16)

        each(act)

    def turn(source, target, offset):
        def one(i):
            for h in range(2):
                v = source[h, rows_at(i * Q + offset, Q, 16), :]
                target[h * 2 * B : (h + 1) * 2 * B, px(i)] = v.T
        each(one)

    each(lambda i: s.xj.__setitem__((px(i), slice(None)), s.X[i, :, lanes(j)]))
    z_step(p2[:1], 1)
    z_step(p2[1:], 1)
    e_stage3.wait_recv()
    total = s.esum[0]
    for k in range(1, J):
        total = total + s.esum[k]
    s.emb[...] = total
    scale = 1.0 + (s.emb[:, lanes(j)] + vec(14))
    shift = s.emb[:, lanes(j + J)] + vec(15)
    arrive(po)
    wo_at = s.WoF.at[yy, :, lanes(cc)]
    s.WoF[yy, :, lanes(cc)] = wo.w[0]
    wo_state = gather_start(wo_at)
    arrive(p1)

    def convolve(A, W, emit):
        def one(i):
            left = jnp.concatenate(
                [A[h, rows_at(i * Q + r * COLS, Q, COLS), :] for r in range(3) for h in range(2)], axis=1
            )
            right = jnp.concatenate(
                [
                    jnp.concatenate([W[0, (3 * r + c) * C : (3 * r + c + 1) * C, :] for r in range(3)], axis=0)
                    for c in range(3)
                ],
                axis=1,
            )
            p = mm(left, right)
            emit(i, p[:, B : 2 * B] + from_left(p[:, :B]) + from_right(p[:, 2 * B :]))
        each(one)

    def save_h1(i, v):
        s.h1[px(i), :] = v + vec(2)

    convolve(s.A1, c1.w, save_h1)
    mean2, inv2 = moments(lambda i: s.h1[px(i), :])
    gather_far(wo_state, s.WoF.at[1 - yy, :, lanes(cc)])
    gather_near(wo_state)
    gather_end(wo_state)

    def xh2(i):
        return (s.h1[px(i), :] - mean2) * inv2

    def u_of(i):
        return (xh2(i) * vec(3) + vec(4)) * scale + shift

    def act2(i):
        u = u_of(i)
        s.A2[yy, rows_at(i * Q + COLS, Q, COLS), lanes(cc)] = (u * jax.nn.sigmoid(u)).astype(bf16)

    each(act2)
    inside = pl.ds(COLS, P)
    a2_state = gather_start(s.A2.at[yy, inside, lanes(cc)])
    for h in range(2):
        part = mm_t(dy_in[:, 0 : 2 * B], s.WoF[0, h * 2 * B : (h + 1) * 2 * B, :])
        part = part + mm_t(dy_in[:, 2 * B : 4 * B], s.WoF[1, h * 2 * B : (h + 1) * 2 * B, :])
        s.dopx[:, h * 2 * B : (h + 1) * 2 * B] = part.astype(bf16)
    do_copies = group(
        [(s.dopx.at[:, lanes(device[1])], s.doj.at[rows_at(j * Q, Q, Q), :], device) for device in img_peers],
        s.doj.at[0 : P - Q, :],
    )
    s.doj[rows_at(j * Q, Q, Q), :] = s.dopx[:, lanes(j)]
    z_step(p2[:1], 2)
    z_step(p2[1:], 2)
    img_done(wq)
    img_done(wc)
    z_start(pq)
    z_start(pc)
    z_step(p2[:1], 3)
    z_step(p2[1:], 3)
    gather_far(a2_state, s.A2.at[1 - yy, inside, lanes(cc)])
    turn(s.A1, s.A1T, COLS)
    z_step(pq, 1)
    z_step(pc, 1)
    gather_near(a2_state)
    gather_end(a2_state)
    arrive(p2)

    def save_y1(i, v):
        s.y1[px(i), :] = s.xj[px(i), :].astype(f32) + v + vec(5)

    convolve(s.A2, c2.w, save_y1)
    mean3, inv3 = moments(lambda i: s.y1[px(i), :])

    def xh3(i):
        return (s.y1[px(i), :] - mean3) * inv3

    def act3(i):
        s.N3[yy, px(i), lanes(cc)] = (xh3(i) * vec(6) + vec(7)).astype(bf16)

    each(act3)
    n_state = gather_start(s.N3.at[yy, :, lanes(cc)])
    z_step(pq, 2)
    z_step(pc, 2)
    turn(s.A2, s.A2T, COLS)

    def turn_weights(W, target, taps, stride):
        for h in range(2):
            for t in range(taps):
                v = W(t)[rows_at(h * 2 * B, 2 * B, 16), :]
                target[h, t * B : (t + 1) * B, :] = v.T

    def conv_tap(W):
        return lambda t: W.w.at[0, pl.ds(t * C, C), :]

    turn_weights(conv_tap(c2), s.W2T, 9, C)
    gather_far(n_state, s.N3.at[1 - yy, :, lanes(cc)])
    z_step(pq, 3)
    z_step(pc, 3)
    turn_weights(conv_tap(c1), s.W1T, 9, C)
    arrive(pq)
    arrive(pc)
    turn_weights(lambda t: wq.w.at[t], s.WqT, 3, C)
    tokens = lax.broadcasted_iota(jnp.int32, (B, B), 0) < T
    for t, target in enumerate((s.Kb, s.Vb)):
        v = mm(s.ctx[...], wc.w[t]) + vec(12 + t)
        target[P : P + B, :] = jnp.where(tokens, v, 0.0).astype(bf16)
    gather_near(n_state)
    gather_end(n_state)

    def tokens_of(owner):
        return s.ctx.at[0:TP, rows_at(owner * XN, XN, B)]

    ctx_copies = group(
        [(tokens_of(device[0]), s.ctxs.at[d, 0:TP, :], device) for device in dp_peers],
        s.ctxs.at[0 : N - 1, 0:TP, :],
    )
    s.ctxs[d, 0:TP, :] = tokens_of(d)[...]

    def project(i):
        left = jnp.concatenate([s.N3[0, px(i), :], s.N3[1, px(i), :]], axis=1)
        right = jnp.concatenate([wq.w[t] for t in range(3)], axis=1)
        v = mm(left, right)
        q = (v[:, :B] + vec(9)).astype(bf16)
        s.qs[px(i), :] = (q.astype(f32) * g.FACTOR).astype(bf16)
        s.Kb[px(i), :] = (v[:, B : 2 * B] + vec(10)).astype(bf16)
        s.Vb[px(i), :] = (v[:, 2 * B :] + vec(11)).astype(bf16)

    each(project)
    for source, target in ((s.Kb, s.KT), (s.Vb, s.VT)):
        for k in range(0, P + B, B):
            target[:, k : k + B] = source[k : k + B, :].T
    do_copies.wait_recv()
    dy_copies.wait_recv()
    s.dK[...] = jnp.zeros((P + B, B), f32)
    s.dV[...] = jnp.zeros((P + B, B), f32)

    HEAD_ = g.HEAD
    lane_row = lax.broadcasted_iota(jnp.int32, (1, B), 1)
    span = 2 * Q
    known = lax.broadcasted_iota(jnp.int32, (B, span), 0) < T
    keeps = [jnp.where(lax.div(lane_row, HEAD_) == h, 1.0, 0.0).astype(bf16) for h in range(B // HEAD_)]

    def attend(i, carry):
        at = rows_at(i * span, span, span)
        q_i, do_i = s.qs[at, :], s.doj[at, :]
        q_m = jnp.concatenate([q_i * keep for keep in keeps], axis=0)
        do_m = jnp.concatenate([do_i * keep for keep in keeps], axis=0)
        all_scores, all_dp = mm_t(s.Kb[...], q_m), mm_t(s.Vb[...], do_m)
        low, slope, mixed, back = [], [], [], []
        for h in range(B // HEAD_):
            scores = all_scores[:, h * span : (h + 1) * span]
            scores = jnp.concatenate([scores[:P], jnp.where(known, scores[P:], -1e30)], axis=0)
            e = jnp.exp(scores - jnp.max(scores, axis=0, keepdims=True))
            probs = e * (1.0 / jnp.sum(e, axis=0, keepdims=True))
            pb = probs.astype(bf16)
            mixed.append(mm(s.VT[h * HEAD_ : (h + 1) * HEAD_, :], pb))
            dp = all_dp[:, h * span : (h + 1) * span]
            ds = (probs * (dp - jnp.sum(dp * probs, axis=0, keepdims=True))).astype(bf16)
            back.append(mm(s.KT[h * HEAD_ : (h + 1) * HEAD_, :], ds))
            low.append(pb)
            slope.append(ds)
        s.dV[...] += mm(jnp.concatenate(low, axis=1), do_m)
        s.dK[...] += mm(jnp.concatenate(slope, axis=1), q_m)
        s.O[yy, at, lanes(cc)] = jnp.concatenate(mixed, axis=0).T.astype(bf16)
        s.dqkv[0, at, :] = (jnp.concatenate(back, axis=0).T * g.FACTOR).astype(bf16)
        return carry

    lax.fori_loop(0, P // span, attend, 0)
    o_state = gather_start(s.O.at[yy, :, lanes(cc)])

    def grads_kv(i):
        s.dqkv[1, px(i), :] = s.dK[px(i), :].astype(bf16)
        s.dqkv[2, px(i), :] = s.dV[px(i), :].astype(bf16)

    each(grads_kv)

    def scatter(bufs, left, right):
        ps, rc, sy, ry = bufs.ps, bufs.rc, bufs.sy, bufs.ry
        near = []
        for slot in range(2):
            half = 1 - yy if slot == 0 else yy

            def one(i):
                v = mm(left(i), right[half]).astype(bf16)
                ps[slot, 0, px(i), :] = v[:, :B]
                ps[slot, 1, px(i), :] = v[:, B:]

            each(one)
            near.append(send(ps.at[slot, 1 - cc], rc.at[slot], sib))
            if slot == 0:
                near[0].wait_recv()

                def add(i):
                    v = ps[0, cc, px(i), :].astype(f32) + rc[0, px(i), :].astype(f32)
                    sy[px(i), :] = v.astype(bf16)

                each(add)
                across = send(sy, ry, ypeer)

        def done():
            near[1].wait_recv()
            across.wait_recv()

        def load(i):
            v = ps[1, cc, px(i), :].astype(f32) + rc[1, px(i), :].astype(f32)
            return v + ry[px(i), :].astype(f32)

        return done, load

    order = list(range(1, Z)) + [0]

    def sum_start(W):
        W.sx, W.zout, W.zin = {}, wires.slot(0), wires.slot(1)
        out = wires.slot(0)
        for k in order:
            W.sx[k] = send(block(W, W.g, zdev[k] * 2 + (1 - xx)), W.rx.at[k], xpeer, out)
        wires.held.append(wires.copy(out, W.zin, W.rx, W.rx, xpeer).wait_send)

    def sum_block(W, k):
        W.sx[k].wait_recv()
        at = rows_at((zdev[k] * 2 + xx) * W.depth, W.depth, 16)
        v = W.g[:, at, :].astype(f32) + W.rx[k].astype(f32)
        W.zs[k] = v.astype(bf16)
        if k:
            wires.copy(W.zout, W.zin, W.zs.at[k], W.zr.at[k], (zdev[k] * 2 + xx, j)).start()

    def sum_z(W):
        for k in order:
            sum_block(W, k)

    def sum_img(W):
        total = wires.copy(W.zout, W.zin, W.zr.at[0 : Z - 1], W.zr.at[0 : Z - 1], xpeer)
        total.wait_recv()
        wires.held.append(total.wait_send)
        v = W.zs[0].astype(f32)
        for k in range(1, Z):
            v = v + W.zr[k].astype(f32)
        to_rows(W, jnp.concatenate([v[t] for t in range(W.wide)], axis=1))

    def to_rows(W, v):
        for t in range(W.wide):
            W.fin[t] = v[:, t * B : (t + 1) * B].astype(bf16)
        W.simg = group(
            [
                (W.fin.at[:, rows_at(device[1] * W.rows, W.rows, 16), :], W.gr.at[j], device)
                for device in img_peers
            ],
            W.gr.at[0 : J - 1],
        )
        W.gr[j] = W.fin[:, rows_at(j * W.rows, W.rows, 16), :]

    def sum_end(W, target):
        W.simg.wait_recv()
        for k in range(J):
            for t in range(W.wide):
                target[:, t * C + k * B : t * C + (k + 1) * B] = W.gr[k, t].astype(f32)

    dn_done, dn_at = scatter(
        dn_bufs, lambda i: jnp.concatenate([s.dqkv[t, px(i), :] for t in range(3)], axis=1), s.WqT
    )
    turn(s.N3, s.N3T, 0)
    for h in range(2):
        at = slice(h * 2 * B, (h + 1) * 2 * B)
        v = mm(s.N3T[at, :], jnp.concatenate([s.dqkv[t] for t in range(3)], axis=1)).astype(bf16)
        for t in range(3):
            wq.g[t, at, :] = v[:, t * B : (t + 1) * B]
    sum_start(wq)
    s.dcx[...] = jnp.concatenate([s.dK[P : P + B, :], s.dV[P : P + B, :]], axis=1).astype(bf16)
    s.dcxs[d] = s.dcx[...]
    dcx_copies = group(
        [(s.dcx.at[0:TP, :], s.dcxs.at[d, 0:TP, :], device) for device in dp_peers],
        s.dcxs.at[0 : N - 1, 0:TP, :],
    )
    gather_far(o_state, s.O.at[1 - yy, :, lanes(cc)])
    gather_near(o_state)
    gather_end(o_state)

    def finish(i):
        left = jnp.concatenate([s.O[0, px(i), :], s.O[1, px(i), :]], axis=1)
        s.outj[px(i), :] = (s.y1[px(i), :] + mm(left, wo.w[0]) + vec(8)).astype(bf16)

    each(finish)

    def to_pixels(source, target):
        copies = group(
            [(source.at[rows_at(device[1] * Q, Q, Q), :], target.at[:, lanes(j)], device) for device in img_peers],
            source.at[0 : P - Q, :],
        )
        target[:, lanes(j)] = source[rows_at(j * Q, Q, Q), :]
        return copies

    out_copies = to_pixels(s.outj, out)
    turn(s.O, s.OT, 0)
    for h in range(2):
        at = slice(h * 2 * B, (h + 1) * 2 * B)
        wo.g[0, at, :] = mm(s.OT[at, :], s.dyj[...]).astype(bf16)
    sum_start(wo)

    def back_sums(grad, normed, factor):
        def one(i, carry):
            v = grad(i)
            return carry[0] + colsum(v), carry[1] + colsum(v * normed(i))
        first, second = each(one, (zero_row, zero_row))
        return first, second, group_sum(first * factor) * (1.0 / count), group_sum(second * factor) * (1.0 / count)

    dn_done()
    sum_z(wq)
    dn_sum, dn_hat, m1, m2 = back_sums(dn_at, xh3, vec(6))

    def shifted(i, v):
        at = rows_at(i * Q + COLS, Q, COLS)
        s.S[0, at, :] = from_right(v).astype(bf16)
        s.S[1, at, :] = v.astype(bf16)
        s.S[2, at, :] = from_left(v).astype(bf16)

    def make_dh2(i, carry):
        dy = s.dyj[px(i), :].astype(f32)
        v = dy + (dn_at(i) * vec(6) - m1 - xh3(i) * m2) * inv3
        s.dy1[px(i), :] = v
        low = v.astype(bf16).astype(f32)
        shifted(i, low)
        return carry[0] + colsum(low), carry[1] + colsum(dy)

    dh2_sum, dy_sum = each(make_dh2, (zero_row, zero_row))

    def tap(t, start, size):
        r, c = t // 3, t % 3
        return s.S[c, rows_at(start + (2 - r) * COLS, size, COLS), :]

    def field(i):
        return jnp.concatenate([tap(t, i * Q, Q) for t in range(9)], axis=1)

    def kernel_grad(W, turned):
        for h in range(2):
            at = slice(h * 2 * B, (h + 1) * 2 * B)
            v = mm(turned[at, :], jnp.concatenate([tap(t, 0, P) for t in range(9)], axis=1)).astype(bf16)
            for t in range(9):
                W.g[0, t * C + h * 2 * B : t * C + (h + 1) * 2 * B, :] = v[:, t * B : (t + 1) * B]

    da2_done, da2_at = scatter(da2_bufs, field, s.W2T)
    kernel_grad(c2, s.A2T)
    sum_start(c2)
    sum_z(wo)
    ctx_copies.wait_recv()
    dcx_copies.wait_recv()
    v = lax.dot_general(
        s.ctxs[...].reshape(N * B, XN), s.dcxs[...].reshape(N * B, 2 * B), (((0,), (0,)), ((), ())),
        preferred_element_type=f32,
    )
    to_rows(wc, v)
    da2_done()

    def slope_of(v):
        sigma = jax.nn.sigmoid(v)
        return sigma * (1.0 + v * (1.0 - sigma))

    def make_du(i, carry):
        du = da2_at(i) * slope_of(u_of(i))
        s.tmp[px(i), :] = du
        return carry[0] + colsum(du), carry[1] + colsum(du * xh2(i))

    du_sum, du_hat = each(make_du, (zero_row, zero_row))
    gain2 = scale * vec(3)
    m1b = group_sum(du_sum * gain2) * (1.0 / count)
    m2b = group_sum(du_hat * gain2) * (1.0 / count)

    def make_dh1(i, carry):
        v = (s.tmp[px(i), :] * gain2 - m1b - xh2(i) * m2b) * inv2
        low = v.astype(bf16).astype(f32)
        shifted(i, low)
        return carry + colsum(low)

    dh1_sum = each(make_dh1, zero_row)
    dscale = vec(3) * du_hat + vec(4) * du_sum
    kernel_grad(c1, s.A1T)
    sum_start(c1)
    da1_done, da1_at = scatter(da1_bufs, field, s.W1T)
    s.dse[j] = jnp.concatenate([dscale, du_sum], axis=0)
    ds_copies = group([(s.dse.at[j], s.dse.at[j], device) for device in img_peers], s.dse.at[0 : J - 1])
    sum_img(wq)
    sum_img(wo)
    sum_z(c2)
    ds_copies.wait_recv()
    s.dsall[d] = s.dse[...]
    ds_copies = group([(s.dse, s.dsall.at[d], device) for device in dp_peers], s.dsall.at[0 : N - 1])
    da1_done()
    mean1, inv1 = s.st1[j, 0:1, :], s.st1[j, 1:2, :]

    def xh1(i):
        return (s.xj[px(i), :].astype(f32) - mean1) * inv1

    def make_dt1(i, carry):
        n1 = xh1(i)
        dt1 = da1_at(i) * slope_of(n1 * vec(0) + vec(1))
        s.tmp[px(i), :] = dt1
        return carry[0] + colsum(dt1), carry[1] + colsum(dt1 * n1)

    dt1_sum, dt1_hat = each(make_dt1, (zero_row, zero_row))
    m1c = group_sum(dt1_sum * vec(0)) * (1.0 / count)
    m2c = group_sum(dt1_hat * vec(0)) * (1.0 / count)

    def make_in(i):
        v = s.dy1[px(i), :] + (s.tmp[px(i), :] * vec(0) - m1c - xh1(i) * m2c) * inv1
        s.inj[px(i), :] = v.astype(bf16)

    each(make_in)
    in_copies = to_pixels(s.inj, in_grad)

    qkv_sums = [each(lambda i, a, t=t: a + colsum(s.dqkv[t, px(i), :].astype(f32)), zero_row) for t in range(3)]
    s.gvec[...] = jnp.concatenate(
        [dt1_hat, dt1_sum, dh1_sum, scale * du_hat, scale * du_sum, dh2_sum, dn_hat, dn_sum, dy_sum]
        + qkv_sums
        + [colsum(s.dK[P : P + B, :]), colsum(s.dV[P : P + B, :]), dscale, du_sum],
        axis=0,
    )
    gv_copies = group([(s.gvec, s.gvs.at[d], device) for device in dp_peers], s.gvs.at[0 : N - 1])
    s.gvs[d] = s.gvec[...]
    sum_z(c1)
    gv_copies.wait_recv()
    total = s.gvs[0]
    for k in range(1, N):
        total = total + s.gvs[k]
    s.gvt[...] = total
    s.gvi[j] = total
    gv_copies = group([(s.gvt, s.gvi.at[j], device) for device in img_peers], s.gvi.at[0 : J - 1])
    sum_img(c2)
    sum_end(wq, g_q)
    sum_end(wc, g_c)
    sum_end(wo, g_o)
    ds_copies.wait_recv()
    e_cols = jnp.concatenate([s.eall[k, :, e_at] for k in range(N)], axis=0)
    for t in range(2):
        for k in range(J):
            rows = jnp.concatenate([s.dsall[i, k, t : t + 1, :] for i in range(N)], axis=0)
            v = lax.dot_general(
                e_cols, rows, (((0,), (0,)), ((), ())), precision=highest, preferred_element_type=f32
            )
            s.geb[:, t * C + k * B : t * C + (k + 1) * B] = v
    g_emb[...] = s.geb[rows_at(lax.rem(flat, 2) * RE, RE, 8), :]
    gv_copies.wait_recv()
    VW = g.VW
    each_block = B // VW
    pick = lax.broadcasted_iota(jnp.int32, (B, VW), 0) == (
        lax.broadcasted_iota(jnp.int32, (B, VW), 1) + lax.rem(flat, each_block) * VW
    )
    g_v[...] = jnp.dot(
        s.gvi[lax.div(flat, each_block)], jnp.where(pick, 1.0, 0.0), precision=highest,
        preferred_element_type=f32,
    )
    sum_end(c2, gc2)
    sum_img(c1)
    sum_end(c1, gc1)
    out_copies.wait_recv()
    in_copies.wait_recv()
    wires.drain()
    assert wires.used[0] <= g.copies[0] and wires.used[1] <= g.copies[1], wires.used


def hand_over(*refs):
    count = len(refs) // 2
    for k in range(count):
        refs[count + k][...] = refs[k][...].astype(refs[count + k].dtype)


def fused(
    image, cond, context, w_conv1, w_conv2, w_embed, w_qkv, w_context, w_out, vectors, cotangent
):
    J, N = lax.axis_size("img"), lax.axis_size("dp")
    local, cols, chans = image.shape[1:]
    g = types.SimpleNamespace(
        P=local * cols * J, Q=local * cols, C=chans, B=chans // J, N=N, J=J, COLS=cols, SIZE=chans // GROUPS,
        T=context.shape[1], X=context.shape[2], E=cond.shape[1], RE=w_embed.shape[0], VW=vectors.shape[1],
        HEAD=HEAD, FACTOR=HEAD ** (-0.5),
        weights=[
            (1, w_conv1.shape[0]), (1, w_conv2.shape[0]), (3, w_qkv.shape[0]), (2, w_context.shape[0]),
            (1, w_out.shape[0]),
        ],
    )
    groups = scratch_plan(g)
    rows = local * cols
    shape = jax.ShapeDtypeStruct
    outs = [
        shape((rows, chans), bf16), shape((rows, chans), bf16), shape(w_conv1.shape, f32), shape(w_conv2.shape, f32),
        shape(w_embed.shape, f32), shape(w_qkv.shape, f32), shape(w_context.shape, f32), shape(w_out.shape, f32),
        shape(vectors.shape, f32),
    ]
    g.copies = (71, 49 + 11 * (N // 2 + 1))
    vmem = pl.BlockSpec(memory_space=pltpu.VMEM)
    result = pl.pallas_call(
        functools.partial(body, g, groups),
        out_shape=outs,
        in_specs=[vmem] * 11,
        out_specs=[vmem] * 9,
        scratch_shapes=[pltpu.VMEM(*spec) for group in groups for spec in group.values()]
        + [pltpu.SemaphoreType.DMA((count,)) for count in g.copies],
        compiler_params=pltpu.CompilerParams(
            collective_id=0, has_side_effects=True, vmem_limit_bytes=60 * 1024 * 1024
        ),
    )(
        image.reshape(rows, chans), cond, context[0], w_conv1, w_conv2, w_embed, w_qkv, w_context, w_out, vectors,
        cotangent.reshape(rows, chans),
    )
    count = len(outs)
    result = pl.pallas_call(
        hand_over, out_shape=outs, in_specs=[vmem] * count, out_specs=[vmem] * count,
    )(*result)
    return (result[0].reshape(image.shape), result[1].reshape(image.shape), *result[2:])


def on_device(
    image, cond, context, w_conv1, w_conv2, w_embed, w_qkv, w_context, w_out, vectors, cotangent
):
    parts = lax.axis_size("img")
    place = lax.axis_index("img")
    images = lax.axis_size("dp")
    rows, cols, chans = image.shape[1] * parts, image.shape[2], image.shape[3]
    pixels = rows * cols
    width = chans // parts
    size = chans // GROUPS
    count = images * parts

    if parts == 4 and width == 128 and images % 2 == 0 and all(
        w.shape[0] % 16 == 0 for w in (w_conv1, w_conv2, w_embed, w_qkv, w_context, w_out)
    ):
        return fused(
            image, cond, context, w_conv1, w_conv2, w_embed, w_qkv, w_context, w_out, vectors, cotangent
        )

    def own(full):
        return lax.dynamic_slice_in_dim(full, place * width, width, full.ndim - 1)

    shards = (w_conv1, w_conv2, w_qkv, w_context, w_embed, w_out)
    lengths = [w.shape[0] * (w.shape[1] // chans) for w in shards]
    packed = jnp.concatenate([columns(w, parts) for w in shards], 1)
    packed = lax.all_to_all(packed, "img", 0, 0, tiled=True)
    packed = lax.all_gather(packed, "dp", axis=0, tiled=True)
    full = []
    start = 0
    for w, length in zip(shards, lengths):
        wide = w.shape[1] // chans
        piece = packed[:, start : start + length].reshape(count, wide, w.shape[0], width)
        full.append(piece.transpose(0, 2, 1, 3).reshape(count * w.shape[0], wide * width))
        start += length
    k1, k2, kq, kc, ke, ko = full
    vec_all = lax.all_gather(vectors, ("dp", "img"), axis=1, tiled=True).astype(f32)
    vec = own(vec_all)

    x_low = lax.all_gather(image[0].reshape(-1, chans), "img", axis=0, tiled=True)
    x_all = x_low.astype(f32)
    normed1_all, inverse1_all = group_norm(x_all, size)
    act1 = jax.nn.silu(normed1_all * vec_all[0] + vec_all[1]).astype(bf16)
    normed1 = own(normed1_all)
    inverse1 = lax.dynamic_slice_in_dim(inverse1_all, place * (GROUPS // parts), GROUPS // parts, 1)
    pre1 = normed1 * vec[0] + vec[1]
    hidden1 = dot(taps_of(act1, rows, cols, False), k1) + vec[2]
    cond_act = jax.nn.silu(cond.astype(f32)).astype(bf16)
    embed = dot(cond_act, ke)[0]
    scale = embed[:width] + vec[14]
    shift = embed[width:] + vec[15]
    normed2, inverse2 = group_norm(hidden1, size)
    affine2 = normed2 * vec[3] + vec[4]
    pre2 = affine2 * (1.0 + scale) + shift
    act2_own = jax.nn.silu(pre2).astype(bf16)
    act2 = lax.all_gather(act2_own, "img", axis=1, tiled=True)
    resid = own(x_all) + dot(taps_of(act2, rows, cols, False), k2) + vec[5]
    normed3, inverse3 = group_norm(resid, size)
    affine3_own = (normed3 * vec[6] + vec[7]).astype(bf16)
    affine3 = lax.all_gather(affine3_own, "img", axis=1, tiled=True)
    qkv = (dot(affine3, kq) + jnp.concatenate([vec[9], vec[10], vec[11]])).astype(bf16)
    ctx = (dot(context[0], kc) + jnp.concatenate([vec[12], vec[13]])).astype(bf16)
    tokens = ctx.shape[0]

    out_full = lax.all_gather(ko, "img", axis=1, tiled=True)
    dy_px = cotangent[0].reshape(-1, chans)
    do_px = lax.dot_general(dy_px, out_full, (((1,), (1,)), ((), ())), preferred_element_type=f32).astype(bf16)
    both = jnp.stack([do_px, dy_px])
    both = lax.all_to_all(both, "img", 2, 1, tiled=True)
    do, dy = both[0], both[1]
    dy_wide = dy.astype(f32)

    keys = jnp.concatenate([ctx[:, :width], qkv[:, width : 2 * width]], 0)
    values = jnp.concatenate([ctx[:, width:], qkv[:, 2 * width :]], 0)
    factor = HEAD ** (-0.5)
    mixed, dq, dk, dv = [], [], [], []
    for h in range(width // HEAD):
        at = slice(h * HEAD, (h + 1) * HEAD)
        q_h, k_h, v_h, do_h = qkv[:, at], keys[:, at], values[:, at], do[:, at]
        scores = dot(k_h, q_h.T) * factor
        top = jnp.max(scores, 0, keepdims=True)
        weights = jnp.exp(scores - top)
        probs = weights / jnp.sum(weights, 0, keepdims=True)
        low = probs.astype(bf16)
        mixed.append(dot(v_h.T, low).T)
        dv.append(dot(low, do_h))
        dp = dot(v_h, do_h.T)
        ds = (probs * (dp - jnp.sum(dp * probs, 0, keepdims=True))).astype(bf16)
        dq.append(dot(k_h.T, ds).T * factor)
        dk.append(dot(ds, q_h) * factor)
    mixed = jnp.concatenate(mixed, 1).astype(bf16)
    dq, dk, dv = (jnp.concatenate(v, 1) for v in (dq, dk, dv))
    mixed_all = lax.all_gather(mixed, "img", axis=1, tiled=True)
    output = (resid + dot(mixed_all, ko) + vec[8]).astype(bf16)

    dqkv = jnp.concatenate([dq, dk[tokens:], dv[tokens:]], 1).astype(bf16)
    dctx = jnp.concatenate([dk[:tokens], dv[:tokens]], 1)
    dn_part = lax.dot_general(dqkv, kq, (((1,), (1,)), ((), ())), preferred_element_type=f32)
    dn = lax.psum_scatter(dn_part.astype(bf16), "img", scatter_dimension=1, tiled=True).astype(f32)
    dy1 = dy_wide + group_back(dn * vec[6], normed3, inverse3, size)
    dh2 = dy1.astype(bf16)

    def turned(kernel):
        return kernel.reshape(9, chans, width).transpose(0, 2, 1).reshape(9 * width, chans)

    def conv_back(dh, kernel, act):
        field = taps_of(dh, rows, cols, True)
        part = dot(field, turned(kernel)).astype(bf16)
        grad = lax.psum_scatter(part, "img", scatter_dimension=1, tiled=True).astype(f32)
        kernel_grad = lax.dot_general(act, field, (((0,), (0,)), ((), ())), preferred_element_type=f32)
        return grad, kernel_grad.reshape(chans, 9, width).transpose(1, 0, 2).reshape(9 * chans, width)

    da2, gk2 = conv_back(dh2, k2, act2)
    du = da2 * silu_slope(pre2)
    dscale = jnp.sum(du * affine2, 0)
    dshift = jnp.sum(du, 0)
    dz = du * (1.0 + scale)
    dh1 = group_back(dz * vec[3], normed2, inverse2, size).astype(bf16)
    da1, gk1 = conv_back(dh1, k1, act1)
    dt1 = da1 * silu_slope(pre1)
    in_grad = (dy1 + group_back(dt1 * vec[0], normed1, inverse1, size)).astype(bf16)

    tops = lax.all_to_all(jnp.stack([output, in_grad]), "img", 1, 2, tiled=True)
    gkq = lax.dot_general(affine3, dqkv, (((0,), (0,)), ((), ())), preferred_element_type=f32)
    gkc = lax.dot_general(context[0], dctx.astype(bf16), (((0,), (0,)), ((), ())), preferred_element_type=f32)
    gko = lax.dot_general(mixed_all, dy, (((0,), (0,)), ((), ())), preferred_element_type=f32)
    gke = cond_act[0].astype(f32)[:, None] * jnp.concatenate([dscale, dshift])[None, :]
    grad_vec = jnp.stack(
        [
            jnp.sum(dt1 * normed1, 0),
            jnp.sum(dt1, 0),
            jnp.sum(dh1.astype(f32), 0),
            jnp.sum(dz * normed2, 0),
            jnp.sum(dz, 0),
            jnp.sum(dh2.astype(f32), 0),
            jnp.sum(dn * normed3, 0),
            jnp.sum(dn, 0),
            jnp.sum(dy_wide, 0),
        ]
        + [jnp.sum(v.astype(f32), 0) for v in jnp.split(dqkv, 3, 1)]
        + [jnp.sum(v, 0) for v in jnp.split(dctx, 2, 1)]
        + [dscale, dshift],
        0,
    )
    grads = (gk1, gk2, gkq, gkc, gke, gko)
    pieces = []
    for w, g in zip(shards, grads):
        wide = w.shape[1] // chans
        piece = g.reshape(count, w.shape[0], wide, width).transpose(0, 2, 1, 3)
        pieces.append(piece.reshape(count, wide * w.shape[0], width))
    packed = jnp.concatenate(pieces, 1).astype(bf16)
    packed = lax.psum_scatter(packed, "dp", scatter_dimension=0, tiled=True).astype(f32)
    packed = lax.all_to_all(packed.astype(bf16), "img", 0, 0, tiled=True).astype(f32)
    outs = []
    start = 0
    for w, length in zip(shards, lengths):
        wide = w.shape[1] // chans
        piece = packed[:, start : start + length].reshape(parts, wide, w.shape[0], width)
        outs.append(piece.transpose(2, 1, 0, 3).reshape(w.shape))
        start += length
    vec_sum = lax.all_gather(lax.psum(grad_vec, "dp"), "img", axis=1, tiled=True)
    each = chans // count
    g_vec = lax.dynamic_slice_in_dim(
        vec_sum, (lax.axis_index("dp") * parts + place) * each, each, 1
    )
    g1, g2, gq, gc, ge, go = outs
    return (tops[0].reshape(image.shape), tops[1].reshape(image.shape), g1, g2, ge, gq, gc, go, g_vec)


def solution(mesh):
    whole = P(("dp", "img"), None)
    field = P("dp", "img", None, None)
    in_specs = (
        field, P("dp", None), P("dp", None, None), whole, whole, whole, whole, whole, whole,
        P(None, ("dp", "img")), field,
    )
    out_specs = (field, field, whole, whole, whole, whole, whole, whole, P(None, ("dp", "img")))
    return jax.shard_map(
        on_device, mesh=mesh, in_specs=in_specs, out_specs=out_specs, check_vma=False
    )
```

```python
import functools
import types

import jax
import jax.numpy as jnp
from jax import lax
from jax.experimental import pallas as pl
from jax.experimental.pallas import tpu as pltpu
from jax.sharding import PartitionSpec as P

HEADS = 8
HEAD = 64
GROUPS = 32

f32 = jnp.float32
bf16 = jnp.bfloat16
highest = lax.Precision.HIGHEST


def dot(a, b):
    return jnp.dot(a, b, preferred_element_type=f32)


def silu_slope(value):
    sigma = jax.nn.sigmoid(value)
    return sigma * (1.0 + value * (1.0 - sigma))


def group_norm(flat, size):
    pixels, chans = flat.shape
    part = flat.reshape(pixels, chans // size, size)
    mean = jnp.mean(part, axis=(0, 2), keepdims=True)
    spread = jnp.mean(jnp.square(part - mean), axis=(0, 2), keepdims=True)
    inverse = lax.rsqrt(spread + 1e-05)
    return ((part - mean) * inverse).reshape(pixels, chans), inverse


def group_back(grad, normed, inverse, size):
    pixels, chans = grad.shape
    upper = grad.reshape(pixels, chans // size, size)
    lower = normed.reshape(pixels, chans // size, size)
    first = jnp.mean(upper, axis=(0, 2), keepdims=True)
    second = jnp.mean(upper * lower, axis=(0, 2), keepdims=True)
    return ((upper - first - lower * second) * inverse).reshape(pixels, chans)


def taps_of(flat, rows, cols, flipped):
    chans = flat.shape[-1]
    padded = jnp.pad(flat.reshape(rows, cols, chans), ((1, 1), (1, 1), (0, 0)))
    pieces = []
    for r in range(3):
        for c in range(3):
            top, left = (2 - r, 2 - c) if flipped else (r, c)
            pieces.append(padded[top : top + rows, left : left + cols].reshape(rows * cols, chans))
    return jnp.concatenate(pieces, 1)


def columns(weight, parts):
    rows, chans = weight.shape
    return weight.reshape(rows, chans // (parts * 128), parts, 128).transpose(2, 1, 0, 3).reshape(parts, -1, 128)


class Wires:
    def __init__(self, sent, landed):
        self.sent, self.landed, self.used, self.held = sent, landed, [0, 0], []

    def slot(self, kind, count=1):
        self.used[kind] += count
        return self.used[kind] - count

    def copy(self, out, at, source, target, device):
        return pltpu.make_async_remote_copy(
            src_ref=source, dst_ref=target, send_sem=self.sent.at[out], recv_sem=self.landed.at[at],
            device_id=device, device_id_type=pl.DeviceIdType.MESH,
        )

    def send(self, source, target, device, out=None):
        copy = self.copy(self.slot(0) if out is None else out, self.slot(1), source, target, device)
        copy.start()
        if out is None:
            self.held.append(copy.wait_send)
        return copy

    def group(self, triples, whole):
        out, at = self.slot(0), self.slot(1)
        for source, target, device in triples:
            self.copy(out, at, source, target, device).start()
        total = self.copy(out, at, whole, whole, triples[0][2])
        self.held.append(total.wait_send)
        return total

    def drain(self):
        for finish in self.held:
            finish()


def scratch_plan(g):
    P, Q, C, B, N, J, X = g.P, g.Q, g.C, g.B, g.N, g.J, g.X
    plan = dict(
        X=((J, Q, C), bf16), vown=((16, C), bf16), vs1=((J, 16, C), bf16),
        vsum=((16, C), bf16), vs2=((N, 16, C), bf16), vecs=((J, 16, B), f32),
        eall=((N, 1, g.E), f32), wemb=((2 * g.RE, 2 * C), bf16), epart=((N, 1, 2 * C), f32),
        erx=((N, 1, 2 * C), f32), esum=((J, 1, 2 * C), f32), emb=((1, 2 * C), f32),
        A1=((2, P + 2 * g.COLS, 2 * B), bf16), A2=((2, P + 2 * g.COLS, 2 * B), bf16),
        N3=((2, P, 2 * B), bf16), O=((2, P, 2 * B), bf16),
        A1T=((C, P), bf16), A2T=((C, P), bf16), N3T=((C, P), bf16), OT=((C, P), bf16),
        st1=((J, 8, B), f32), xj=((P, B), bf16),
        h1=((P, B), f32), y1=((P, B), f32), dy1=((P, B), f32), tmp=((P, B), f32),
        W1T=((2, 9 * B, 2 * B), bf16), W2T=((2, 9 * B, 2 * B), bf16), WqT=((2, 3 * B, 2 * B), bf16),
        ctx=((B, X), bf16), ctxs=((N, B, X // N), bf16), dcx=((B, 2 * B), bf16), dcxs=((N, B, 2 * B), bf16),
        Kb=((P + B, B), bf16), Vb=((P + B, B), bf16), KT=((B, P + B), bf16), VT=((B, P + B), bf16),
        qs=((P, B), bf16), dK=((P + B, B), f32), dV=((P + B, B), f32), dqkv=((3, P, B), bf16),
        WoF=((2, C, 2 * B), bf16), dopx=((Q, C), bf16), doj=((P, B), bf16), dyj=((P, B), bf16),
        outj=((P, B), bf16), inj=((P, B), bf16),
        S=((3, P + 2 * g.COLS, B), bf16),
        dse=((J, 2, B), f32), dsall=((N, J, 2, B), f32), geb=((2 * g.RE, 2 * C), f32),
        gvec=((16, B), f32), gvs=((N, 16, B), f32), gvi=((J, 16, B), f32), gvt=((16, B), f32),
    )
    half = dict(ps=((2, 2, P, B), bf16), rc=((2, P, B), bf16), sy=((P, B), bf16), ry=((P, B), bf16))
    groups = [plan, half, half, half]
    for wide, rows in g.weights:
        depth = rows * J
        summed = {} if wide == 2 else dict(
            g=((wide, depth * N, B), bf16), rx=((N // 2, wide, depth, B), bf16), zs=((N // 2, wide, depth, B), bf16),
            zr=((N // 2, wide, depth, B), bf16),
        )
        groups.append(dict(
            w=((wide, depth * N, B), bf16), fin=((wide, depth, B), bf16), gr=((J, wide, rows, B), bf16), **summed
        ))
    return groups


def body(g, groups, *refs):
    (x_in, cond, ctx_in, w1, w2, w_emb, w_q, w_c, w_o, vec_in, dy_in) = refs[:11]
    (out, in_grad, gc1, gc2, g_emb, g_q, g_c, g_o, g_v) = refs[11:20]
    left = list(refs[20:-2])
    spaces = [types.SimpleNamespace(**{name: left.pop(0) for name in group}) for group in groups]
    s, dn_bufs, da2_bufs, da1_bufs = spaces[:4]
    c1, c2, wq, wc, wo = spaces[4:]
    for weight, shape, ref in zip(spaces[4:], g.weights, (w1, w2, w_q, w_c, w_o)):
        weight.wide, weight.rows, weight.ref = shape[0], shape[1], ref
        weight.depth = weight.rows * g.J
    rest = (wq, wc, wo)
    P, Q, C, B, N, J, COLS, SIZE = g.P, g.Q, g.C, g.B, g.N, g.J, g.COLS, g.SIZE
    T, E, RE = g.T, g.E, g.RE
    XN, TP = g.X // N, (T + 15) // 16 * 16
    Z = N // 2
    STEPS = P // Q
    wires = Wires(refs[-2], refs[-1])
    send, group = wires.send, wires.group
    d = lax.axis_index("dp")
    j = lax.axis_index("img")
    flat = d * J + j
    z, xx = lax.div(d, 2), lax.rem(d, 2)
    yy, cc = lax.div(j, 2), lax.rem(j, 2)
    sib = (d, yy * 2 + (1 - cc))
    ypeer = (d, (1 - yy) * 2 + cc)
    diag = (d, (1 - yy) * 2 + (1 - cc))
    img_peers = [ypeer, diag, sib]
    dp_peers = [(lax.rem(d + k, N), j) for k in range(1, N)]
    zdev = [lax.rem(z + k, Z) for k in range(Z)]
    zsrc = [lax.rem(z + Z - k, Z) for k in range(Z)]
    xpeer = (z * 2 + (1 - xx), j)

    def lanes(k):
        return pl.ds(pl.multiple_of(k * B, B), B)

    def rows_at(start, size, unit):
        return pl.ds(pl.multiple_of(start, unit), size)

    def px(i):
        return pl.ds(pl.multiple_of(i * Q, Q), Q)

    def each(fn, init=None):
        if init is None:
            lax.fori_loop(0, STEPS, lambda i, carry: (fn(i), carry)[1], 0)
            return None
        return lax.fori_loop(0, STEPS, fn, init)

    def mm(a, b):
        return jnp.dot(a, b, preferred_element_type=f32)

    def mm_t(a, b):
        return lax.dot_general(a, b, (((1,), (1,)), ((), ())), preferred_element_type=f32)

    lane8 = lax.broadcasted_iota(jnp.int32, (8, B), 1)

    def group_sum(row):
        v = jnp.broadcast_to(row, (8, B))
        step = 1
        while step < SIZE:
            down, up = pltpu.roll(v, B - step, 1), pltpu.roll(v, step, 1)
            v = v + jnp.where((lane8 & step) == 0, down, up)
            step *= 2
        return v[0:1]

    def colsum(v):
        while v.shape[0] % 32 == 0:
            half = v.shape[0] // 2
            v = v[:half] + v[half:]
        return jnp.sum(v, axis=0, keepdims=True)

    zero_row = jnp.zeros((1, B), f32)
    count = P * SIZE

    def moments(load):
        total = each(lambda i, a: a + colsum(load(i)), zero_row)
        mean = group_sum(total) * (1.0 / count)
        spread = each(lambda i, a: a + colsum(jnp.square(load(i) - mean)), zero_row)
        return mean, lax.rsqrt(group_sum(spread) * (1.0 / count) + 1e-05)

    def column_of(v):
        return lax.rem(lax.broadcasted_iota(jnp.int32, v.shape, 0), COLS)

    def from_left(v):
        return jnp.where(column_of(v) == 0, 0.0, pltpu.roll(v, 1, 0))

    def from_right(v):
        return jnp.where(column_of(v) == COLS - 1, 0.0, pltpu.roll(v, v.shape[0] - 1, 0))

    BIG = 2 * Q

    def big(i):
        return pl.ds(i * BIG, BIG)

    hot = lax.broadcasted_iota(jnp.int32, (16, C), 1) == (
        lax.broadcasted_iota(jnp.int32, (16, C), 0) + flat * g.VW
    )
    hot = jnp.where(hot, 1.0, 0.0).astype(bf16)
    own_vec = mm(vec_in[...], hot).astype(bf16)
    s.vown[...] = own_vec
    s.vs1[j] = own_vec
    e_own = cond[...].astype(f32)
    e_own = (e_own * jax.nn.sigmoid(e_own)).astype(bf16).astype(f32)
    s.eall[d] = e_own

    barrier = pltpu.get_barrier_semaphore()
    for device in img_peers + dp_peers:
        pl.semaphore_signal(barrier, inc=1, device_id=device, device_id_type=pl.DeviceIdType.MESH)
    pl.semaphore_wait(barrier, len(img_peers) + len(dp_peers))

    def stage_img(W):
        start = d * W.depth + j * W.rows
        W.img = group(
            [
                (W.ref.at[:, rows_at(t * C + device[1] * B, B, B)], W.w.at[t, rows_at(start, W.rows, 16), :], device)
                for device in img_peers
                for t in range(W.wide)
            ],
            W.w.at[:, 0 : (J - 1) * W.rows, :],
        )

    def own_img(W):
        start = d * W.depth + j * W.rows
        for t in range(W.wide):
            W.w[t, rows_at(start, W.rows, 16), :] = W.ref[:, rows_at(t * C + j * B, B, B)]

    def block(W, ref, owner):
        return ref.at[:, rows_at(owner * W.depth, W.depth, 16), :]

    def img_done(W):
        W.img.wait_recv()

    above, below = z < Z - 1, z > 0
    up, down = ((z + 1) * 2 + xx, j), ((z - 1) * 2 + xx, j)

    def piece(W, start, size):
        p = types.SimpleNamespace(W=W, start=start, size=size)
        p.zr, p.xr, p.zs, p.xs = wires.slot(1, Z), wires.slot(1), wires.slot(0), wires.slot(0)
        p.at = lambda owner: W.w.at[:, rows_at(owner * W.depth + start, size, 16), :]
        p.first = lambda count: W.w.at[:, 0 : count * size, :]

        def finish():
            wires.copy(p.xs, p.xr, p.first(Z), p.first(Z), xpeer).wait_send()
            for count, gate in ((Z + 1, above & below), (1, (z == 0) | (z == Z - 1))):
                pl.when(gate)(
                    lambda: wires.copy(p.zs, p.xr, p.first(count), p.first(count), xpeer).wait_send()
                )

        wires.held.append(finish)
        return p

    def move(p, owner, device):
        here = p.at(owner * 2 + xx)
        wires.copy(p.zs, p.zr + owner, here, here, device).start()

    def across(p, owner):
        here = p.at(owner * 2 + xx)
        wires.copy(p.xs, p.xr, here, here, xpeer).start()

    def z_start(pieces):
        for p in pieces:
            pl.when(above)(lambda: move(p, z, up))
            pl.when(below)(lambda: move(p, z, down))
        for p in pieces:
            across(p, z)

    def z_step(pieces, step):
        def take(owner, onward, device):
            for p in pieces:
                here = p.at(owner * 2 + xx)
                wires.copy(p.zs, p.zr + owner, here, here, xpeer).wait_recv()
                if step < Z - 1:
                    pl.when(onward)(lambda: move(p, owner, device))
                across(p, owner)

        pl.when(z >= step)(lambda: take(z - step, above, up))
        pl.when(z + step < Z)(lambda: take(z + step, below, down))

    def arrive(pieces):
        for p in pieces:
            wires.copy(p.xs, p.xr, p.first(Z), p.first(Z), xpeer).wait_recv()

    def halves(W):
        half = W.depth // 32 * 16
        return [piece(W, 0, half), piece(W, half, W.depth - half)]

    p1, p2 = halves(c1), halves(c2)
    pq, pc, po = ([piece(W, 0, W.depth)] for W in rest)

    def gather_start(mine):
        return types.SimpleNamespace(y=send(mine, mine, ypeer), c=send(mine, mine, sib))

    def gather_near(state):
        state.c.wait_recv()

    def gather_far(state, theirs):
        state.y.wait_recv()
        state.f = send(theirs, theirs, sib)

    def gather_end(state):
        state.f.wait_recv()

    stage_img(c1)
    stage_img(wo)
    v_stage1 = group([(s.vown, s.vs1.at[j], device) for device in img_peers], s.vs1.at[0 : J - 1])
    x_own = s.X.at[j]
    x_state = types.SimpleNamespace(y=send(x_in, x_own, ypeer), c=send(x_in, x_own, sib))
    e_stage1 = group([(s.eall.at[d], s.eall.at[d], device) for device in dp_peers], s.eall.at[0 : N - 1])
    own_img(c1)
    s.X[j] = x_in[...]
    for W in (c2, *rest):
        own_img(W)
    for buf in (s.A1, s.A2):
        for h in range(2):
            buf[h, 0:COLS, :] = jnp.zeros((COLS, 2 * B), bf16)
            buf[h, P + COLS : P + 2 * COLS, :] = jnp.zeros((COLS, 2 * B), bf16)
    for c in range(3):
        s.S[c, 0:COLS, :] = jnp.zeros((COLS, B), bf16)
        s.S[c, P + COLS : P + 2 * COLS, :] = jnp.zeros((COLS, B), bf16)
    s.ctx[...] = jnp.zeros((B, g.X), bf16)
    s.ctx[0:T, :] = ctx_in[...]
    if TP < B:
        s.ctxs[:, TP:B, :] = jnp.zeros((N, B - TP, XN), bf16)
        s.dcxs[:, TP:B, :] = jnp.zeros((N, B - TP, 2 * B), bf16)
    img_done(c1)
    z_start(p1[:1])
    z_start(p1[1:])
    img_done(wo)
    z_start(po)
    v_stage1.wait_recv()
    total = s.vs1[0].astype(f32)
    for k in range(1, J):
        total = total + s.vs1[k].astype(f32)
    s.vsum[...] = total.astype(bf16)
    s.vs2[d] = total.astype(bf16)
    v_stage2 = group([(s.vsum, s.vs2.at[d], device) for device in dp_peers], s.vs2.at[0 : N - 1])
    stage_img(c2)

    x_state.y.wait_recv()
    far = s.X.at[(1 - yy) * 2 + cc]
    x_state.f = send(far, far, sib)
    stage_img(wq)
    stage_img(wc)
    dy_copies = group(
        [(dy_in.at[:, lanes(device[1])], s.dyj.at[rows_at(j * Q, Q, Q), :], device) for device in img_peers],
        s.dyj.at[0 : P - Q, :],
    )
    s.dyj[rows_at(j * Q, Q, Q), :] = dy_in[:, lanes(j)]
    z_step(p1[:1], 1)
    z_step(p1[1:] + po, 1)
    img_done(c2)
    z_start(p2[:1])

    e_stage1.wait_recv()
    s.wemb[...] = jnp.zeros((2 * RE, 2 * C), bf16)
    s.wemb[rows_at(lax.rem(flat, 2) * RE, RE, 16), :] = w_emb[...]
    e_at = rows_at(lax.div(flat, 2) * (2 * RE), 2 * RE, B)
    e_rows = jnp.concatenate([s.eall[k, :, e_at] for k in range(N)], axis=0)
    part = mm(e_rows.astype(bf16), s.wemb[...])
    for k in range(N):
        s.epart[k] = part[k : k + 1]
    s.erx[d] = s.epart[d]
    e_stage2 = group([(s.epart.at[device[0]], s.erx.at[d], device) for device in dp_peers], s.erx.at[0 : N - 1])

    x_state.c.wait_recv()
    x_state.f.wait_recv()

    def load_x(k):
        return lambda i: s.X[i, :, k * B : (k + 1) * B].astype(f32)

    def stats(k):
        mean, inverse = moments(load_x(k))
        s.st1[k, 0:1, :] = mean
        s.st1[k, 1:2, :] = inverse

    stats(0)
    stats(1)
    z_step(p1[:1], 2)
    z_step(p1[1:] + po, 2)
    z_start(p2[1:])
    stats(2)
    stats(3)
    e_stage2.wait_recv()
    total = s.erx[0]
    for k in range(1, N):
        total = total + s.erx[k]
    s.esum[j] = total
    e_stage3 = group([(s.esum.at[j], s.esum.at[j], device) for device in img_peers], s.esum.at[0 : J - 1])
    v_stage2.wait_recv()
    total = s.vs2[0].astype(f32)
    for k in range(1, N):
        total = total + s.vs2[k].astype(f32)
    for k in range(J):
        s.vecs[k] = total[:, k * B : (k + 1) * B]

    def vec(row):
        return s.vecs[j, row : row + 1, :]

    z_step(p1[:1], 3)
    z_step(p1[1:] + po, 3)
    img_done(wq)
    z_start(pq)
    for k in range(J):
        mean, inverse = s.st1[k, 0:1, :], s.st1[k, 1:2, :]
        gain, bias = s.vecs[k, 0:1, :], s.vecs[k, 1:2, :]
        load = load_x(k)

        def act(i):
            t1 = (load(i) - mean) * inverse * gain + bias
            a1 = t1 * jax.nn.sigmoid(t1)
            s.A1[k // 2, rows_at(i * Q + COLS, Q, COLS), (k % 2) * B : (k % 2 + 1) * B] = a1.astype(bf16)

        each(act)

    def turn(source, target, offset):
        def one(i):
            for h in range(2):
                v = source[h, rows_at(i * Q + offset, Q, 16), :]
                target[h * 2 * B : (h + 1) * 2 * B, px(i)] = v.T
        each(one)

    each(lambda i: s.xj.__setitem__((px(i), slice(None)), s.X[i, :, lanes(j)]))
    z_step(p2[:1], 1)
    z_step(p2[1:], 1)
    img_done(wc)
    z_start(pc)
    e_stage3.wait_recv()
    total = s.esum[0]
    for k in range(1, J):
        total = total + s.esum[k]
    s.emb[...] = total
    scale = 1.0 + (s.emb[:, lanes(j)] + vec(14))
    shift = s.emb[:, lanes(j + J)] + vec(15)
    arrive(po)
    wo_at = s.WoF.at[yy, :, lanes(cc)]
    s.WoF[yy, :, lanes(cc)] = wo.w[0]
    wo_state = gather_start(wo_at)
    arrive(p1)

    def convolve(A, W, emit):
        right = jnp.concatenate(
            [
                jnp.concatenate([W[0, (3 * r + c) * C : (3 * r + c + 1) * C, :] for r in range(3)], axis=0)
                for c in range(3)
            ],
            axis=1,
        )
        for i in range(P // BIG):
            left = jnp.concatenate(
                [A[h, i * BIG + r * COLS : (i + 1) * BIG + r * COLS, :] for r in range(3) for h in range(2)], axis=1
            )
            p = mm(left, right)
            emit(big(i), p[:, B : 2 * B] + from_left(p[:, :B]) + from_right(p[:, 2 * B :]))

    def save_h1(at, v):
        s.h1[at, :] = v + vec(2)

    convolve(s.A1, c1.w, save_h1)
    mean2, inv2 = moments(lambda i: s.h1[px(i), :])
    gather_far(wo_state, s.WoF.at[1 - yy, :, lanes(cc)])
    gather_near(wo_state)
    gather_end(wo_state)

    def xh2(i):
        return (s.h1[px(i), :] - mean2) * inv2

    def u_of(i):
        return (xh2(i) * vec(3) + vec(4)) * scale + shift

    def act2(i):
        u = u_of(i)
        s.A2[yy, rows_at(i * Q + COLS, Q, COLS), lanes(cc)] = (u * jax.nn.sigmoid(u)).astype(bf16)

    def halves_out(act, place):
        states = []
        for i in range(P // BIG):
            lax.fori_loop(i * BIG // Q, (i + 1) * BIG // Q, lambda n, carry: (act(n), carry)[1], 0)
            states.append(gather_start(place(i, yy)))
        return states

    def halves_in(states, place):
        for i, state in enumerate(states):
            gather_far(state, place(i, 1 - yy))

    def halves_end(states):
        for state in states:
            gather_near(state)
            gather_end(state)

    def a2_at(i, half):
        return s.A2.at[half, pl.ds(COLS + i * BIG, BIG), lanes(cc)]

    a2_state = halves_out(act2, a2_at)
    for h in range(2):
        part = mm_t(dy_in[:, 0 : 2 * B], s.WoF[0, h * 2 * B : (h + 1) * 2 * B, :])
        part = part + mm_t(dy_in[:, 2 * B : 4 * B], s.WoF[1, h * 2 * B : (h + 1) * 2 * B, :])
        s.dopx[:, h * 2 * B : (h + 1) * 2 * B] = part.astype(bf16)
    do_copies = group(
        [(s.dopx.at[:, lanes(device[1])], s.doj.at[rows_at(j * Q, Q, Q), :], device) for device in img_peers],
        s.doj.at[0 : P - Q, :],
    )
    s.doj[rows_at(j * Q, Q, Q), :] = s.dopx[:, lanes(j)]
    z_step(p2[:1], 2)
    z_step(p2[1:], 2)
    z_step(pq, 1)
    z_step(p2[:1], 3)
    z_step(p2[1:], 3)
    z_step(pc, 1)
    z_step(pq, 2)
    halves_in(a2_state, a2_at)
    turn(s.A1, s.A1T, COLS)
    halves_end(a2_state)
    z_step(pc, 2)
    z_step(pq, 3)
    arrive(p2)

    def save_y1(at, v):
        s.y1[at, :] = s.xj[at, :].astype(f32) + v + vec(5)

    convolve(s.A2, c2.w, save_y1)
    mean3, inv3 = moments(lambda i: s.y1[px(i), :])

    def xh3(i):
        return (s.y1[px(i), :] - mean3) * inv3

    def act3(i):
        s.N3[yy, px(i), lanes(cc)] = (xh3(i) * vec(6) + vec(7)).astype(bf16)

    def n_at(i, half):
        return s.N3.at[half, big(i), lanes(cc)]

    n_state = halves_out(act3, n_at)
    turn(s.A2, s.A2T, COLS)

    def turn_weights(W, target, taps, stride):
        for h in range(2):
            for t in range(taps):
                v = W(t)[rows_at(h * 2 * B, 2 * B, 16), :]
                target[h, t * B : (t + 1) * B, :] = v.T

    def conv_tap(W):
        return lambda t: W.w.at[0, pl.ds(t * C, C), :]

    turn_weights(conv_tap(c2), s.W2T, 9, C)
    z_step(pc, 3)
    halves_in(n_state, n_at)
    turn_weights(conv_tap(c1), s.W1T, 9, C)
    arrive(pq)
    arrive(pc)
    turn_weights(lambda t: wq.w.at[t], s.WqT, 3, C)
    tokens = lax.broadcasted_iota(jnp.int32, (B, B), 0) < T
    for t, target in enumerate((s.Kb, s.Vb)):
        v = mm(s.ctx[...], wc.w[t]) + vec(12 + t)
        target[P : P + B, :] = jnp.where(tokens, v, 0.0).astype(bf16)
    halves_end(n_state)

    def tokens_of(owner):
        return s.ctx.at[0:TP, rows_at(owner * XN, XN, B)]

    ctx_copies = group(
        [(tokens_of(device[0]), s.ctxs.at[d, 0:TP, :], device) for device in dp_peers],
        s.ctxs.at[0 : N - 1, 0:TP, :],
    )
    s.ctxs[d, 0:TP, :] = tokens_of(d)[...]

    def project(at):
        left = jnp.concatenate([s.N3[0, at, :], s.N3[1, at, :]], axis=1)
        right = jnp.concatenate([wq.w[t] for t in range(3)], axis=1)
        v = mm(left, right)
        q = (v[:, :B] + vec(9)).astype(bf16)
        s.qs[at, :] = (q.astype(f32) * g.FACTOR).astype(bf16)
        s.Kb[at, :] = (v[:, B : 2 * B] + vec(10)).astype(bf16)
        s.Vb[at, :] = (v[:, 2 * B :] + vec(11)).astype(bf16)

    for i in range(P // BIG):
        project(big(i))
    for source, target in ((s.Kb, s.KT), (s.Vb, s.VT)):
        for k in range(0, P + B, B):
            target[:, k : k + B] = source[k : k + B, :].T
    do_copies.wait_recv()
    dy_copies.wait_recv()
    s.dK[...] = jnp.zeros((P + B, B), f32)
    s.dV[...] = jnp.zeros((P + B, B), f32)

    HEAD_ = g.HEAD
    lane_row = lax.broadcasted_iota(jnp.int32, (1, B), 1)
    span = 2 * Q
    known = lax.broadcasted_iota(jnp.int32, (B, span), 0) < T
    keeps = [jnp.where(lax.div(lane_row, HEAD_) == h, 1.0, 0.0).astype(bf16) for h in range(B // HEAD_)]

    def attend(i):
        at = pl.ds(i * span, span)
        q_i, do_i = s.qs[at, :], s.doj[at, :]
        q_m = jnp.concatenate([q_i * keep for keep in keeps], axis=0)
        do_m = jnp.concatenate([do_i * keep for keep in keeps], axis=0)
        all_scores, all_dp = mm_t(s.Kb[...], q_m), mm_t(s.Vb[...], do_m)
        low, slope, mixed, back = [], [], [], []
        for h in range(B // HEAD_):
            scores = all_scores[:, h * span : (h + 1) * span]
            scores = jnp.concatenate([scores[:P], jnp.where(known, scores[P:], -1e30)], axis=0)
            e = jnp.exp(scores - jnp.max(scores, axis=0, keepdims=True))
            probs = e * (1.0 / jnp.sum(e, axis=0, keepdims=True))
            pb = probs.astype(bf16)
            mixed.append(mm(s.VT[h * HEAD_ : (h + 1) * HEAD_, :], pb))
            dp = all_dp[:, h * span : (h + 1) * span]
            ds = (probs * (dp - jnp.sum(dp * probs, axis=0, keepdims=True))).astype(bf16)
            back.append(mm(s.KT[h * HEAD_ : (h + 1) * HEAD_, :], ds))
            low.append(pb)
            slope.append(ds)
        s.dV[...] += mm(jnp.concatenate(low, axis=1), do_m)
        s.dK[...] += mm(jnp.concatenate(slope, axis=1), q_m)
        s.O[yy, at, lanes(cc)] = jnp.concatenate(mixed, axis=0).T.astype(bf16)
        s.dqkv[0, at, :] = (jnp.concatenate(back, axis=0).T * g.FACTOR).astype(bf16)
        return gather_start(s.O.at[yy, at, lanes(cc)])

    o_states = [attend(i) for i in range(P // span)]

    def grads_kv(i):
        s.dqkv[1, px(i), :] = s.dK[px(i), :].astype(bf16)
        s.dqkv[2, px(i), :] = s.dV[px(i), :].astype(bf16)

    each(grads_kv)

    def scatter(bufs, left, right):
        ps, rc, sy, ry = bufs.ps, bufs.rc, bufs.sy, bufs.ry
        near, y_in = [], []
        part = BIG // Q

        def halves_of(slot, half):
            other = 1 - yy if slot == 0 else yy

            at = big(half)
            v = mm(left(half * BIG, BIG), right[other]).astype(bf16)
            ps[slot, 0, at, :] = v[:, :B]
            ps[slot, 1, at, :] = v[:, B:]
            return send(ps.at[slot, 1 - cc, at, :], rc.at[slot, at, :], sib)

        far = [halves_of(0, half) for half in range(P // BIG)]
        for half in range(P // BIG):
            near.append(halves_of(1, half))
            far[half].wait_recv()

            def add(n, carry):
                i = n + half * part
                v = ps[0, cc, px(i), :].astype(f32) + rc[0, px(i), :].astype(f32)
                sy[px(i), :] = v.astype(bf16)
                return carry

            lax.fori_loop(0, part, add, 0)
            at = big(half)
            y_in.append(send(sy.at[at, :], ry.at[at, :], ypeer))

        def done():
            for copy in near + y_in:
                copy.wait_recv()

        def load(i):
            v = ps[1, cc, px(i), :].astype(f32) + rc[1, px(i), :].astype(f32)
            return v + ry[px(i), :].astype(f32)

        return done, load

    order = sorted(range(1, Z), key=lambda k: -min(k, Z - k)) + [0]

    def sum_start(W):
        W.sx, W.zout, W.zin = {}, wires.slot(0), wires.slot(1)
        out = wires.slot(0)
        for k in order:
            W.sx[k] = send(block(W, W.g, zdev[k] * 2 + (1 - xx)), W.rx.at[k], xpeer, out)
        wires.held.append(wires.copy(out, W.zin, W.rx, W.rx, xpeer).wait_send)

    def sum_block(W, k):
        W.sx[k].wait_recv()
        at = rows_at((zdev[k] * 2 + xx) * W.depth, W.depth, 16)
        v = W.g[:, at, :].astype(f32) + W.rx[k].astype(f32)
        W.zs[k] = v.astype(bf16)
        if k:
            wires.copy(W.zout, W.zin, W.zs.at[k], W.zr.at[k], (zdev[k] * 2 + xx, j)).start()

    def sum_z(W):
        for k in order:
            sum_block(W, k)

    def sum_img(W):
        total = wires.copy(W.zout, W.zin, W.zr.at[0 : Z - 1], W.zr.at[0 : Z - 1], xpeer)
        total.wait_recv()
        wires.held.append(total.wait_send)
        v = W.zs[0].astype(f32)
        for k in range(1, Z):
            v = v + W.zr[k].astype(f32)
        to_rows(W, jnp.concatenate([v[t] for t in range(W.wide)], axis=1))

    def to_rows(W, v):
        for t in range(W.wide):
            W.fin[t] = v[:, t * B : (t + 1) * B].astype(bf16)
        W.simg = group(
            [
                (W.fin.at[:, rows_at(device[1] * W.rows, W.rows, 16), :], W.gr.at[j], device)
                for device in img_peers
            ],
            W.gr.at[0 : J - 1],
        )
        W.gr[j] = W.fin[:, rows_at(j * W.rows, W.rows, 16), :]

    def sum_end(W, target):
        W.simg.wait_recv()
        for k in range(J):
            for t in range(W.wide):
                target[:, t * C + k * B : t * C + (k + 1) * B] = W.gr[k, t].astype(f32)

    dn_done, dn_at = scatter(
        dn_bufs, lambda at, size: jnp.concatenate([s.dqkv[t, pl.ds(at, size), :] for t in range(3)], axis=1), s.WqT
    )
    turn(s.N3, s.N3T, 0)
    for h in range(2):
        at = slice(h * 2 * B, (h + 1) * 2 * B)
        v = mm(s.N3T[at, :], jnp.concatenate([s.dqkv[t] for t in range(3)], axis=1)).astype(bf16)
        for t in range(3):
            wq.g[t, at, :] = v[:, t * B : (t + 1) * B]
    sum_start(wq)
    s.dcx[...] = jnp.concatenate([s.dK[P : P + B, :], s.dV[P : P + B, :]], axis=1).astype(bf16)
    s.dcxs[d] = s.dcx[...]
    dcx_copies = group(
        [(s.dcx.at[0:TP, :], s.dcxs.at[d, 0:TP, :], device) for device in dp_peers],
        s.dcxs.at[0 : N - 1, 0:TP, :],
    )
    for i, state in enumerate(o_states):
        gather_far(state, s.O.at[1 - yy, pl.ds(i * span, span), lanes(cc)])
    for state in o_states:
        gather_near(state)
        gather_end(state)

    def finish(at):
        left = jnp.concatenate([s.O[0, at, :], s.O[1, at, :]], axis=1)
        s.outj[at, :] = (s.y1[at, :] + mm(left, wo.w[0]) + vec(8)).astype(bf16)

    for i in range(P // BIG):
        finish(big(i))

    def to_pixels(source, target):
        copies = group(
            [(source.at[rows_at(device[1] * Q, Q, Q), :], target.at[:, lanes(j)], device) for device in img_peers],
            source.at[0 : P - Q, :],
        )
        target[:, lanes(j)] = source[rows_at(j * Q, Q, Q), :]
        return copies

    out_copies = to_pixels(s.outj, out)
    turn(s.O, s.OT, 0)
    for h in range(2):
        at = slice(h * 2 * B, (h + 1) * 2 * B)
        wo.g[0, at, :] = mm(s.OT[at, :], s.dyj[...]).astype(bf16)
    sum_start(wo)

    def back_sums(grad, normed, factor):
        def one(i, carry):
            v = grad(i)
            return carry[0] + colsum(v), carry[1] + colsum(v * normed(i))
        first, second = each(one, (zero_row, zero_row))
        return first, second, group_sum(first * factor) * (1.0 / count), group_sum(second * factor) * (1.0 / count)

    dn_done()
    sum_z(wq)
    dn_sum, dn_hat, m1, m2 = back_sums(dn_at, xh3, vec(6))

    def shifted(i, v):
        at = rows_at(i * Q + COLS, Q, COLS)
        s.S[0, at, :] = from_right(v).astype(bf16)
        s.S[1, at, :] = v.astype(bf16)
        s.S[2, at, :] = from_left(v).astype(bf16)

    def make_dh2(i, carry):
        dy = s.dyj[px(i), :].astype(f32)
        v = dy + (dn_at(i) * vec(6) - m1 - xh3(i) * m2) * inv3
        s.dy1[px(i), :] = v
        low = v.astype(bf16).astype(f32)
        shifted(i, low)
        return carry[0] + colsum(low), carry[1] + colsum(dy)

    dh2_sum, dy_sum = each(make_dh2, (zero_row, zero_row))

    def tap(t, start, size):
        r, c = t // 3, t % 3
        return s.S[c, rows_at(start + (2 - r) * COLS, size, COLS), :]

    def field(at, size):
        return jnp.concatenate([tap(t, at, size) for t in range(9)], axis=1)

    def kernel_grad(W, turned):
        for h in range(2):
            at = slice(h * 2 * B, (h + 1) * 2 * B)
            v = mm(turned[at, :], jnp.concatenate([tap(t, 0, P) for t in range(9)], axis=1)).astype(bf16)
            for t in range(9):
                W.g[0, t * C + h * 2 * B : t * C + (h + 1) * 2 * B, :] = v[:, t * B : (t + 1) * B]

    da2_done, da2_at = scatter(da2_bufs, field, s.W2T)
    kernel_grad(c2, s.A2T)
    sum_start(c2)
    sum_z(wo)
    ctx_copies.wait_recv()
    dcx_copies.wait_recv()
    v = lax.dot_general(
        s.ctxs[...].reshape(N * B, XN), s.dcxs[...].reshape(N * B, 2 * B), (((0,), (0,)), ((), ())),
        preferred_element_type=f32,
    )
    to_rows(wc, v)
    da2_done()

    def slope_of(v):
        sigma = jax.nn.sigmoid(v)
        return sigma * (1.0 + v * (1.0 - sigma))

    def make_du(i, carry):
        du = da2_at(i) * slope_of(u_of(i))
        s.tmp[px(i), :] = du
        return carry[0] + colsum(du), carry[1] + colsum(du * xh2(i))

    du_sum, du_hat = each(make_du, (zero_row, zero_row))
    gain2 = scale * vec(3)
    m1b = group_sum(du_sum * gain2) * (1.0 / count)
    m2b = group_sum(du_hat * gain2) * (1.0 / count)

    def make_dh1(i, carry):
        v = (s.tmp[px(i), :] * gain2 - m1b - xh2(i) * m2b) * inv2
        low = v.astype(bf16).astype(f32)
        shifted(i, low)
        return carry + colsum(low)

    dh1_sum = each(make_dh1, zero_row)
    dscale = vec(3) * du_hat + vec(4) * du_sum
    kernel_grad(c1, s.A1T)
    sum_start(c1)
    da1_done, da1_at = scatter(da1_bufs, field, s.W1T)
    s.dse[j] = jnp.concatenate([dscale, du_sum], axis=0)
    ds_copies = group([(s.dse.at[j], s.dse.at[j], device) for device in img_peers], s.dse.at[0 : J - 1])
    sum_img(wq)
    sum_img(wo)
    sum_z(c2)
    ds_copies.wait_recv()
    s.dsall[d] = s.dse[...]
    ds_copies = group([(s.dse, s.dsall.at[d], device) for device in dp_peers], s.dsall.at[0 : N - 1])
    sum_block(c1, order[0])
    da1_done()
    mean1, inv1 = s.st1[j, 0:1, :], s.st1[j, 1:2, :]

    def xh1(i):
        return (s.xj[px(i), :].astype(f32) - mean1) * inv1

    def make_dt1(i, carry):
        n1 = xh1(i)
        dt1 = da1_at(i) * slope_of(n1 * vec(0) + vec(1))
        s.tmp[px(i), :] = dt1
        return carry[0] + colsum(dt1), carry[1] + colsum(dt1 * n1)

    dt1_sum, dt1_hat = each(make_dt1, (zero_row, zero_row))
    sum_block(c1, order[1])
    m1c = group_sum(dt1_sum * vec(0)) * (1.0 / count)
    m2c = group_sum(dt1_hat * vec(0)) * (1.0 / count)

    def make_in(i):
        v = s.dy1[px(i), :] + (s.tmp[px(i), :] * vec(0) - m1c - xh1(i) * m2c) * inv1
        s.inj[px(i), :] = v.astype(bf16)

    each(make_in)
    in_copies = to_pixels(s.inj, in_grad)

    qkv_sums = [each(lambda i, a, t=t: a + colsum(s.dqkv[t, px(i), :].astype(f32)), zero_row) for t in range(3)]
    s.gvec[...] = jnp.concatenate(
        [dt1_hat, dt1_sum, dh1_sum, scale * du_hat, scale * du_sum, dh2_sum, dn_hat, dn_sum, dy_sum]
        + qkv_sums
        + [colsum(s.dK[P : P + B, :]), colsum(s.dV[P : P + B, :]), dscale, du_sum],
        axis=0,
    )
    gv_copies = group([(s.gvec, s.gvs.at[d], device) for device in dp_peers], s.gvs.at[0 : N - 1])
    s.gvs[d] = s.gvec[...]
    for k in order[2:]:
        sum_block(c1, k)
    gv_copies.wait_recv()
    total = s.gvs[0]
    for k in range(1, N):
        total = total + s.gvs[k]
    s.gvt[...] = total
    s.gvi[j] = total
    gv_copies = group([(s.gvt, s.gvi.at[j], device) for device in img_peers], s.gvi.at[0 : J - 1])
    sum_img(c2)
    sum_end(wq, g_q)
    sum_end(wc, g_c)
    sum_end(wo, g_o)
    ds_copies.wait_recv()
    e_cols = jnp.concatenate([s.eall[k, :, e_at] for k in range(N)], axis=0)
    for t in range(2):
        for k in range(J):
            rows = jnp.concatenate([s.dsall[i, k, t : t + 1, :] for i in range(N)], axis=0)
            v = lax.dot_general(
                e_cols, rows, (((0,), (0,)), ((), ())), precision=highest, preferred_element_type=f32
            )
            s.geb[:, t * C + k * B : t * C + (k + 1) * B] = v
    g_emb[...] = s.geb[rows_at(lax.rem(flat, 2) * RE, RE, 8), :]
    gv_copies.wait_recv()
    VW = g.VW
    each_block = B // VW
    pick = lax.broadcasted_iota(jnp.int32, (B, VW), 0) == (
        lax.broadcasted_iota(jnp.int32, (B, VW), 1) + lax.rem(flat, each_block) * VW
    )
    g_v[...] = jnp.dot(
        s.gvi[lax.div(flat, each_block)], jnp.where(pick, 1.0, 0.0), precision=highest,
        preferred_element_type=f32,
    )
    sum_end(c2, gc2)
    sum_img(c1)
    sum_end(c1, gc1)
    out_copies.wait_recv()
    in_copies.wait_recv()
    wires.drain()
    assert wires.used[0] <= g.copies[0] and wires.used[1] <= g.copies[1], wires.used


def hand_over(*refs):
    count = len(refs) // 2
    for k in range(count):
        refs[count + k][...] = refs[k][...].astype(refs[count + k].dtype)


def fused(
    image, cond, context, w_conv1, w_conv2, w_embed, w_qkv, w_context, w_out, vectors, cotangent
):
    J, N = lax.axis_size("img"), lax.axis_size("dp")
    local, cols, chans = image.shape[1:]
    g = types.SimpleNamespace(
        P=local * cols * J, Q=local * cols, C=chans, B=chans // J, N=N, J=J, COLS=cols, SIZE=chans // GROUPS,
        T=context.shape[1], X=context.shape[2], E=cond.shape[1], RE=w_embed.shape[0], VW=vectors.shape[1],
        HEAD=HEAD, FACTOR=HEAD ** (-0.5),
        weights=[
            (1, w_conv1.shape[0]), (1, w_conv2.shape[0]), (3, w_qkv.shape[0]), (2, w_context.shape[0]),
            (1, w_out.shape[0]),
        ],
    )
    groups = scratch_plan(g)
    rows = local * cols
    shape = jax.ShapeDtypeStruct
    outs = [
        shape((rows, chans), bf16), shape((rows, chans), bf16), shape(w_conv1.shape, f32), shape(w_conv2.shape, f32),
        shape(w_embed.shape, f32), shape(w_qkv.shape, f32), shape(w_context.shape, f32), shape(w_out.shape, f32),
        shape(vectors.shape, f32),
    ]
    g.copies = (89, 67 + 11 * (N // 2 + 1))
    vmem = pl.BlockSpec(memory_space=pltpu.VMEM)
    result = pl.pallas_call(
        functools.partial(body, g, groups),
        out_shape=outs,
        in_specs=[vmem] * 11,
        out_specs=[vmem] * 9,
        scratch_shapes=[pltpu.VMEM(*spec) for group in groups for spec in group.values()]
        + [pltpu.SemaphoreType.DMA((count,)) for count in g.copies],
        compiler_params=pltpu.CompilerParams(
            collective_id=0, has_side_effects=True, vmem_limit_bytes=60 * 1024 * 1024
        ),
    )(
        image.reshape(rows, chans), cond, context[0], w_conv1, w_conv2, w_embed, w_qkv, w_context, w_out, vectors,
        cotangent.reshape(rows, chans),
    )
    count = len(outs)
    result = pl.pallas_call(
        hand_over, out_shape=outs, in_specs=[vmem] * count, out_specs=[vmem] * count,
    )(*result)
    return (result[0].reshape(image.shape), result[1].reshape(image.shape), *result[2:])


def on_device(
    image, cond, context, w_conv1, w_conv2, w_embed, w_qkv, w_context, w_out, vectors, cotangent
):
    parts = lax.axis_size("img")
    place = lax.axis_index("img")
    images = lax.axis_size("dp")
    rows, cols, chans = image.shape[1] * parts, image.shape[2], image.shape[3]
    pixels = rows * cols
    width = chans // parts
    size = chans // GROUPS
    count = images * parts

    if parts == 4 and width == 128 and images % 2 == 0 and all(
        w.shape[0] % 16 == 0 for w in (w_conv1, w_conv2, w_embed, w_qkv, w_context, w_out)
    ):
        return fused(
            image, cond, context, w_conv1, w_conv2, w_embed, w_qkv, w_context, w_out, vectors, cotangent
        )

    def own(full):
        return lax.dynamic_slice_in_dim(full, place * width, width, full.ndim - 1)

    shards = (w_conv1, w_conv2, w_qkv, w_context, w_embed, w_out)
    lengths = [w.shape[0] * (w.shape[1] // chans) for w in shards]
    packed = jnp.concatenate([columns(w, parts) for w in shards], 1)
    packed = lax.all_to_all(packed, "img", 0, 0, tiled=True)
    packed = lax.all_gather(packed, "dp", axis=0, tiled=True)
    full = []
    start = 0
    for w, length in zip(shards, lengths):
        wide = w.shape[1] // chans
        piece = packed[:, start : start + length].reshape(count, wide, w.shape[0], width)
        full.append(piece.transpose(0, 2, 1, 3).reshape(count * w.shape[0], wide * width))
        start += length
    k1, k2, kq, kc, ke, ko = full
    vec_all = lax.all_gather(vectors, ("dp", "img"), axis=1, tiled=True).astype(f32)
    vec = own(vec_all)

    x_low = lax.all_gather(image[0].reshape(-1, chans), "img", axis=0, tiled=True)
    x_all = x_low.astype(f32)
    normed1_all, inverse1_all = group_norm(x_all, size)
    act1 = jax.nn.silu(normed1_all * vec_all[0] + vec_all[1]).astype(bf16)
    normed1 = own(normed1_all)
    inverse1 = lax.dynamic_slice_in_dim(inverse1_all, place * (GROUPS // parts), GROUPS // parts, 1)
    pre1 = normed1 * vec[0] + vec[1]
    hidden1 = dot(taps_of(act1, rows, cols, False), k1) + vec[2]
    cond_act = jax.nn.silu(cond.astype(f32)).astype(bf16)
    embed = dot(cond_act, ke)[0]
    scale = embed[:width] + vec[14]
    shift = embed[width:] + vec[15]
    normed2, inverse2 = group_norm(hidden1, size)
    affine2 = normed2 * vec[3] + vec[4]
    pre2 = affine2 * (1.0 + scale) + shift
    act2_own = jax.nn.silu(pre2).astype(bf16)
    act2 = lax.all_gather(act2_own, "img", axis=1, tiled=True)
    resid = own(x_all) + dot(taps_of(act2, rows, cols, False), k2) + vec[5]
    normed3, inverse3 = group_norm(resid, size)
    affine3_own = (normed3 * vec[6] + vec[7]).astype(bf16)
    affine3 = lax.all_gather(affine3_own, "img", axis=1, tiled=True)
    qkv = (dot(affine3, kq) + jnp.concatenate([vec[9], vec[10], vec[11]])).astype(bf16)
    ctx = (dot(context[0], kc) + jnp.concatenate([vec[12], vec[13]])).astype(bf16)
    tokens = ctx.shape[0]

    out_full = lax.all_gather(ko, "img", axis=1, tiled=True)
    dy_px = cotangent[0].reshape(-1, chans)
    do_px = lax.dot_general(dy_px, out_full, (((1,), (1,)), ((), ())), preferred_element_type=f32).astype(bf16)
    both = jnp.stack([do_px, dy_px])
    both = lax.all_to_all(both, "img", 2, 1, tiled=True)
    do, dy = both[0], both[1]
    dy_wide = dy.astype(f32)

    keys = jnp.concatenate([ctx[:, :width], qkv[:, width : 2 * width]], 0)
    values = jnp.concatenate([ctx[:, width:], qkv[:, 2 * width :]], 0)
    factor = HEAD ** (-0.5)
    mixed, dq, dk, dv = [], [], [], []
    for h in range(width // HEAD):
        at = slice(h * HEAD, (h + 1) * HEAD)
        q_h, k_h, v_h, do_h = qkv[:, at], keys[:, at], values[:, at], do[:, at]
        scores = dot(k_h, q_h.T) * factor
        top = jnp.max(scores, 0, keepdims=True)
        weights = jnp.exp(scores - top)
        probs = weights / jnp.sum(weights, 0, keepdims=True)
        low = probs.astype(bf16)
        mixed.append(dot(v_h.T, low).T)
        dv.append(dot(low, do_h))
        dp = dot(v_h, do_h.T)
        ds = (probs * (dp - jnp.sum(dp * probs, 0, keepdims=True))).astype(bf16)
        dq.append(dot(k_h.T, ds).T * factor)
        dk.append(dot(ds, q_h) * factor)
    mixed = jnp.concatenate(mixed, 1).astype(bf16)
    dq, dk, dv = (jnp.concatenate(v, 1) for v in (dq, dk, dv))
    mixed_all = lax.all_gather(mixed, "img", axis=1, tiled=True)
    output = (resid + dot(mixed_all, ko) + vec[8]).astype(bf16)

    dqkv = jnp.concatenate([dq, dk[tokens:], dv[tokens:]], 1).astype(bf16)
    dctx = jnp.concatenate([dk[:tokens], dv[:tokens]], 1)
    dn_part = lax.dot_general(dqkv, kq, (((1,), (1,)), ((), ())), preferred_element_type=f32)
    dn = lax.psum_scatter(dn_part.astype(bf16), "img", scatter_dimension=1, tiled=True).astype(f32)
    dy1 = dy_wide + group_back(dn * vec[6], normed3, inverse3, size)
    dh2 = dy1.astype(bf16)

    def turned(kernel):
        return kernel.reshape(9, chans, width).transpose(0, 2, 1).reshape(9 * width, chans)

    def conv_back(dh, kernel, act):
        field = taps_of(dh, rows, cols, True)
        part = dot(field, turned(kernel)).astype(bf16)
        grad = lax.psum_scatter(part, "img", scatter_dimension=1, tiled=True).astype(f32)
        kernel_grad = lax.dot_general(act, field, (((0,), (0,)), ((), ())), preferred_element_type=f32)
        return grad, kernel_grad.reshape(chans, 9, width).transpose(1, 0, 2).reshape(9 * chans, width)

    da2, gk2 = conv_back(dh2, k2, act2)
    du = da2 * silu_slope(pre2)
    dscale = jnp.sum(du * affine2, 0)
    dshift = jnp.sum(du, 0)
    dz = du * (1.0 + scale)
    dh1 = group_back(dz * vec[3], normed2, inverse2, size).astype(bf16)
    da1, gk1 = conv_back(dh1, k1, act1)
    dt1 = da1 * silu_slope(pre1)
    in_grad = (dy1 + group_back(dt1 * vec[0], normed1, inverse1, size)).astype(bf16)

    tops = lax.all_to_all(jnp.stack([output, in_grad]), "img", 1, 2, tiled=True)
    gkq = lax.dot_general(affine3, dqkv, (((0,), (0,)), ((), ())), preferred_element_type=f32)
    gkc = lax.dot_general(context[0], dctx.astype(bf16), (((0,), (0,)), ((), ())), preferred_element_type=f32)
    gko = lax.dot_general(mixed_all, dy, (((0,), (0,)), ((), ())), preferred_element_type=f32)
    gke = cond_act[0].astype(f32)[:, None] * jnp.concatenate([dscale, dshift])[None, :]
    grad_vec = jnp.stack(
        [
            jnp.sum(dt1 * normed1, 0),
            jnp.sum(dt1, 0),
            jnp.sum(dh1.astype(f32), 0),
            jnp.sum(dz * normed2, 0),
            jnp.sum(dz, 0),
            jnp.sum(dh2.astype(f32), 0),
            jnp.sum(dn * normed3, 0),
            jnp.sum(dn, 0),
            jnp.sum(dy_wide, 0),
        ]
        + [jnp.sum(v.astype(f32), 0) for v in jnp.split(dqkv, 3, 1)]
        + [jnp.sum(v, 0) for v in jnp.split(dctx, 2, 1)]
        + [dscale, dshift],
        0,
    )
    grads = (gk1, gk2, gkq, gkc, gke, gko)
    pieces = []
    for w, g in zip(shards, grads):
        wide = w.shape[1] // chans
        piece = g.reshape(count, w.shape[0], wide, width).transpose(0, 2, 1, 3)
        pieces.append(piece.reshape(count, wide * w.shape[0], width))
    packed = jnp.concatenate(pieces, 1).astype(bf16)
    packed = lax.psum_scatter(packed, "dp", scatter_dimension=0, tiled=True).astype(f32)
    packed = lax.all_to_all(packed.astype(bf16), "img", 0, 0, tiled=True).astype(f32)
    outs = []
    start = 0
    for w, length in zip(shards, lengths):
        wide = w.shape[1] // chans
        piece = packed[:, start : start + length].reshape(parts, wide, w.shape[0], width)
        outs.append(piece.transpose(2, 1, 0, 3).reshape(w.shape))
        start += length
    vec_sum = lax.all_gather(lax.psum(grad_vec, "dp"), "img", axis=1, tiled=True)
    each = chans // count
    g_vec = lax.dynamic_slice_in_dim(
        vec_sum, (lax.axis_index("dp") * parts + place) * each, each, 1
    )
    g1, g2, gq, gc, ge, go = outs
    return (tops[0].reshape(image.shape), tops[1].reshape(image.shape), g1, g2, ge, gq, gc, go, g_vec)


def solution(mesh):
    whole = P(("dp", "img"), None)
    field = P("dp", "img", None, None)
    in_specs = (
        field, P("dp", None), P("dp", None, None), whole, whole, whole, whole, whole, whole,
        P(None, ("dp", "img")), field,
    )
    out_specs = (field, field, whole, whole, whole, whole, whole, whole, P(None, ("dp", "img")))
    return jax.shard_map(
        on_device, mesh=mesh, in_specs=in_specs, out_specs=out_specs, check_vma=False
    )
```

```python
import functools
import types

import jax
import jax.numpy as jnp
from jax import lax
from jax.experimental import pallas as pl
from jax.experimental.pallas import tpu as pltpu
from jax.sharding import PartitionSpec as P

HEADS = 8
HEAD = 64
GROUPS = 32

f32 = jnp.float32
bf16 = jnp.bfloat16
highest = lax.Precision.HIGHEST


def dot(a, b):
    return jnp.dot(a, b, preferred_element_type=f32)


def silu_slope(value):
    sigma = jax.nn.sigmoid(value)
    return sigma * (1.0 + value * (1.0 - sigma))


def group_norm(flat, size):
    pixels, chans = flat.shape
    part = flat.reshape(pixels, chans // size, size)
    mean = jnp.mean(part, axis=(0, 2), keepdims=True)
    spread = jnp.mean(jnp.square(part - mean), axis=(0, 2), keepdims=True)
    inverse = lax.rsqrt(spread + 1e-05)
    return ((part - mean) * inverse).reshape(pixels, chans), inverse


def group_back(grad, normed, inverse, size):
    pixels, chans = grad.shape
    upper = grad.reshape(pixels, chans // size, size)
    lower = normed.reshape(pixels, chans // size, size)
    first = jnp.mean(upper, axis=(0, 2), keepdims=True)
    second = jnp.mean(upper * lower, axis=(0, 2), keepdims=True)
    return ((upper - first - lower * second) * inverse).reshape(pixels, chans)


def taps_of(flat, rows, cols, flipped):
    chans = flat.shape[-1]
    padded = jnp.pad(flat.reshape(rows, cols, chans), ((1, 1), (1, 1), (0, 0)))
    pieces = []
    for r in range(3):
        for c in range(3):
            top, left = (2 - r, 2 - c) if flipped else (r, c)
            pieces.append(padded[top : top + rows, left : left + cols].reshape(rows * cols, chans))
    return jnp.concatenate(pieces, 1)


def columns(weight, parts):
    rows, chans = weight.shape
    return weight.reshape(rows, chans // (parts * 128), parts, 128).transpose(2, 1, 0, 3).reshape(parts, -1, 128)


class Wires:
    def __init__(self, sent, landed):
        self.sent, self.landed, self.used, self.held = sent, landed, [0, 0], []

    def slot(self, kind, count=1):
        self.used[kind] += count
        return self.used[kind] - count

    def copy(self, out, at, source, target, device):
        return pltpu.make_async_remote_copy(
            src_ref=source, dst_ref=target, send_sem=self.sent.at[out], recv_sem=self.landed.at[at],
            device_id=device, device_id_type=pl.DeviceIdType.MESH,
        )

    def send(self, source, target, device, out=None):
        copy = self.copy(self.slot(0) if out is None else out, self.slot(1), source, target, device)
        copy.start()
        if out is None:
            self.held.append(copy.wait_send)
        return copy

    def group(self, triples, whole):
        out, at = self.slot(0), self.slot(1)
        for source, target, device in triples:
            self.copy(out, at, source, target, device).start()
        total = self.copy(out, at, whole, whole, triples[0][2])
        self.held.append(total.wait_send)
        return total

    def drain(self):
        for finish in self.held:
            finish()


def scratch_plan(g):
    P, Q, C, B, N, J, X = g.P, g.Q, g.C, g.B, g.N, g.J, g.X
    plan = dict(
        X=((J, Q, C), bf16), vown=((16, C), bf16), vs1=((J, 16, C), bf16),
        vsum=((16, C), bf16), vs2=((N, 16, C), bf16), vecs=((J, 16, B), f32),
        eall=((N, 1, g.E), f32), wemb=((2 * g.RE, 2 * C), bf16), epart=((N, 1, 2 * C), f32),
        erx=((N, 1, 2 * C), f32), esum=((J, 1, 2 * C), f32), emb=((1, 2 * C), f32),
        A1=((2, P + 2 * g.COLS, 2 * B), bf16), A2=((2, P + 2 * g.COLS, 2 * B), bf16),
        N3=((2, P, 2 * B), bf16), O=((2, P, 2 * B), bf16),
        A1T=((C, P), bf16), A2T=((C, P), bf16), N3T=((C, P), bf16), OT=((C, P), bf16),
        st1=((J, 8, B), f32), xj=((P, B), bf16),
        h1=((P, B), f32), y1=((P, B), f32), dy1=((P, B), f32), tmp=((P, B), f32),
        W1T=((2, 9 * B, 2 * B), bf16), W2T=((2, 9 * B, 2 * B), bf16), WqT=((2, 3 * B, 2 * B), bf16),
        ctx=((B, X), bf16), ctxs=((N, B, X // N), bf16), dcx=((B, 2 * B), bf16), dcxs=((N, B, 2 * B), bf16),
        Kb=((P + B, B), bf16), Vb=((P + B, B), bf16), KT=((B, P + B), bf16), VT=((B, P + B), bf16),
        qs=((P, B), bf16), dK=((P + B, B), f32), dV=((P + B, B), f32), dqkv=((3, P, B), bf16),
        WoF=((2, C, 2 * B), bf16), dopx=((Q, C), bf16), doj=((P, B), bf16), dyj=((P, B), bf16),
        outj=((P, B), bf16), inj=((P, B), bf16),
        S=((3, P + 2 * g.COLS, B), bf16),
        dse=((J, 2, B), f32), dsall=((N, J, 2, B), f32), geb=((2 * g.RE, 2 * C), f32),
        gvec=((16, B), f32), gvs=((N, 16, B), f32), gvi=((J, 16, B), f32), gvt=((16, B), f32),
    )
    half = dict(ps=((2, 2, P, B), bf16), rc=((2, P, B), bf16), sy=((P, B), bf16), ry=((P, B), bf16))
    groups = [plan, half, half, half]
    for wide, rows in g.weights:
        depth = rows * J
        summed = {} if wide == 2 else dict(
            g=((wide, depth * N, B), bf16), rx=((N // 2, wide, depth, B), bf16), zs=((N // 2, wide, depth, B), bf16),
            zr=((N // 2, wide, depth, B), bf16),
        )
        groups.append(dict(
            w=((wide, depth * N, B), bf16), fin=((wide, depth, B), bf16), gr=((J, wide, rows, B), bf16), **summed
        ))
    return groups


def body(g, groups, *refs):
    (x_in, cond, ctx_in, w1, w2, w_emb, w_q, w_c, w_o, vec_in, dy_in) = refs[:11]
    (out, in_grad, gc1, gc2, g_emb, g_q, g_c, g_o, g_v) = refs[11:20]
    left = list(refs[20:-2])
    spaces = [types.SimpleNamespace(**{name: left.pop(0) for name in group}) for group in groups]
    s, dn_bufs, da2_bufs, da1_bufs = spaces[:4]
    c1, c2, wq, wc, wo = spaces[4:]
    for weight, shape, ref in zip(spaces[4:], g.weights, (w1, w2, w_q, w_c, w_o)):
        weight.wide, weight.rows, weight.ref = shape[0], shape[1], ref
        weight.depth = weight.rows * g.J
    rest = (wq, wc, wo)
    P, Q, C, B, N, J, COLS, SIZE = g.P, g.Q, g.C, g.B, g.N, g.J, g.COLS, g.SIZE
    T, E, RE = g.T, g.E, g.RE
    XN, TP = g.X // N, (T + 15) // 16 * 16
    Z = N // 2
    STEPS = P // Q
    wires = Wires(refs[-2], refs[-1])
    send, group = wires.send, wires.group
    d = lax.axis_index("dp")
    j = lax.axis_index("img")
    flat = d * J + j
    z, xx = lax.div(d, 2), lax.rem(d, 2)
    yy, cc = lax.div(j, 2), lax.rem(j, 2)
    sib = (d, yy * 2 + (1 - cc))
    ypeer = (d, (1 - yy) * 2 + cc)
    diag = (d, (1 - yy) * 2 + (1 - cc))
    img_peers = [ypeer, diag, sib]
    dp_peers = [(lax.rem(d + k, N), j) for k in range(1, N)]
    zdev = [lax.rem(z + k, Z) for k in range(Z)]
    zsrc = [lax.rem(z + Z - k, Z) for k in range(Z)]
    xpeer = (z * 2 + (1 - xx), j)

    def lanes(k):
        return pl.ds(pl.multiple_of(k * B, B), B)

    def rows_at(start, size, unit):
        return pl.ds(pl.multiple_of(start, unit), size)

    def px(i):
        return pl.ds(pl.multiple_of(i * Q, Q), Q)

    def each(fn, init=None):
        if init is None:
            lax.fori_loop(0, STEPS, lambda i, carry: (fn(i), carry)[1], 0)
            return None
        return lax.fori_loop(0, STEPS, fn, init)

    def mm(a, b):
        return jnp.dot(a, b, preferred_element_type=f32)

    def mm_t(a, b):
        return lax.dot_general(a, b, (((1,), (1,)), ((), ())), preferred_element_type=f32)

    lane8 = lax.broadcasted_iota(jnp.int32, (8, B), 1)

    def group_sum(row):
        v = jnp.broadcast_to(row, (8, B))
        step = 1
        while step < SIZE:
            down, up = pltpu.roll(v, B - step, 1), pltpu.roll(v, step, 1)
            v = v + jnp.where((lane8 & step) == 0, down, up)
            step *= 2
        return v[0:1]

    def colsum(v):
        while v.shape[0] % 32 == 0:
            half = v.shape[0] // 2
            v = v[:half] + v[half:]
        return jnp.sum(v, axis=0, keepdims=True)

    zero_row = jnp.zeros((1, B), f32)
    count = P * SIZE

    def moments(load):
        total = each(lambda i, a: a + colsum(load(i)), zero_row)
        mean = group_sum(total) * (1.0 / count)
        spread = each(lambda i, a: a + colsum(jnp.square(load(i) - mean)), zero_row)
        return mean, lax.rsqrt(group_sum(spread) * (1.0 / count) + 1e-05)

    def column_of(v):
        return lax.rem(lax.broadcasted_iota(jnp.int32, v.shape, 0), COLS)

    def from_left(v):
        return jnp.where(column_of(v) == 0, 0.0, pltpu.roll(v, 1, 0))

    def from_right(v):
        return jnp.where(column_of(v) == COLS - 1, 0.0, pltpu.roll(v, v.shape[0] - 1, 0))

    BIG = 2 * Q

    def big(i):
        return pl.ds(i * BIG, BIG)

    hot = lax.broadcasted_iota(jnp.int32, (16, C), 1) == (
        lax.broadcasted_iota(jnp.int32, (16, C), 0) + flat * g.VW
    )
    hot = jnp.where(hot, 1.0, 0.0).astype(bf16)
    own_vec = mm(vec_in[...], hot).astype(bf16)
    s.vown[...] = own_vec
    s.vs1[j] = own_vec
    e_own = cond[...].astype(f32)
    e_own = (e_own * jax.nn.sigmoid(e_own)).astype(bf16).astype(f32)
    s.eall[d] = e_own

    barrier = pltpu.get_barrier_semaphore()
    for device in img_peers + dp_peers:
        pl.semaphore_signal(barrier, inc=1, device_id=device, device_id_type=pl.DeviceIdType.MESH)
    pl.semaphore_wait(barrier, len(img_peers) + len(dp_peers))

    def stage_img(W):
        start = d * W.depth + j * W.rows
        W.img = group(
            [
                (W.ref.at[:, rows_at(t * C + device[1] * B, B, B)], W.w.at[t, rows_at(start, W.rows, 16), :], device)
                for device in img_peers
                for t in range(W.wide)
            ],
            W.w.at[:, 0 : (J - 1) * W.rows, :],
        )

    def own_img(W):
        start = d * W.depth + j * W.rows
        for t in range(W.wide):
            W.w[t, rows_at(start, W.rows, 16), :] = W.ref[:, rows_at(t * C + j * B, B, B)]

    def block(W, ref, owner):
        return ref.at[:, rows_at(owner * W.depth, W.depth, 16), :]

    def img_done(W):
        W.img.wait_recv()

    above, below = z < Z - 1, z > 0
    up, down = ((z + 1) * 2 + xx, j), ((z - 1) * 2 + xx, j)

    def piece(W, start, size):
        p = types.SimpleNamespace(W=W, start=start, size=size)
        p.zr, p.xr, p.zs, p.xs = wires.slot(1, Z), wires.slot(1), wires.slot(0), wires.slot(0)
        p.at = lambda owner: W.w.at[:, rows_at(owner * W.depth + start, size, 16), :]
        p.first = lambda count: W.w.at[:, 0 : count * size, :]

        def finish():
            wires.copy(p.xs, p.xr, p.first(Z), p.first(Z), xpeer).wait_send()
            for count, gate in ((Z + 1, above & below), (1, (z == 0) | (z == Z - 1))):
                pl.when(gate)(
                    lambda: wires.copy(p.zs, p.xr, p.first(count), p.first(count), xpeer).wait_send()
                )

        wires.held.append(finish)
        return p

    def move(p, owner, device):
        here = p.at(owner * 2 + xx)
        wires.copy(p.zs, p.zr + owner, here, here, device).start()

    def across(p, owner):
        here = p.at(owner * 2 + xx)
        wires.copy(p.xs, p.xr, here, here, xpeer).start()

    def z_start(pieces):
        for p in pieces:
            pl.when(above)(lambda: move(p, z, up))
            pl.when(below)(lambda: move(p, z, down))
        for p in pieces:
            across(p, z)

    def z_step(pieces, step):
        def take(owner, onward, device):
            for p in pieces:
                here = p.at(owner * 2 + xx)
                wires.copy(p.zs, p.zr + owner, here, here, xpeer).wait_recv()
                if step < Z - 1:
                    pl.when(onward)(lambda: move(p, owner, device))
                across(p, owner)

        pl.when(z >= step)(lambda: take(z - step, above, up))
        pl.when(z + step < Z)(lambda: take(z + step, below, down))

    def arrive(pieces):
        for p in pieces:
            wires.copy(p.xs, p.xr, p.first(Z), p.first(Z), xpeer).wait_recv()

    def halves(W):
        half = W.depth // 32 * 16
        return [piece(W, 0, half), piece(W, half, W.depth - half)]

    p1, p2 = halves(c1), halves(c2)
    pq, pc, po = ([piece(W, 0, W.depth)] for W in rest)

    def gather_start(mine):
        return types.SimpleNamespace(y=send(mine, mine, ypeer), c=send(mine, mine, sib))

    def gather_near(state):
        state.c.wait_recv()

    def gather_far(state, theirs):
        state.y.wait_recv()
        state.f = send(theirs, theirs, sib)

    def gather_end(state):
        state.f.wait_recv()

    stage_img(c1)
    stage_img(wo)
    v_stage1 = group([(s.vown, s.vs1.at[j], device) for device in img_peers], s.vs1.at[0 : J - 1])
    x_own = s.X.at[j]
    x_state = types.SimpleNamespace(y=send(x_in, x_own, ypeer), c=send(x_in, x_own, sib))
    e_stage1 = group([(s.eall.at[d], s.eall.at[d], device) for device in dp_peers], s.eall.at[0 : N - 1])
    own_img(c1)
    s.X[j] = x_in[...]
    for W in (c2, *rest):
        own_img(W)
    for buf in (s.A1, s.A2):
        for h in range(2):
            buf[h, 0:COLS, :] = jnp.zeros((COLS, 2 * B), bf16)
            buf[h, P + COLS : P + 2 * COLS, :] = jnp.zeros((COLS, 2 * B), bf16)
    for c in range(3):
        s.S[c, 0:COLS, :] = jnp.zeros((COLS, B), bf16)
        s.S[c, P + COLS : P + 2 * COLS, :] = jnp.zeros((COLS, B), bf16)
    s.ctx[...] = jnp.zeros((B, g.X), bf16)
    s.ctx[0:T, :] = ctx_in[...]
    if TP < B:
        s.ctxs[:, TP:B, :] = jnp.zeros((N, B - TP, XN), bf16)
        s.dcxs[:, TP:B, :] = jnp.zeros((N, B - TP, 2 * B), bf16)
    img_done(c1)
    z_start(p1[:1])
    z_start(p1[1:])
    img_done(wo)
    z_start(po)
    v_stage1.wait_recv()
    total = s.vs1[0].astype(f32)
    for k in range(1, J):
        total = total + s.vs1[k].astype(f32)
    s.vsum[...] = total.astype(bf16)
    s.vs2[d] = total.astype(bf16)
    v_stage2 = group([(s.vsum, s.vs2.at[d], device) for device in dp_peers], s.vs2.at[0 : N - 1])
    stage_img(c2)

    x_state.y.wait_recv()
    far = s.X.at[(1 - yy) * 2 + cc]
    x_state.f = send(far, far, sib)
    stage_img(wq)
    stage_img(wc)
    dy_copies = group(
        [(dy_in.at[:, lanes(device[1])], s.dyj.at[rows_at(j * Q, Q, Q), :], device) for device in img_peers],
        s.dyj.at[0 : P - Q, :],
    )
    s.dyj[rows_at(j * Q, Q, Q), :] = dy_in[:, lanes(j)]
    z_step(p1[:1], 1)
    z_step(p1[1:] + po, 1)
    img_done(c2)
    z_start(p2[:1])

    e_stage1.wait_recv()
    s.wemb[...] = jnp.zeros((2 * RE, 2 * C), bf16)
    s.wemb[rows_at(lax.rem(flat, 2) * RE, RE, 16), :] = w_emb[...]
    e_at = rows_at(lax.div(flat, 2) * (2 * RE), 2 * RE, B)
    e_rows = jnp.concatenate([s.eall[k, :, e_at] for k in range(N)], axis=0)
    part = mm(e_rows.astype(bf16), s.wemb[...])
    for k in range(N):
        s.epart[k] = part[k : k + 1]
    s.erx[d] = s.epart[d]
    e_stage2 = group([(s.epart.at[device[0]], s.erx.at[d], device) for device in dp_peers], s.erx.at[0 : N - 1])

    x_state.c.wait_recv()
    x_state.f.wait_recv()

    def load_x(k):
        return lambda i: s.X[i, :, k * B : (k + 1) * B].astype(f32)

    def stats(k):
        mean, inverse = moments(load_x(k))
        s.st1[k, 0:1, :] = mean
        s.st1[k, 1:2, :] = inverse

    stats(0)
    stats(1)
    z_step(p1[:1], 2)
    z_step(p1[1:] + po, 2)
    z_start(p2[1:])
    stats(2)
    stats(3)
    e_stage2.wait_recv()
    total = s.erx[0]
    for k in range(1, N):
        total = total + s.erx[k]
    s.esum[j] = total
    e_stage3 = group([(s.esum.at[j], s.esum.at[j], device) for device in img_peers], s.esum.at[0 : J - 1])
    v_stage2.wait_recv()
    total = s.vs2[0].astype(f32)
    for k in range(1, N):
        total = total + s.vs2[k].astype(f32)
    for k in range(J):
        s.vecs[k] = total[:, k * B : (k + 1) * B]

    def vec(row):
        return s.vecs[j, row : row + 1, :]

    z_step(p1[:1], 3)
    z_step(p1[1:] + po, 3)
    img_done(wq)
    z_start(pq)
    for k in range(J):
        mean, inverse = s.st1[k, 0:1, :], s.st1[k, 1:2, :]
        gain, bias = s.vecs[k, 0:1, :], s.vecs[k, 1:2, :]
        load = load_x(k)

        def act(i):
            t1 = (load(i) - mean) * inverse * gain + bias
            a1 = t1 * jax.nn.sigmoid(t1)
            s.A1[k // 2, rows_at(i * Q + COLS, Q, COLS), (k % 2) * B : (k % 2 + 1) * B] = a1.astype(bf16)

        each(act)

    def turn(source, target, offset):
        def one(i):
            for h in range(2):
                v = source[h, rows_at(i * Q + offset, Q, 16), :]
                target[h * 2 * B : (h + 1) * 2 * B, px(i)] = v.T
        each(one)

    each(lambda i: s.xj.__setitem__((px(i), slice(None)), s.X[i, :, lanes(j)]))
    z_step(p2[:1], 1)
    z_step(p2[1:], 1)
    img_done(wc)
    z_start(pc)
    e_stage3.wait_recv()
    total = s.esum[0]
    for k in range(1, J):
        total = total + s.esum[k]
    s.emb[...] = total
    scale = 1.0 + (s.emb[:, lanes(j)] + vec(14))
    shift = s.emb[:, lanes(j + J)] + vec(15)
    arrive(po)
    wo_at = s.WoF.at[yy, :, lanes(cc)]
    s.WoF[yy, :, lanes(cc)] = wo.w[0]
    wo_state = gather_start(wo_at)
    arrive(p1)

    def convolve(A, W, emit):
        right = jnp.concatenate(
            [
                jnp.concatenate([W[0, (3 * r + c) * C : (3 * r + c + 1) * C, :] for r in range(3)], axis=0)
                for c in range(3)
            ],
            axis=1,
        )
        for i in range(P // BIG):
            left = jnp.concatenate(
                [A[h, i * BIG + r * COLS : (i + 1) * BIG + r * COLS, :] for r in range(3) for h in range(2)], axis=1
            )
            p = mm(left, right)
            emit(big(i), p[:, B : 2 * B] + from_left(p[:, :B]) + from_right(p[:, 2 * B :]))

    def save_h1(at, v):
        s.h1[at, :] = v + vec(2)

    convolve(s.A1, c1.w, save_h1)
    mean2, inv2 = moments(lambda i: s.h1[px(i), :])
    gather_far(wo_state, s.WoF.at[1 - yy, :, lanes(cc)])
    gather_near(wo_state)
    gather_end(wo_state)

    def xh2(i):
        return (s.h1[px(i), :] - mean2) * inv2

    def u_of(i):
        return (xh2(i) * vec(3) + vec(4)) * scale + shift

    def act2(i):
        u = u_of(i)
        s.A2[yy, rows_at(i * Q + COLS, Q, COLS), lanes(cc)] = (u * jax.nn.sigmoid(u)).astype(bf16)

    def halves_out(act, place):
        states = []
        for i in range(P // BIG):
            lax.fori_loop(i * BIG // Q, (i + 1) * BIG // Q, lambda n, carry: (act(n), carry)[1], 0)
            states.append(gather_start(place(i, yy)))
        return states

    def halves_in(states, place):
        for i, state in enumerate(states):
            gather_far(state, place(i, 1 - yy))

    def halves_end(states):
        for state in states:
            gather_near(state)
            gather_end(state)

    def a2_at(i, half):
        return s.A2.at[half, pl.ds(COLS + i * BIG, BIG), lanes(cc)]

    a2_state = halves_out(act2, a2_at)
    for h in range(2):
        part = mm_t(dy_in[:, 0 : 2 * B], s.WoF[0, h * 2 * B : (h + 1) * 2 * B, :])
        part = part + mm_t(dy_in[:, 2 * B : 4 * B], s.WoF[1, h * 2 * B : (h + 1) * 2 * B, :])
        s.dopx[:, h * 2 * B : (h + 1) * 2 * B] = part.astype(bf16)
    do_copies = group(
        [(s.dopx.at[:, lanes(device[1])], s.doj.at[rows_at(j * Q, Q, Q), :], device) for device in img_peers],
        s.doj.at[0 : P - Q, :],
    )
    s.doj[rows_at(j * Q, Q, Q), :] = s.dopx[:, lanes(j)]
    z_step(p2[:1], 2)
    z_step(p2[1:], 2)
    z_step(pq, 1)
    z_step(p2[:1], 3)
    z_step(p2[1:], 3)
    z_step(pc, 1)
    z_step(pq, 2)
    halves_in(a2_state, a2_at)
    turn(s.A1, s.A1T, COLS)
    halves_end(a2_state)
    z_step(pc, 2)
    z_step(pq, 3)
    arrive(p2)

    def save_y1(at, v):
        s.y1[at, :] = s.xj[at, :].astype(f32) + v + vec(5)

    convolve(s.A2, c2.w, save_y1)
    mean3, inv3 = moments(lambda i: s.y1[px(i), :])

    def xh3(i):
        return (s.y1[px(i), :] - mean3) * inv3

    def act3(i):
        s.N3[yy, px(i), lanes(cc)] = (xh3(i) * vec(6) + vec(7)).astype(bf16)

    def n_at(i, half):
        return s.N3.at[half, big(i), lanes(cc)]

    n_state = halves_out(act3, n_at)
    turn(s.A2, s.A2T, COLS)

    def turn_weights(W, target, taps, stride):
        for h in range(2):
            for t in range(taps):
                v = W(t)[rows_at(h * 2 * B, 2 * B, 16), :]
                target[h, t * B : (t + 1) * B, :] = v.T

    def conv_tap(W):
        return lambda t: W.w.at[0, pl.ds(t * C, C), :]

    turn_weights(conv_tap(c2), s.W2T, 9, C)
    z_step(pc, 3)
    halves_in(n_state, n_at)
    turn_weights(conv_tap(c1), s.W1T, 9, C)
    arrive(pq)
    arrive(pc)
    turn_weights(lambda t: wq.w.at[t], s.WqT, 3, C)
    tokens = lax.broadcasted_iota(jnp.int32, (B, B), 0) < T
    for t, target in enumerate((s.Kb, s.Vb)):
        v = mm(s.ctx[...], wc.w[t]) + vec(12 + t)
        target[P : P + B, :] = jnp.where(tokens, v, 0.0).astype(bf16)
    halves_end(n_state)

    def tokens_of(owner):
        return s.ctx.at[0:TP, rows_at(owner * XN, XN, B)]

    ctx_copies = group(
        [(tokens_of(device[0]), s.ctxs.at[d, 0:TP, :], device) for device in dp_peers],
        s.ctxs.at[0 : N - 1, 0:TP, :],
    )
    s.ctxs[d, 0:TP, :] = tokens_of(d)[...]

    def project(at):
        left = jnp.concatenate([s.N3[0, at, :], s.N3[1, at, :]], axis=1)
        right = jnp.concatenate([wq.w[t] for t in range(3)], axis=1)
        v = mm(left, right)
        q = (v[:, :B] + vec(9)).astype(bf16)
        s.qs[at, :] = (q.astype(f32) * g.FACTOR).astype(bf16)
        s.Kb[at, :] = (v[:, B : 2 * B] + vec(10)).astype(bf16)
        s.Vb[at, :] = (v[:, 2 * B :] + vec(11)).astype(bf16)

    for i in range(P // BIG):
        project(big(i))
    for source, target in ((s.Kb, s.KT), (s.Vb, s.VT)):
        for k in range(0, P + B, B):
            target[:, k : k + B] = source[k : k + B, :].T
    do_copies.wait_recv()
    dy_copies.wait_recv()
    s.dK[...] = jnp.zeros((P + B, B), f32)
    s.dV[...] = jnp.zeros((P + B, B), f32)

    HEAD_ = g.HEAD
    lane_row = lax.broadcasted_iota(jnp.int32, (1, B), 1)
    span = 2 * Q
    known = lax.broadcasted_iota(jnp.int32, (B, span), 0) < T
    keeps = [jnp.where(lax.div(lane_row, HEAD_) == h, 1.0, 0.0).astype(bf16) for h in range(B // HEAD_)]

    def attend(i):
        at = pl.ds(i * span, span)
        q_i, do_i = s.qs[at, :], s.doj[at, :]
        q_m = jnp.concatenate([q_i * keep for keep in keeps], axis=0)
        do_m = jnp.concatenate([do_i * keep for keep in keeps], axis=0)
        all_scores, all_dp = mm_t(s.Kb[...], q_m), mm_t(s.Vb[...], do_m)
        low, slope, mixed, back = [], [], [], []
        for h in range(B // HEAD_):
            scores = all_scores[:, h * span : (h + 1) * span]
            scores = jnp.concatenate([scores[:P], jnp.where(known, scores[P:], -1e30)], axis=0)
            e = jnp.exp(scores - jnp.max(scores, axis=0, keepdims=True))
            probs = e * (1.0 / jnp.sum(e, axis=0, keepdims=True))
            pb = probs.astype(bf16)
            mixed.append(mm(s.VT[h * HEAD_ : (h + 1) * HEAD_, :], pb))
            dp = all_dp[:, h * span : (h + 1) * span]
            ds = (probs * (dp - jnp.sum(dp * probs, axis=0, keepdims=True))).astype(bf16)
            back.append(mm(s.KT[h * HEAD_ : (h + 1) * HEAD_, :], ds))
            low.append(pb)
            slope.append(ds)
        s.dV[...] += mm(jnp.concatenate(low, axis=1), do_m)
        s.dK[...] += mm(jnp.concatenate(slope, axis=1), q_m)
        s.O[yy, at, lanes(cc)] = jnp.concatenate(mixed, axis=0).T.astype(bf16)
        s.dqkv[0, at, :] = (jnp.concatenate(back, axis=0).T * g.FACTOR).astype(bf16)
        return gather_start(s.O.at[yy, at, lanes(cc)])

    o_states = [attend(i) for i in range(P // span)]

    def grads_kv(i):
        s.dqkv[1, px(i), :] = s.dK[px(i), :].astype(bf16)
        s.dqkv[2, px(i), :] = s.dV[px(i), :].astype(bf16)

    each(grads_kv)

    def scatter(bufs, left, right):
        ps, rc, sy, ry = bufs.ps, bufs.rc, bufs.sy, bufs.ry
        near, y_in = [], []
        part = BIG // Q

        def halves_of(slot, half):
            other = 1 - yy if slot == 0 else yy

            at = big(half)
            v = mm(left(half * BIG, BIG), right[other]).astype(bf16)
            ps[slot, 0, at, :] = v[:, :B]
            ps[slot, 1, at, :] = v[:, B:]
            return send(ps.at[slot, 1 - cc, at, :], rc.at[slot, at, :], sib)

        far = [halves_of(0, half) for half in range(P // BIG)]
        for half in range(P // BIG):
            near.append(halves_of(1, half))
            far[half].wait_recv()

            def add(n, carry):
                i = n + half * part
                v = ps[0, cc, px(i), :].astype(f32) + rc[0, px(i), :].astype(f32)
                sy[px(i), :] = v.astype(bf16)
                return carry

            lax.fori_loop(0, part, add, 0)
            at = big(half)
            y_in.append(send(sy.at[at, :], ry.at[at, :], ypeer))

        def done():
            for copy in near + y_in:
                copy.wait_recv()

        def load(i):
            v = ps[1, cc, px(i), :].astype(f32) + rc[1, px(i), :].astype(f32)
            return v + ry[px(i), :].astype(f32)

        return done, load

    order = sorted(range(1, Z), key=lambda k: -min(k, Z - k)) + [0]

    def sum_start(W):
        W.sx, W.zout, W.zin = {}, wires.slot(0), wires.slot(1)
        out = wires.slot(0)
        for k in order:
            W.sx[k] = send(block(W, W.g, zdev[k] * 2 + (1 - xx)), W.rx.at[k], xpeer, out)
        wires.held.append(wires.copy(out, W.zin, W.rx, W.rx, xpeer).wait_send)

    def sum_block(W, k):
        W.sx[k].wait_recv()
        at = rows_at((zdev[k] * 2 + xx) * W.depth, W.depth, 16)
        v = W.g[:, at, :].astype(f32) + W.rx[k].astype(f32)
        W.zs[k] = v.astype(bf16)
        if k:
            wires.copy(W.zout, W.zin, W.zs.at[k], W.zr.at[k], (zdev[k] * 2 + xx, j)).start()

    def sum_z(W):
        for k in order:
            sum_block(W, k)

    def sum_img(W):
        total = wires.copy(W.zout, W.zin, W.zr.at[0 : Z - 1], W.zr.at[0 : Z - 1], xpeer)
        total.wait_recv()
        wires.held.append(total.wait_send)
        v = W.zs[0].astype(f32)
        for k in range(1, Z):
            v = v + W.zr[k].astype(f32)
        to_rows(W, jnp.concatenate([v[t] for t in range(W.wide)], axis=1))

    def to_rows(W, v):
        for t in range(W.wide):
            W.fin[t] = v[:, t * B : (t + 1) * B].astype(bf16)
        W.simg = group(
            [
                (W.fin.at[:, rows_at(device[1] * W.rows, W.rows, 16), :], W.gr.at[j], device)
                for device in img_peers
            ],
            W.gr.at[0 : J - 1],
        )
        W.gr[j] = W.fin[:, rows_at(j * W.rows, W.rows, 16), :]

    def sum_end(W, target):
        W.simg.wait_recv()
        for k in range(J):
            for t in range(W.wide):
                target[:, t * C + k * B : t * C + (k + 1) * B] = W.gr[k, t].astype(f32)

    dn_done, dn_at = scatter(
        dn_bufs, lambda at, size: jnp.concatenate([s.dqkv[t, pl.ds(at, size), :] for t in range(3)], axis=1), s.WqT
    )
    turn(s.N3, s.N3T, 0)
    for h in range(2):
        at = slice(h * 2 * B, (h + 1) * 2 * B)
        v = mm(s.N3T[at, :], jnp.concatenate([s.dqkv[t] for t in range(3)], axis=1)).astype(bf16)
        for t in range(3):
            wq.g[t, at, :] = v[:, t * B : (t + 1) * B]
    sum_start(wq)
    s.dcx[...] = jnp.concatenate([s.dK[P : P + B, :], s.dV[P : P + B, :]], axis=1).astype(bf16)
    s.dcxs[d] = s.dcx[...]
    dcx_copies = group(
        [(s.dcx.at[0:TP, :], s.dcxs.at[d, 0:TP, :], device) for device in dp_peers],
        s.dcxs.at[0 : N - 1, 0:TP, :],
    )
    for i, state in enumerate(o_states):
        gather_far(state, s.O.at[1 - yy, pl.ds(i * span, span), lanes(cc)])
    for state in o_states:
        gather_near(state)
        gather_end(state)

    def finish(at):
        left = jnp.concatenate([s.O[0, at, :], s.O[1, at, :]], axis=1)
        s.outj[at, :] = (s.y1[at, :] + mm(left, wo.w[0]) + vec(8)).astype(bf16)

    for i in range(P // BIG):
        finish(big(i))

    def to_pixels(source, target):
        copies = group(
            [(source.at[rows_at(device[1] * Q, Q, Q), :], target.at[:, lanes(j)], device) for device in img_peers],
            source.at[0 : P - Q, :],
        )
        target[:, lanes(j)] = source[rows_at(j * Q, Q, Q), :]
        return copies

    out_copies = to_pixels(s.outj, out)
    turn(s.O, s.OT, 0)
    for h in range(2):
        at = slice(h * 2 * B, (h + 1) * 2 * B)
        wo.g[0, at, :] = mm(s.OT[at, :], s.dyj[...]).astype(bf16)
    sum_start(wo)

    def back_sums(grad, normed, factor):
        def one(i, carry):
            v = grad(i)
            return carry[0] + colsum(v), carry[1] + colsum(v * normed(i))
        first, second = each(one, (zero_row, zero_row))
        return first, second, group_sum(first * factor) * (1.0 / count), group_sum(second * factor) * (1.0 / count)

    dn_done()
    sum_z(wq)
    dn_sum, dn_hat, m1, m2 = back_sums(dn_at, xh3, vec(6))

    def shifted(i, v):
        at = rows_at(i * Q + COLS, Q, COLS)
        s.S[0, at, :] = from_right(v).astype(bf16)
        s.S[1, at, :] = v.astype(bf16)
        s.S[2, at, :] = from_left(v).astype(bf16)

    def make_dh2(i, carry):
        dy = s.dyj[px(i), :].astype(f32)
        v = dy + (dn_at(i) * vec(6) - m1 - xh3(i) * m2) * inv3
        s.dy1[px(i), :] = v
        low = v.astype(bf16).astype(f32)
        shifted(i, low)
        return carry[0] + colsum(low), carry[1] + colsum(dy)

    dh2_sum, dy_sum = each(make_dh2, (zero_row, zero_row))

    def tap(t, start, size):
        r, c = t // 3, t % 3
        return s.S[c, rows_at(start + (2 - r) * COLS, size, COLS), :]

    def field(at, size):
        return jnp.concatenate([tap(t, at, size) for t in range(9)], axis=1)

    def kernel_grad(W, turned):
        for h in range(2):
            at = slice(h * 2 * B, (h + 1) * 2 * B)
            v = mm(turned[at, :], jnp.concatenate([tap(t, 0, P) for t in range(9)], axis=1)).astype(bf16)
            for t in range(9):
                W.g[0, t * C + h * 2 * B : t * C + (h + 1) * 2 * B, :] = v[:, t * B : (t + 1) * B]

    da2_done, da2_at = scatter(da2_bufs, field, s.W2T)
    kernel_grad(c2, s.A2T)
    sum_start(c2)
    sum_z(wo)
    ctx_copies.wait_recv()
    dcx_copies.wait_recv()
    v = lax.dot_general(
        s.ctxs[...].reshape(N * B, XN), s.dcxs[...].reshape(N * B, 2 * B), (((0,), (0,)), ((), ())),
        preferred_element_type=f32,
    )
    to_rows(wc, v)
    da2_done()

    def slope_of(v):
        sigma = jax.nn.sigmoid(v)
        return sigma * (1.0 + v * (1.0 - sigma))

    def make_du(i, carry):
        du = da2_at(i) * slope_of(u_of(i))
        s.tmp[px(i), :] = du
        return carry[0] + colsum(du), carry[1] + colsum(du * xh2(i))

    du_sum, du_hat = each(make_du, (zero_row, zero_row))
    gain2 = scale * vec(3)
    m1b = group_sum(du_sum * gain2) * (1.0 / count)
    m2b = group_sum(du_hat * gain2) * (1.0 / count)

    def make_dh1(i, carry):
        v = (s.tmp[px(i), :] * gain2 - m1b - xh2(i) * m2b) * inv2
        low = v.astype(bf16).astype(f32)
        shifted(i, low)
        return carry + colsum(low)

    dh1_sum = each(make_dh1, zero_row)
    dscale = vec(3) * du_hat + vec(4) * du_sum
    kernel_grad(c1, s.A1T)
    sum_start(c1)
    da1_done, da1_at = scatter(da1_bufs, field, s.W1T)
    s.dse[j] = jnp.concatenate([dscale, du_sum], axis=0)
    ds_copies = group([(s.dse.at[j], s.dse.at[j], device) for device in img_peers], s.dse.at[0 : J - 1])
    sum_img(wq)
    sum_img(wo)
    sum_z(c2)
    ds_copies.wait_recv()
    s.dsall[d] = s.dse[...]
    ds_copies = group([(s.dse, s.dsall.at[d], device) for device in dp_peers], s.dsall.at[0 : N - 1])
    sum_block(c1, order[0])
    da1_done()
    mean1, inv1 = s.st1[j, 0:1, :], s.st1[j, 1:2, :]

    def xh1(i):
        return (s.xj[px(i), :].astype(f32) - mean1) * inv1

    def make_dt1(i, carry):
        n1 = xh1(i)
        dt1 = da1_at(i) * slope_of(n1 * vec(0) + vec(1))
        s.tmp[px(i), :] = dt1
        return carry[0] + colsum(dt1), carry[1] + colsum(dt1 * n1)

    dt1_sum, dt1_hat = each(make_dt1, (zero_row, zero_row))
    sum_block(c1, order[1])
    m1c = group_sum(dt1_sum * vec(0)) * (1.0 / count)
    m2c = group_sum(dt1_hat * vec(0)) * (1.0 / count)

    def make_in(i):
        v = s.dy1[px(i), :] + (s.tmp[px(i), :] * vec(0) - m1c - xh1(i) * m2c) * inv1
        s.inj[px(i), :] = v.astype(bf16)

    each(make_in)
    in_copies = to_pixels(s.inj, in_grad)

    qkv_sums = [each(lambda i, a, t=t: a + colsum(s.dqkv[t, px(i), :].astype(f32)), zero_row) for t in range(3)]
    s.gvec[...] = jnp.concatenate(
        [dt1_hat, dt1_sum, dh1_sum, scale * du_hat, scale * du_sum, dh2_sum, dn_hat, dn_sum, dy_sum]
        + qkv_sums
        + [colsum(s.dK[P : P + B, :]), colsum(s.dV[P : P + B, :]), dscale, du_sum],
        axis=0,
    )
    gv_copies = group([(s.gvec, s.gvs.at[d], device) for device in dp_peers], s.gvs.at[0 : N - 1])
    s.gvs[d] = s.gvec[...]
    for k in order[2:]:
        sum_block(c1, k)
    gv_copies.wait_recv()
    total = s.gvs[0]
    for k in range(1, N):
        total = total + s.gvs[k]
    s.gvt[...] = total
    s.gvi[j] = total
    gv_copies = group([(s.gvt, s.gvi.at[j], device) for device in img_peers], s.gvi.at[0 : J - 1])
    sum_img(c2)
    sum_img(c1)
    sum_end(wq, g_q)
    sum_end(wc, g_c)
    sum_end(wo, g_o)
    ds_copies.wait_recv()
    e_cols = jnp.concatenate([s.eall[k, :, e_at] for k in range(N)], axis=0)
    for t in range(2):
        for k in range(J):
            rows = jnp.concatenate([s.dsall[i, k, t : t + 1, :] for i in range(N)], axis=0)
            v = lax.dot_general(
                e_cols, rows, (((0,), (0,)), ((), ())), precision=highest, preferred_element_type=f32
            )
            s.geb[:, t * C + k * B : t * C + (k + 1) * B] = v
    g_emb[...] = s.geb[rows_at(lax.rem(flat, 2) * RE, RE, 8), :]
    gv_copies.wait_recv()
    VW = g.VW
    each_block = B // VW
    pick = lax.broadcasted_iota(jnp.int32, (B, VW), 0) == (
        lax.broadcasted_iota(jnp.int32, (B, VW), 1) + lax.rem(flat, each_block) * VW
    )
    g_v[...] = jnp.dot(
        s.gvi[lax.div(flat, each_block)], jnp.where(pick, 1.0, 0.0), precision=highest,
        preferred_element_type=f32,
    )
    sum_end(c2, gc2)
    sum_end(c1, gc1)
    out_copies.wait_recv()
    in_copies.wait_recv()
    wires.drain()
    assert wires.used[0] <= g.copies[0] and wires.used[1] <= g.copies[1], wires.used


def hand_over(*refs):
    count = len(refs) // 2
    for k in range(count):
        refs[count + k][...] = refs[k][...].astype(refs[count + k].dtype)


def fused(
    image, cond, context, w_conv1, w_conv2, w_embed, w_qkv, w_context, w_out, vectors, cotangent
):
    J, N = lax.axis_size("img"), lax.axis_size("dp")
    local, cols, chans = image.shape[1:]
    g = types.SimpleNamespace(
        P=local * cols * J, Q=local * cols, C=chans, B=chans // J, N=N, J=J, COLS=cols, SIZE=chans // GROUPS,
        T=context.shape[1], X=context.shape[2], E=cond.shape[1], RE=w_embed.shape[0], VW=vectors.shape[1],
        HEAD=HEAD, FACTOR=HEAD ** (-0.5),
        weights=[
            (1, w_conv1.shape[0]), (1, w_conv2.shape[0]), (3, w_qkv.shape[0]), (2, w_context.shape[0]),
            (1, w_out.shape[0]),
        ],
    )
    groups = scratch_plan(g)
    rows = local * cols
    shape = jax.ShapeDtypeStruct
    outs = [
        shape((rows, chans), bf16), shape((rows, chans), bf16), shape(w_conv1.shape, f32), shape(w_conv2.shape, f32),
        shape(w_embed.shape, f32), shape(w_qkv.shape, f32), shape(w_context.shape, f32), shape(w_out.shape, f32),
        shape(vectors.shape, f32),
    ]
    g.copies = (89, 67 + 11 * (N // 2 + 1))
    vmem = pl.BlockSpec(memory_space=pltpu.VMEM)
    result = pl.pallas_call(
        functools.partial(body, g, groups),
        out_shape=outs,
        in_specs=[vmem] * 11,
        out_specs=[vmem] * 9,
        scratch_shapes=[pltpu.VMEM(*spec) for group in groups for spec in group.values()]
        + [pltpu.SemaphoreType.DMA((count,)) for count in g.copies],
        compiler_params=pltpu.CompilerParams(
            collective_id=0, has_side_effects=True, vmem_limit_bytes=60 * 1024 * 1024
        ),
    )(
        image.reshape(rows, chans), cond, context[0], w_conv1, w_conv2, w_embed, w_qkv, w_context, w_out, vectors,
        cotangent.reshape(rows, chans),
    )
    count = len(outs)
    result = pl.pallas_call(
        hand_over, out_shape=outs, in_specs=[vmem] * count, out_specs=[vmem] * count,
    )(*result)
    return (result[0].reshape(image.shape), result[1].reshape(image.shape), *result[2:])


def on_device(
    image, cond, context, w_conv1, w_conv2, w_embed, w_qkv, w_context, w_out, vectors, cotangent
):
    parts = lax.axis_size("img")
    place = lax.axis_index("img")
    images = lax.axis_size("dp")
    rows, cols, chans = image.shape[1] * parts, image.shape[2], image.shape[3]
    pixels = rows * cols
    width = chans // parts
    size = chans // GROUPS
    count = images * parts

    if parts == 4 and width == 128 and images % 2 == 0 and all(
        w.shape[0] % 16 == 0 for w in (w_conv1, w_conv2, w_embed, w_qkv, w_context, w_out)
    ):
        return fused(
            image, cond, context, w_conv1, w_conv2, w_embed, w_qkv, w_context, w_out, vectors, cotangent
        )

    def own(full):
        return lax.dynamic_slice_in_dim(full, place * width, width, full.ndim - 1)

    shards = (w_conv1, w_conv2, w_qkv, w_context, w_embed, w_out)
    lengths = [w.shape[0] * (w.shape[1] // chans) for w in shards]
    packed = jnp.concatenate([columns(w, parts) for w in shards], 1)
    packed = lax.all_to_all(packed, "img", 0, 0, tiled=True)
    packed = lax.all_gather(packed, "dp", axis=0, tiled=True)
    full = []
    start = 0
    for w, length in zip(shards, lengths):
        wide = w.shape[1] // chans
        piece = packed[:, start : start + length].reshape(count, wide, w.shape[0], width)
        full.append(piece.transpose(0, 2, 1, 3).reshape(count * w.shape[0], wide * width))
        start += length
    k1, k2, kq, kc, ke, ko = full
    vec_all = lax.all_gather(vectors, ("dp", "img"), axis=1, tiled=True).astype(f32)
    vec = own(vec_all)

    x_low = lax.all_gather(image[0].reshape(-1, chans), "img", axis=0, tiled=True)
    x_all = x_low.astype(f32)
    normed1_all, inverse1_all = group_norm(x_all, size)
    act1 = jax.nn.silu(normed1_all * vec_all[0] + vec_all[1]).astype(bf16)
    normed1 = own(normed1_all)
    inverse1 = lax.dynamic_slice_in_dim(inverse1_all, place * (GROUPS // parts), GROUPS // parts, 1)
    pre1 = normed1 * vec[0] + vec[1]
    hidden1 = dot(taps_of(act1, rows, cols, False), k1) + vec[2]
    cond_act = jax.nn.silu(cond.astype(f32)).astype(bf16)
    embed = dot(cond_act, ke)[0]
    scale = embed[:width] + vec[14]
    shift = embed[width:] + vec[15]
    normed2, inverse2 = group_norm(hidden1, size)
    affine2 = normed2 * vec[3] + vec[4]
    pre2 = affine2 * (1.0 + scale) + shift
    act2_own = jax.nn.silu(pre2).astype(bf16)
    act2 = lax.all_gather(act2_own, "img", axis=1, tiled=True)
    resid = own(x_all) + dot(taps_of(act2, rows, cols, False), k2) + vec[5]
    normed3, inverse3 = group_norm(resid, size)
    affine3_own = (normed3 * vec[6] + vec[7]).astype(bf16)
    affine3 = lax.all_gather(affine3_own, "img", axis=1, tiled=True)
    qkv = (dot(affine3, kq) + jnp.concatenate([vec[9], vec[10], vec[11]])).astype(bf16)
    ctx = (dot(context[0], kc) + jnp.concatenate([vec[12], vec[13]])).astype(bf16)
    tokens = ctx.shape[0]

    out_full = lax.all_gather(ko, "img", axis=1, tiled=True)
    dy_px = cotangent[0].reshape(-1, chans)
    do_px = lax.dot_general(dy_px, out_full, (((1,), (1,)), ((), ())), preferred_element_type=f32).astype(bf16)
    both = jnp.stack([do_px, dy_px])
    both = lax.all_to_all(both, "img", 2, 1, tiled=True)
    do, dy = both[0], both[1]
    dy_wide = dy.astype(f32)

    keys = jnp.concatenate([ctx[:, :width], qkv[:, width : 2 * width]], 0)
    values = jnp.concatenate([ctx[:, width:], qkv[:, 2 * width :]], 0)
    factor = HEAD ** (-0.5)
    mixed, dq, dk, dv = [], [], [], []
    for h in range(width // HEAD):
        at = slice(h * HEAD, (h + 1) * HEAD)
        q_h, k_h, v_h, do_h = qkv[:, at], keys[:, at], values[:, at], do[:, at]
        scores = dot(k_h, q_h.T) * factor
        top = jnp.max(scores, 0, keepdims=True)
        weights = jnp.exp(scores - top)
        probs = weights / jnp.sum(weights, 0, keepdims=True)
        low = probs.astype(bf16)
        mixed.append(dot(v_h.T, low).T)
        dv.append(dot(low, do_h))
        dp = dot(v_h, do_h.T)
        ds = (probs * (dp - jnp.sum(dp * probs, 0, keepdims=True))).astype(bf16)
        dq.append(dot(k_h.T, ds).T * factor)
        dk.append(dot(ds, q_h) * factor)
    mixed = jnp.concatenate(mixed, 1).astype(bf16)
    dq, dk, dv = (jnp.concatenate(v, 1) for v in (dq, dk, dv))
    mixed_all = lax.all_gather(mixed, "img", axis=1, tiled=True)
    output = (resid + dot(mixed_all, ko) + vec[8]).astype(bf16)

    dqkv = jnp.concatenate([dq, dk[tokens:], dv[tokens:]], 1).astype(bf16)
    dctx = jnp.concatenate([dk[:tokens], dv[:tokens]], 1)
    dn_part = lax.dot_general(dqkv, kq, (((1,), (1,)), ((), ())), preferred_element_type=f32)
    dn = lax.psum_scatter(dn_part.astype(bf16), "img", scatter_dimension=1, tiled=True).astype(f32)
    dy1 = dy_wide + group_back(dn * vec[6], normed3, inverse3, size)
    dh2 = dy1.astype(bf16)

    def turned(kernel):
        return kernel.reshape(9, chans, width).transpose(0, 2, 1).reshape(9 * width, chans)

    def conv_back(dh, kernel, act):
        field = taps_of(dh, rows, cols, True)
        part = dot(field, turned(kernel)).astype(bf16)
        grad = lax.psum_scatter(part, "img", scatter_dimension=1, tiled=True).astype(f32)
        kernel_grad = lax.dot_general(act, field, (((0,), (0,)), ((), ())), preferred_element_type=f32)
        return grad, kernel_grad.reshape(chans, 9, width).transpose(1, 0, 2).reshape(9 * chans, width)

    da2, gk2 = conv_back(dh2, k2, act2)
    du = da2 * silu_slope(pre2)
    dscale = jnp.sum(du * affine2, 0)
    dshift = jnp.sum(du, 0)
    dz = du * (1.0 + scale)
    dh1 = group_back(dz * vec[3], normed2, inverse2, size).astype(bf16)
    da1, gk1 = conv_back(dh1, k1, act1)
    dt1 = da1 * silu_slope(pre1)
    in_grad = (dy1 + group_back(dt1 * vec[0], normed1, inverse1, size)).astype(bf16)

    tops = lax.all_to_all(jnp.stack([output, in_grad]), "img", 1, 2, tiled=True)
    gkq = lax.dot_general(affine3, dqkv, (((0,), (0,)), ((), ())), preferred_element_type=f32)
    gkc = lax.dot_general(context[0], dctx.astype(bf16), (((0,), (0,)), ((), ())), preferred_element_type=f32)
    gko = lax.dot_general(mixed_all, dy, (((0,), (0,)), ((), ())), preferred_element_type=f32)
    gke = cond_act[0].astype(f32)[:, None] * jnp.concatenate([dscale, dshift])[None, :]
    grad_vec = jnp.stack(
        [
            jnp.sum(dt1 * normed1, 0),
            jnp.sum(dt1, 0),
            jnp.sum(dh1.astype(f32), 0),
            jnp.sum(dz * normed2, 0),
            jnp.sum(dz, 0),
            jnp.sum(dh2.astype(f32), 0),
            jnp.sum(dn * normed3, 0),
            jnp.sum(dn, 0),
            jnp.sum(dy_wide, 0),
        ]
        + [jnp.sum(v.astype(f32), 0) for v in jnp.split(dqkv, 3, 1)]
        + [jnp.sum(v, 0) for v in jnp.split(dctx, 2, 1)]
        + [dscale, dshift],
        0,
    )
    grads = (gk1, gk2, gkq, gkc, gke, gko)
    pieces = []
    for w, g in zip(shards, grads):
        wide = w.shape[1] // chans
        piece = g.reshape(count, w.shape[0], wide, width).transpose(0, 2, 1, 3)
        pieces.append(piece.reshape(count, wide * w.shape[0], width))
    packed = jnp.concatenate(pieces, 1).astype(bf16)
    packed = lax.psum_scatter(packed, "dp", scatter_dimension=0, tiled=True).astype(f32)
    packed = lax.all_to_all(packed.astype(bf16), "img", 0, 0, tiled=True).astype(f32)
    outs = []
    start = 0
    for w, length in zip(shards, lengths):
        wide = w.shape[1] // chans
        piece = packed[:, start : start + length].reshape(parts, wide, w.shape[0], width)
        outs.append(piece.transpose(2, 1, 0, 3).reshape(w.shape))
        start += length
    vec_sum = lax.all_gather(lax.psum(grad_vec, "dp"), "img", axis=1, tiled=True)
    each = chans // count
    g_vec = lax.dynamic_slice_in_dim(
        vec_sum, (lax.axis_index("dp") * parts + place) * each, each, 1
    )
    g1, g2, gq, gc, ge, go = outs
    return (tops[0].reshape(image.shape), tops[1].reshape(image.shape), g1, g2, ge, gq, gc, go, g_vec)


def solution(mesh):
    whole = P(("dp", "img"), None)
    field = P("dp", "img", None, None)
    in_specs = (
        field, P("dp", None), P("dp", None, None), whole, whole, whole, whole, whole, whole,
        P(None, ("dp", "img")), field,
    )
    out_specs = (field, field, whole, whole, whole, whole, whole, whole, P(None, ("dp", "img")))
    return jax.shard_map(
        on_device, mesh=mesh, in_specs=in_specs, out_specs=out_specs, check_vma=False
    )
```

```python
import functools
import types

import jax
import jax.numpy as jnp
from jax import lax
from jax.experimental import pallas as pl
from jax.experimental.pallas import tpu as pltpu
from jax.sharding import PartitionSpec as P

HEADS = 8
HEAD = 64
GROUPS = 32

f32 = jnp.float32
bf16 = jnp.bfloat16
highest = lax.Precision.HIGHEST


def dot(a, b):
    return jnp.dot(a, b, preferred_element_type=f32)


def silu_slope(value):
    sigma = jax.nn.sigmoid(value)
    return sigma * (1.0 + value * (1.0 - sigma))


def group_norm(flat, size):
    pixels, chans = flat.shape
    part = flat.reshape(pixels, chans // size, size)
    mean = jnp.mean(part, axis=(0, 2), keepdims=True)
    spread = jnp.mean(jnp.square(part - mean), axis=(0, 2), keepdims=True)
    inverse = lax.rsqrt(spread + 1e-05)
    return ((part - mean) * inverse).reshape(pixels, chans), inverse


def group_back(grad, normed, inverse, size):
    pixels, chans = grad.shape
    upper = grad.reshape(pixels, chans // size, size)
    lower = normed.reshape(pixels, chans // size, size)
    first = jnp.mean(upper, axis=(0, 2), keepdims=True)
    second = jnp.mean(upper * lower, axis=(0, 2), keepdims=True)
    return ((upper - first - lower * second) * inverse).reshape(pixels, chans)


def taps_of(flat, rows, cols, flipped):
    chans = flat.shape[-1]
    padded = jnp.pad(flat.reshape(rows, cols, chans), ((1, 1), (1, 1), (0, 0)))
    pieces = []
    for r in range(3):
        for c in range(3):
            top, left = (2 - r, 2 - c) if flipped else (r, c)
            pieces.append(padded[top : top + rows, left : left + cols].reshape(rows * cols, chans))
    return jnp.concatenate(pieces, 1)


def columns(weight, parts):
    rows, chans = weight.shape
    return weight.reshape(rows, chans // (parts * 128), parts, 128).transpose(2, 1, 0, 3).reshape(parts, -1, 128)


class Wires:
    def __init__(self, sent, landed):
        self.sent, self.landed, self.used, self.held = sent, landed, [0, 0], []

    def slot(self, kind, count=1):
        self.used[kind] += count
        return self.used[kind] - count

    def copy(self, out, at, source, target, device):
        return pltpu.make_async_remote_copy(
            src_ref=source, dst_ref=target, send_sem=self.sent.at[out], recv_sem=self.landed.at[at],
            device_id=device, device_id_type=pl.DeviceIdType.MESH,
        )

    def send(self, source, target, device, out=None):
        copy = self.copy(self.slot(0) if out is None else out, self.slot(1), source, target, device)
        copy.start()
        if out is None:
            self.held.append(copy.wait_send)
        return copy

    def group(self, triples, whole):
        out, at = self.slot(0), self.slot(1)
        for source, target, device in triples:
            self.copy(out, at, source, target, device).start()
        total = self.copy(out, at, whole, whole, triples[0][2])
        self.held.append(total.wait_send)
        return total

    def drain(self):
        for finish in self.held:
            finish()


def scratch_plan(g):
    P, Q, C, B, N, J, X = g.P, g.Q, g.C, g.B, g.N, g.J, g.X
    plan = dict(
        X=((J, Q, C), bf16), vown=((16, C), bf16), vs1=((J, 16, C), bf16),
        vsum=((16, C), bf16), vs2=((N, 16, C), bf16), vecs=((J, 16, B), f32),
        eall=((N, 1, g.E), f32), wemb=((2 * g.RE, 2 * C), bf16), epart=((N, 1, 2 * C), f32),
        erx=((N, 1, 2 * C), f32), esum=((J, 1, 2 * C), f32), emb=((1, 2 * C), f32),
        A1=((2, P + 2 * g.COLS, 2 * B), bf16), A2=((2, P + 2 * g.COLS, 2 * B), bf16),
        N3=((2, P, 2 * B), bf16), O=((2, P, 2 * B), bf16),
        A1T=((C, P), bf16), A2T=((C, P), bf16), N3T=((C, P), bf16), OT=((C, P), bf16),
        st1=((J, 8, B), f32), xj=((P, B), bf16),
        h1=((P, B), f32), y1=((P, B), f32), dy1=((P, B), f32), tmp=((P, B), f32),
        W1T=((2, 9 * B, 2 * B), bf16), W2T=((2, 9 * B, 2 * B), bf16), WqT=((2, 3 * B, 2 * B), bf16),
        ctx=((B, X), bf16), ctxs=((N, B, X // N), bf16), dcx=((B, 2 * B), bf16), dcxs=((N, B, 2 * B), bf16),
        Kb=((P + B, B), bf16), Vb=((P + B, B), bf16), KT=((B, P + B), bf16), VT=((B, P + B), bf16),
        qs=((P, B), bf16), dK=((P + B, B), f32), dV=((P + B, B), f32), dqkv=((3, P, B), bf16),
        WoF=((2, C, 2 * B), bf16), dopx=((Q, C), bf16), doj=((P, B), bf16), dyj=((P, B), bf16),
        outj=((P, B), bf16), inj=((P, B), bf16),
        S=((3, P + 2 * g.COLS, B), bf16),
        dse=((J, 2, B), f32), dsall=((N, J, 2, B), f32), geb=((2 * g.RE, 2 * C), f32),
        gvec=((16, B), f32), gvs=((N, 16, B), f32), gvi=((J, 16, B), f32), gvt=((16, B), f32),
    )
    half = dict(ps=((2, 2, P, B), bf16), rc=((2, P, B), bf16), sy=((P, B), bf16), ry=((P, B), bf16))
    groups = [plan, half, half, half]
    for wide, rows in g.weights:
        depth = rows * J
        summed = {} if wide == 2 else dict(
            g=((wide, depth * N, B), bf16), rx=((N // 2, wide, depth, B), bf16), zs=((N // 2, wide, depth, B), bf16),
            zr=((N // 2, wide, depth, B), bf16),
        )
        groups.append(dict(
            w=((wide, depth * N, B), bf16), fin=((wide, depth, B), bf16), gr=((J, wide, rows, B), bf16), **summed
        ))
    return groups


def body(g, groups, *refs):
    (x_in, cond, ctx_in, w1, w2, w_emb, w_q, w_c, w_o, vec_in, dy_in) = refs[:11]
    (out, in_grad, gc1, gc2, g_emb, g_q, g_c, g_o, g_v) = refs[11:20]
    left = list(refs[20:-2])
    spaces = [types.SimpleNamespace(**{name: left.pop(0) for name in group}) for group in groups]
    s, dn_bufs, da2_bufs, da1_bufs = spaces[:4]
    c1, c2, wq, wc, wo = spaces[4:]
    for weight, shape, ref in zip(spaces[4:], g.weights, (w1, w2, w_q, w_c, w_o)):
        weight.wide, weight.rows, weight.ref = shape[0], shape[1], ref
        weight.depth = weight.rows * g.J
    rest = (wq, wc, wo)
    P, Q, C, B, N, J, COLS, SIZE = g.P, g.Q, g.C, g.B, g.N, g.J, g.COLS, g.SIZE
    T, E, RE = g.T, g.E, g.RE
    XN, TP = g.X // N, (T + 15) // 16 * 16
    Z = N // 2
    STEPS = P // Q
    wires = Wires(refs[-2], refs[-1])
    send, group = wires.send, wires.group
    d = lax.axis_index("dp")
    j = lax.axis_index("img")
    flat = d * J + j
    z, xx = lax.div(d, 2), lax.rem(d, 2)
    yy, cc = lax.div(j, 2), lax.rem(j, 2)
    sib = (d, yy * 2 + (1 - cc))
    ypeer = (d, (1 - yy) * 2 + cc)
    diag = (d, (1 - yy) * 2 + (1 - cc))
    img_peers = [ypeer, diag, sib]
    dp_peers = [(lax.rem(d + k, N), j) for k in range(1, N)]
    zdev = [lax.rem(z + k, Z) for k in range(Z)]
    zsrc = [lax.rem(z + Z - k, Z) for k in range(Z)]
    xpeer = (z * 2 + (1 - xx), j)

    def lanes(k):
        return pl.ds(pl.multiple_of(k * B, B), B)

    def rows_at(start, size, unit):
        return pl.ds(pl.multiple_of(start, unit), size)

    def px(i):
        return pl.ds(pl.multiple_of(i * Q, Q), Q)

    def each(fn, init=None):
        if init is None:
            lax.fori_loop(0, STEPS, lambda i, carry: (fn(i), carry)[1], 0)
            return None
        return lax.fori_loop(0, STEPS, fn, init)

    def mm(a, b):
        return jnp.dot(a, b, preferred_element_type=f32)

    def mm_t(a, b):
        return lax.dot_general(a, b, (((1,), (1,)), ((), ())), preferred_element_type=f32)

    lane8 = lax.broadcasted_iota(jnp.int32, (8, B), 1)

    def group_sum(row):
        v = jnp.broadcast_to(row, (8, B))
        step = 1
        while step < SIZE:
            down, up = pltpu.roll(v, B - step, 1), pltpu.roll(v, step, 1)
            v = v + jnp.where((lane8 & step) == 0, down, up)
            step *= 2
        return v[0:1]

    def colsum(v):
        while v.shape[0] % 32 == 0:
            half = v.shape[0] // 2
            v = v[:half] + v[half:]
        return jnp.sum(v, axis=0, keepdims=True)

    zero_row = jnp.zeros((1, B), f32)
    count = P * SIZE

    def moments(load):
        total = each(lambda i, a: a + colsum(load(i)), zero_row)
        mean = group_sum(total) * (1.0 / count)
        spread = each(lambda i, a: a + colsum(jnp.square(load(i) - mean)), zero_row)
        return mean, lax.rsqrt(group_sum(spread) * (1.0 / count) + 1e-05)

    def column_of(v):
        return lax.rem(lax.broadcasted_iota(jnp.int32, v.shape, 0), COLS)

    def from_left(v):
        return jnp.where(column_of(v) == 0, 0.0, pltpu.roll(v, 1, 0))

    def from_right(v):
        return jnp.where(column_of(v) == COLS - 1, 0.0, pltpu.roll(v, v.shape[0] - 1, 0))

    BIG = 2 * Q

    def big(i):
        return pl.ds(i * BIG, BIG)

    hot = lax.broadcasted_iota(jnp.int32, (16, C), 1) == (
        lax.broadcasted_iota(jnp.int32, (16, C), 0) + flat * g.VW
    )
    hot = jnp.where(hot, 1.0, 0.0).astype(bf16)
    own_vec = mm(vec_in[...], hot).astype(bf16)
    s.vown[...] = own_vec
    s.vs1[j] = own_vec
    e_own = cond[...].astype(f32)
    e_own = (e_own * jax.nn.sigmoid(e_own)).astype(bf16).astype(f32)
    s.eall[d] = e_own

    barrier = pltpu.get_barrier_semaphore()
    for device in img_peers + dp_peers:
        pl.semaphore_signal(barrier, inc=1, device_id=device, device_id_type=pl.DeviceIdType.MESH)
    pl.semaphore_wait(barrier, len(img_peers) + len(dp_peers))

    def stage_img(W):
        start = d * W.depth + j * W.rows
        W.img = group(
            [
                (W.ref.at[:, rows_at(t * C + device[1] * B, B, B)], W.w.at[t, rows_at(start, W.rows, 16), :], device)
                for device in img_peers
                for t in range(W.wide)
            ],
            W.w.at[:, 0 : (J - 1) * W.rows, :],
        )

    def own_img(W):
        start = d * W.depth + j * W.rows
        for t in range(W.wide):
            W.w[t, rows_at(start, W.rows, 16), :] = W.ref[:, rows_at(t * C + j * B, B, B)]

    def block(W, ref, owner):
        return ref.at[:, rows_at(owner * W.depth, W.depth, 16), :]

    def img_done(W):
        W.img.wait_recv()

    above, below = z < Z - 1, z > 0
    up, down = ((z + 1) * 2 + xx, j), ((z - 1) * 2 + xx, j)

    def piece(W, start, size):
        p = types.SimpleNamespace(W=W, start=start, size=size)
        p.zr, p.xr, p.zs, p.xs = wires.slot(1, Z), wires.slot(1), wires.slot(0), wires.slot(0)
        p.at = lambda owner: W.w.at[:, rows_at(owner * W.depth + start, size, 16), :]
        p.first = lambda count: W.w.at[:, 0 : count * size, :]

        def finish():
            wires.copy(p.xs, p.xr, p.first(Z), p.first(Z), xpeer).wait_send()
            for count, gate in ((Z + 1, above & below), (1, (z == 0) | (z == Z - 1))):
                pl.when(gate)(
                    lambda: wires.copy(p.zs, p.xr, p.first(count), p.first(count), xpeer).wait_send()
                )

        wires.held.append(finish)
        return p

    def move(p, owner, device):
        here = p.at(owner * 2 + xx)
        wires.copy(p.zs, p.zr + owner, here, here, device).start()

    def across(p, owner):
        here = p.at(owner * 2 + xx)
        wires.copy(p.xs, p.xr, here, here, xpeer).start()

    def z_start(pieces):
        for p in pieces:
            pl.when(above)(lambda: move(p, z, up))
            pl.when(below)(lambda: move(p, z, down))
        for p in pieces:
            across(p, z)

    def z_step(pieces, step):
        def take(owner, onward, device):
            for p in pieces:
                here = p.at(owner * 2 + xx)
                wires.copy(p.zs, p.zr + owner, here, here, xpeer).wait_recv()
                if step < Z - 1:
                    pl.when(onward)(lambda: move(p, owner, device))
                across(p, owner)

        pl.when(z >= step)(lambda: take(z - step, above, up))
        pl.when(z + step < Z)(lambda: take(z + step, below, down))

    def arrive(pieces):
        for p in pieces:
            wires.copy(p.xs, p.xr, p.first(Z), p.first(Z), xpeer).wait_recv()

    def halves(W):
        half = W.depth // 32 * 16
        return [piece(W, 0, half), piece(W, half, W.depth - half)]

    third = c1.depth // 48 * 16
    p1 = [piece(c1, 0, third), piece(c1, third, third), piece(c1, 2 * third, c1.depth - 2 * third)]
    p2 = halves(c2)
    pq, pc, po = ([piece(W, 0, W.depth)] for W in rest)

    def gather_start(mine):
        return types.SimpleNamespace(y=send(mine, mine, ypeer), c=send(mine, mine, sib))

    def gather_near(state):
        state.c.wait_recv()

    def gather_far(state, theirs):
        state.y.wait_recv()
        state.f = send(theirs, theirs, sib)

    def gather_end(state):
        state.f.wait_recv()

    stage_img(c1)
    stage_img(wo)
    v_stage1 = group([(s.vown, s.vs1.at[j], device) for device in img_peers], s.vs1.at[0 : J - 1])
    x_own = s.X.at[j]
    x_state = types.SimpleNamespace(y=send(x_in, x_own, ypeer), c=send(x_in, x_own, sib))
    e_stage1 = group([(s.eall.at[d], s.eall.at[d], device) for device in dp_peers], s.eall.at[0 : N - 1])
    own_img(c1)
    s.X[j] = x_in[...]
    for W in (c2, *rest):
        own_img(W)
    for buf in (s.A1, s.A2):
        for h in range(2):
            buf[h, 0:COLS, :] = jnp.zeros((COLS, 2 * B), bf16)
            buf[h, P + COLS : P + 2 * COLS, :] = jnp.zeros((COLS, 2 * B), bf16)
    for c in range(3):
        s.S[c, 0:COLS, :] = jnp.zeros((COLS, B), bf16)
        s.S[c, P + COLS : P + 2 * COLS, :] = jnp.zeros((COLS, B), bf16)
    s.ctx[...] = jnp.zeros((B, g.X), bf16)
    s.ctx[0:T, :] = ctx_in[...]
    if TP < B:
        s.ctxs[:, TP:B, :] = jnp.zeros((N, B - TP, XN), bf16)
        s.dcxs[:, TP:B, :] = jnp.zeros((N, B - TP, 2 * B), bf16)
    img_done(c1)
    z_start(p1[:1])
    z_start(p1[1:])
    img_done(wo)
    z_start(po)
    v_stage1.wait_recv()
    total = s.vs1[0].astype(f32)
    for k in range(1, J):
        total = total + s.vs1[k].astype(f32)
    s.vsum[...] = total.astype(bf16)
    s.vs2[d] = total.astype(bf16)
    v_stage2 = group([(s.vsum, s.vs2.at[d], device) for device in dp_peers], s.vs2.at[0 : N - 1])
    stage_img(c2)

    x_state.y.wait_recv()
    far = s.X.at[(1 - yy) * 2 + cc]
    x_state.f = send(far, far, sib)
    stage_img(wq)
    stage_img(wc)
    dy_copies = group(
        [(dy_in.at[:, lanes(device[1])], s.dyj.at[rows_at(j * Q, Q, Q), :], device) for device in img_peers],
        s.dyj.at[0 : P - Q, :],
    )
    s.dyj[rows_at(j * Q, Q, Q), :] = dy_in[:, lanes(j)]
    z_step(p1[:1], 1)
    z_step(p1[1:] + po, 1)
    img_done(c2)
    z_start(p2[:1])

    e_stage1.wait_recv()
    s.wemb[...] = jnp.zeros((2 * RE, 2 * C), bf16)
    s.wemb[rows_at(lax.rem(flat, 2) * RE, RE, 16), :] = w_emb[...]
    e_at = rows_at(lax.div(flat, 2) * (2 * RE), 2 * RE, B)
    e_rows = jnp.concatenate([s.eall[k, :, e_at] for k in range(N)], axis=0)
    part = mm(e_rows.astype(bf16), s.wemb[...])
    for k in range(N):
        s.epart[k] = part[k : k + 1]
    s.erx[d] = s.epart[d]
    e_stage2 = group([(s.epart.at[device[0]], s.erx.at[d], device) for device in dp_peers], s.erx.at[0 : N - 1])

    x_state.c.wait_recv()
    x_state.f.wait_recv()

    def load_x(k):
        return lambda i: s.X[i, :, k * B : (k + 1) * B].astype(f32)

    def stats(k):
        mean, inverse = moments(load_x(k))
        s.st1[k, 0:1, :] = mean
        s.st1[k, 1:2, :] = inverse

    stats(0)
    stats(1)
    z_step(p1[:1], 2)
    z_step(p1[1:] + po, 2)
    z_start(p2[1:])
    stats(2)
    stats(3)
    e_stage2.wait_recv()
    total = s.erx[0]
    for k in range(1, N):
        total = total + s.erx[k]
    s.esum[j] = total
    e_stage3 = group([(s.esum.at[j], s.esum.at[j], device) for device in img_peers], s.esum.at[0 : J - 1])
    v_stage2.wait_recv()
    total = s.vs2[0].astype(f32)
    for k in range(1, N):
        total = total + s.vs2[k].astype(f32)
    for k in range(J):
        s.vecs[k] = total[:, k * B : (k + 1) * B]

    def vec(row):
        return s.vecs[j, row : row + 1, :]

    z_step(p1[:1], 3)
    z_step(p1[1:] + po, 3)
    img_done(wq)
    z_start(pq)
    for k in range(J):
        mean, inverse = s.st1[k, 0:1, :], s.st1[k, 1:2, :]
        gain, bias = s.vecs[k, 0:1, :], s.vecs[k, 1:2, :]
        load = load_x(k)

        def act(i):
            t1 = (load(i) - mean) * inverse * gain + bias
            a1 = t1 * jax.nn.sigmoid(t1)
            s.A1[k // 2, rows_at(i * Q + COLS, Q, COLS), (k % 2) * B : (k % 2 + 1) * B] = a1.astype(bf16)

        each(act)

    def turn(source, target, offset):
        def one(i):
            for h in range(2):
                v = source[h, rows_at(i * Q + offset, Q, 16), :]
                target[h * 2 * B : (h + 1) * 2 * B, px(i)] = v.T
        each(one)

    each(lambda i: s.xj.__setitem__((px(i), slice(None)), s.X[i, :, lanes(j)]))
    z_step(p2[:1], 1)
    z_step(p2[1:], 1)
    img_done(wc)
    z_start(pc)
    e_stage3.wait_recv()
    total = s.esum[0]
    for k in range(1, J):
        total = total + s.esum[k]
    s.emb[...] = total
    scale = 1.0 + (s.emb[:, lanes(j)] + vec(14))
    shift = s.emb[:, lanes(j + J)] + vec(15)
    arrive(po)
    wo_at = s.WoF.at[yy, :, lanes(cc)]
    s.WoF[yy, :, lanes(cc)] = wo.w[0]
    wo_state = gather_start(wo_at)
    arrive(p1)

    def convolve(A, W, emit):
        right = jnp.concatenate(
            [
                jnp.concatenate([W[0, (3 * r + c) * C : (3 * r + c + 1) * C, :] for r in range(3)], axis=0)
                for c in range(3)
            ],
            axis=1,
        )
        for i in range(P // BIG):
            left = jnp.concatenate(
                [A[h, i * BIG + r * COLS : (i + 1) * BIG + r * COLS, :] for r in range(3) for h in range(2)], axis=1
            )
            p = mm(left, right)
            emit(big(i), p[:, B : 2 * B] + from_left(p[:, :B]) + from_right(p[:, 2 * B :]))

    def save_h1(at, v):
        s.h1[at, :] = v + vec(2)

    convolve(s.A1, c1.w, save_h1)
    mean2, inv2 = moments(lambda i: s.h1[px(i), :])
    gather_far(wo_state, s.WoF.at[1 - yy, :, lanes(cc)])
    gather_near(wo_state)
    gather_end(wo_state)

    def xh2(i):
        return (s.h1[px(i), :] - mean2) * inv2

    def u_of(i):
        return (xh2(i) * vec(3) + vec(4)) * scale + shift

    def act2(i):
        u = u_of(i)
        s.A2[yy, rows_at(i * Q + COLS, Q, COLS), lanes(cc)] = (u * jax.nn.sigmoid(u)).astype(bf16)

    def halves_out(act, place):
        states = []
        for i in range(P // BIG):
            lax.fori_loop(i * BIG // Q, (i + 1) * BIG // Q, lambda n, carry: (act(n), carry)[1], 0)
            states.append(gather_start(place(i, yy)))
        return states

    def halves_in(states, place):
        for i, state in enumerate(states):
            gather_far(state, place(i, 1 - yy))

    def halves_end(states):
        for state in states:
            gather_near(state)
            gather_end(state)

    def a2_at(i, half):
        return s.A2.at[half, pl.ds(COLS + i * BIG, BIG), lanes(cc)]

    a2_state = halves_out(act2, a2_at)
    for h in range(2):
        part = mm_t(dy_in[:, 0 : 2 * B], s.WoF[0, h * 2 * B : (h + 1) * 2 * B, :])
        part = part + mm_t(dy_in[:, 2 * B : 4 * B], s.WoF[1, h * 2 * B : (h + 1) * 2 * B, :])
        s.dopx[:, h * 2 * B : (h + 1) * 2 * B] = part.astype(bf16)
    do_copies = group(
        [(s.dopx.at[:, lanes(device[1])], s.doj.at[rows_at(j * Q, Q, Q), :], device) for device in img_peers],
        s.doj.at[0 : P - Q, :],
    )
    s.doj[rows_at(j * Q, Q, Q), :] = s.dopx[:, lanes(j)]
    z_step(p2[:1], 2)
    z_step(p2[1:], 2)
    z_step(pq, 1)
    z_step(p2[:1], 3)
    z_step(p2[1:], 3)
    z_step(pc, 1)
    z_step(pq, 2)
    halves_in(a2_state, a2_at)
    turn(s.A1, s.A1T, COLS)
    halves_end(a2_state)
    z_step(pc, 2)
    z_step(pq, 3)
    arrive(p2)

    def save_y1(at, v):
        s.y1[at, :] = s.xj[at, :].astype(f32) + v + vec(5)

    convolve(s.A2, c2.w, save_y1)
    mean3, inv3 = moments(lambda i: s.y1[px(i), :])

    def xh3(i):
        return (s.y1[px(i), :] - mean3) * inv3

    def act3(i):
        s.N3[yy, px(i), lanes(cc)] = (xh3(i) * vec(6) + vec(7)).astype(bf16)

    def n_at(i, half):
        return s.N3.at[half, big(i), lanes(cc)]

    n_state = halves_out(act3, n_at)
    turn(s.A2, s.A2T, COLS)

    def turn_weights(W, target, taps, stride):
        for h in range(2):
            for t in range(taps):
                v = W(t)[rows_at(h * 2 * B, 2 * B, 16), :]
                target[h, t * B : (t + 1) * B, :] = v.T

    def conv_tap(W):
        return lambda t: W.w.at[0, pl.ds(t * C, C), :]

    turn_weights(conv_tap(c2), s.W2T, 9, C)
    z_step(pc, 3)
    halves_in(n_state, n_at)
    turn_weights(conv_tap(c1), s.W1T, 9, C)
    arrive(pq)
    arrive(pc)
    turn_weights(lambda t: wq.w.at[t], s.WqT, 3, C)
    tokens = lax.broadcasted_iota(jnp.int32, (B, B), 0) < T
    for t, target in enumerate((s.Kb, s.Vb)):
        v = mm(s.ctx[...], wc.w[t]) + vec(12 + t)
        target[P : P + B, :] = jnp.where(tokens, v, 0.0).astype(bf16)
    halves_end(n_state)

    def tokens_of(owner):
        return s.ctx.at[0:TP, rows_at(owner * XN, XN, B)]

    ctx_copies = group(
        [(tokens_of(device[0]), s.ctxs.at[d, 0:TP, :], device) for device in dp_peers],
        s.ctxs.at[0 : N - 1, 0:TP, :],
    )
    s.ctxs[d, 0:TP, :] = tokens_of(d)[...]

    def project(at):
        left = jnp.concatenate([s.N3[0, at, :], s.N3[1, at, :]], axis=1)
        right = jnp.concatenate([wq.w[t] for t in range(3)], axis=1)
        v = mm(left, right)
        q = (v[:, :B] + vec(9)).astype(bf16)
        s.qs[at, :] = (q.astype(f32) * g.FACTOR).astype(bf16)
        s.Kb[at, :] = (v[:, B : 2 * B] + vec(10)).astype(bf16)
        s.Vb[at, :] = (v[:, 2 * B :] + vec(11)).astype(bf16)

    for i in range(P // BIG):
        project(big(i))
    for source, target in ((s.Kb, s.KT), (s.Vb, s.VT)):
        for k in range(0, P + B, B):
            target[:, k : k + B] = source[k : k + B, :].T
    do_copies.wait_recv()
    dy_copies.wait_recv()
    s.dK[...] = jnp.zeros((P + B, B), f32)
    s.dV[...] = jnp.zeros((P + B, B), f32)

    HEAD_ = g.HEAD
    lane_row = lax.broadcasted_iota(jnp.int32, (1, B), 1)
    span = 2 * Q
    known = lax.broadcasted_iota(jnp.int32, (B, span), 0) < T
    keeps = [jnp.where(lax.div(lane_row, HEAD_) == h, 1.0, 0.0).astype(bf16) for h in range(B // HEAD_)]

    def attend(i):
        at = pl.ds(i * span, span)
        q_i, do_i = s.qs[at, :], s.doj[at, :]
        q_m = jnp.concatenate([q_i * keep for keep in keeps], axis=0)
        do_m = jnp.concatenate([do_i * keep for keep in keeps], axis=0)
        all_scores, all_dp = mm_t(s.Kb[...], q_m), mm_t(s.Vb[...], do_m)
        low, slope, mixed, back = [], [], [], []
        for h in range(B // HEAD_):
            scores = all_scores[:, h * span : (h + 1) * span]
            scores = jnp.concatenate([scores[:P], jnp.where(known, scores[P:], -1e30)], axis=0)
            e = jnp.exp(scores - jnp.max(scores, axis=0, keepdims=True))
            probs = e * (1.0 / jnp.sum(e, axis=0, keepdims=True))
            pb = probs.astype(bf16)
            mixed.append(mm(s.VT[h * HEAD_ : (h + 1) * HEAD_, :], pb))
            dp = all_dp[:, h * span : (h + 1) * span]
            ds = (probs * (dp - jnp.sum(dp * probs, axis=0, keepdims=True))).astype(bf16)
            back.append(mm(s.KT[h * HEAD_ : (h + 1) * HEAD_, :], ds))
            low.append(pb)
            slope.append(ds)
        s.dV[...] += mm(jnp.concatenate(low, axis=1), do_m)
        s.dK[...] += mm(jnp.concatenate(slope, axis=1), q_m)
        s.O[yy, at, lanes(cc)] = jnp.concatenate(mixed, axis=0).T.astype(bf16)
        s.dqkv[0, at, :] = (jnp.concatenate(back, axis=0).T * g.FACTOR).astype(bf16)
        return gather_start(s.O.at[yy, at, lanes(cc)])

    o_states = [attend(i) for i in range(P // span)]

    def grads_kv(i):
        s.dqkv[1, px(i), :] = s.dK[px(i), :].astype(bf16)
        s.dqkv[2, px(i), :] = s.dV[px(i), :].astype(bf16)

    each(grads_kv)

    def scatter(bufs, left, right):
        ps, rc, sy, ry = bufs.ps, bufs.rc, bufs.sy, bufs.ry
        near, y_in = [], []
        part = BIG // Q

        def halves_of(slot, half):
            other = 1 - yy if slot == 0 else yy

            at = big(half)
            v = mm(left(half * BIG, BIG), right[other]).astype(bf16)
            ps[slot, 0, at, :] = v[:, :B]
            ps[slot, 1, at, :] = v[:, B:]
            return send(ps.at[slot, 1 - cc, at, :], rc.at[slot, at, :], sib)

        far = [halves_of(0, half) for half in range(P // BIG)]
        for half in range(P // BIG):
            near.append(halves_of(1, half))
            far[half].wait_recv()

            def add(n, carry):
                i = n + half * part
                v = ps[0, cc, px(i), :].astype(f32) + rc[0, px(i), :].astype(f32)
                sy[px(i), :] = v.astype(bf16)
                return carry

            lax.fori_loop(0, part, add, 0)
            at = big(half)
            y_in.append(send(sy.at[at, :], ry.at[at, :], ypeer))

        def done():
            for copy in near + y_in:
                copy.wait_recv()

        def load(i):
            v = ps[1, cc, px(i), :].astype(f32) + rc[1, px(i), :].astype(f32)
            return v + ry[px(i), :].astype(f32)

        return done, load

    order = sorted(range(1, Z), key=lambda k: -min(k, Z - k)) + [0]

    def sum_start(W):
        W.sx, W.zout, W.zin = {}, wires.slot(0), wires.slot(1)
        out = wires.slot(0)
        for k in order:
            W.sx[k] = send(block(W, W.g, zdev[k] * 2 + (1 - xx)), W.rx.at[k], xpeer, out)
        wires.held.append(wires.copy(out, W.zin, W.rx, W.rx, xpeer).wait_send)

    def sum_block(W, k):
        W.sx[k].wait_recv()
        at = rows_at((zdev[k] * 2 + xx) * W.depth, W.depth, 16)
        v = W.g[:, at, :].astype(f32) + W.rx[k].astype(f32)
        W.zs[k] = v.astype(bf16)
        if k:
            wires.copy(W.zout, W.zin, W.zs.at[k], W.zr.at[k], (zdev[k] * 2 + xx, j)).start()

    def sum_z(W):
        for k in order:
            sum_block(W, k)

    def sum_img(W):
        total = wires.copy(W.zout, W.zin, W.zr.at[0 : Z - 1], W.zr.at[0 : Z - 1], xpeer)
        total.wait_recv()
        wires.held.append(total.wait_send)
        v = W.zs[0].astype(f32)
        for k in range(1, Z):
            v = v + W.zr[k].astype(f32)
        to_rows(W, jnp.concatenate([v[t] for t in range(W.wide)], axis=1))

    def to_rows(W, v):
        for t in range(W.wide):
            W.fin[t] = v[:, t * B : (t + 1) * B].astype(bf16)
        W.simg = group(
            [
                (W.fin.at[:, rows_at(device[1] * W.rows, W.rows, 16), :], W.gr.at[j], device)
                for device in img_peers
            ],
            W.gr.at[0 : J - 1],
        )
        W.gr[j] = W.fin[:, rows_at(j * W.rows, W.rows, 16), :]

    def sum_end(W, target):
        W.simg.wait_recv()
        for k in range(J):
            for t in range(W.wide):
                target[:, t * C + k * B : t * C + (k + 1) * B] = W.gr[k, t].astype(f32)

    dn_done, dn_at = scatter(
        dn_bufs, lambda at, size: jnp.concatenate([s.dqkv[t, pl.ds(at, size), :] for t in range(3)], axis=1), s.WqT
    )
    turn(s.N3, s.N3T, 0)
    for h in range(2):
        at = slice(h * 2 * B, (h + 1) * 2 * B)
        v = mm(s.N3T[at, :], jnp.concatenate([s.dqkv[t] for t in range(3)], axis=1)).astype(bf16)
        for t in range(3):
            wq.g[t, at, :] = v[:, t * B : (t + 1) * B]
    sum_start(wq)
    s.dcx[...] = jnp.concatenate([s.dK[P : P + B, :], s.dV[P : P + B, :]], axis=1).astype(bf16)
    s.dcxs[d] = s.dcx[...]
    dcx_copies = group(
        [(s.dcx.at[0:TP, :], s.dcxs.at[d, 0:TP, :], device) for device in dp_peers],
        s.dcxs.at[0 : N - 1, 0:TP, :],
    )
    for i, state in enumerate(o_states):
        gather_far(state, s.O.at[1 - yy, pl.ds(i * span, span), lanes(cc)])
    for state in o_states:
        gather_near(state)
        gather_end(state)

    def finish(at):
        left = jnp.concatenate([s.O[0, at, :], s.O[1, at, :]], axis=1)
        s.outj[at, :] = (s.y1[at, :] + mm(left, wo.w[0]) + vec(8)).astype(bf16)

    for i in range(P // BIG):
        finish(big(i))

    def to_pixels(source, target):
        copies = group(
            [(source.at[rows_at(device[1] * Q, Q, Q), :], target.at[:, lanes(j)], device) for device in img_peers],
            source.at[0 : P - Q, :],
        )
        target[:, lanes(j)] = source[rows_at(j * Q, Q, Q), :]
        return copies

    out_copies = to_pixels(s.outj, out)
    turn(s.O, s.OT, 0)
    for h in range(2):
        at = slice(h * 2 * B, (h + 1) * 2 * B)
        wo.g[0, at, :] = mm(s.OT[at, :], s.dyj[...]).astype(bf16)
    sum_start(wo)

    def back_sums(grad, normed, factor):
        def one(i, carry):
            v = grad(i)
            return carry[0] + colsum(v), carry[1] + colsum(v * normed(i))
        first, second = each(one, (zero_row, zero_row))
        return first, second, group_sum(first * factor) * (1.0 / count), group_sum(second * factor) * (1.0 / count)

    dn_done()
    sum_z(wq)
    dn_sum, dn_hat, m1, m2 = back_sums(dn_at, xh3, vec(6))

    def shifted(i, v):
        at = rows_at(i * Q + COLS, Q, COLS)
        s.S[0, at, :] = from_right(v).astype(bf16)
        s.S[1, at, :] = v.astype(bf16)
        s.S[2, at, :] = from_left(v).astype(bf16)

    def make_dh2(i, carry):
        dy = s.dyj[px(i), :].astype(f32)
        v = dy + (dn_at(i) * vec(6) - m1 - xh3(i) * m2) * inv3
        s.dy1[px(i), :] = v
        low = v.astype(bf16).astype(f32)
        shifted(i, low)
        return carry[0] + colsum(low), carry[1] + colsum(dy)

    dh2_sum, dy_sum = each(make_dh2, (zero_row, zero_row))

    def tap(t, start, size):
        r, c = t // 3, t % 3
        return s.S[c, rows_at(start + (2 - r) * COLS, size, COLS), :]

    def field(at, size):
        return jnp.concatenate([tap(t, at, size) for t in range(9)], axis=1)

    def kernel_grad(W, turned):
        for h in range(2):
            at = slice(h * 2 * B, (h + 1) * 2 * B)
            v = mm(turned[at, :], jnp.concatenate([tap(t, 0, P) for t in range(9)], axis=1)).astype(bf16)
            for t in range(9):
                W.g[0, t * C + h * 2 * B : t * C + (h + 1) * 2 * B, :] = v[:, t * B : (t + 1) * B]

    da2_done, da2_at = scatter(da2_bufs, field, s.W2T)
    kernel_grad(c2, s.A2T)
    sum_start(c2)
    sum_z(wo)
    ctx_copies.wait_recv()
    dcx_copies.wait_recv()
    v = lax.dot_general(
        s.ctxs[...].reshape(N * B, XN), s.dcxs[...].reshape(N * B, 2 * B), (((0,), (0,)), ((), ())),
        preferred_element_type=f32,
    )
    to_rows(wc, v)
    da2_done()

    def slope_of(v):
        sigma = jax.nn.sigmoid(v)
        return sigma * (1.0 + v * (1.0 - sigma))

    def make_du(i, carry):
        du = da2_at(i) * slope_of(u_of(i))
        s.tmp[px(i), :] = du
        return carry[0] + colsum(du), carry[1] + colsum(du * xh2(i))

    du_sum, du_hat = each(make_du, (zero_row, zero_row))
    gain2 = scale * vec(3)
    m1b = group_sum(du_sum * gain2) * (1.0 / count)
    m2b = group_sum(du_hat * gain2) * (1.0 / count)

    def make_dh1(i, carry):
        v = (s.tmp[px(i), :] * gain2 - m1b - xh2(i) * m2b) * inv2
        low = v.astype(bf16).astype(f32)
        shifted(i, low)
        return carry + colsum(low)

    dh1_sum = each(make_dh1, zero_row)
    dscale = vec(3) * du_hat + vec(4) * du_sum
    kernel_grad(c1, s.A1T)
    sum_start(c1)
    da1_done, da1_at = scatter(da1_bufs, field, s.W1T)
    s.dse[j] = jnp.concatenate([dscale, du_sum], axis=0)
    ds_copies = group([(s.dse.at[j], s.dse.at[j], device) for device in img_peers], s.dse.at[0 : J - 1])
    sum_img(wq)
    sum_img(wo)
    sum_z(c2)
    ds_copies.wait_recv()
    s.dsall[d] = s.dse[...]
    ds_copies = group([(s.dse, s.dsall.at[d], device) for device in dp_peers], s.dsall.at[0 : N - 1])
    sum_block(c1, order[0])
    da1_done()
    mean1, inv1 = s.st1[j, 0:1, :], s.st1[j, 1:2, :]

    def xh1(i):
        return (s.xj[px(i), :].astype(f32) - mean1) * inv1

    def make_dt1(i, carry):
        n1 = xh1(i)
        dt1 = da1_at(i) * slope_of(n1 * vec(0) + vec(1))
        s.tmp[px(i), :] = dt1
        return carry[0] + colsum(dt1), carry[1] + colsum(dt1 * n1)

    dt1_sum, dt1_hat = each(make_dt1, (zero_row, zero_row))
    sum_block(c1, order[1])
    m1c = group_sum(dt1_sum * vec(0)) * (1.0 / count)
    m2c = group_sum(dt1_hat * vec(0)) * (1.0 / count)

    def make_in(i):
        v = s.dy1[px(i), :] + (s.tmp[px(i), :] * vec(0) - m1c - xh1(i) * m2c) * inv1
        s.inj[px(i), :] = v.astype(bf16)

    each(make_in)
    in_copies = to_pixels(s.inj, in_grad)

    qkv_sums = [each(lambda i, a, t=t: a + colsum(s.dqkv[t, px(i), :].astype(f32)), zero_row) for t in range(3)]
    s.gvec[...] = jnp.concatenate(
        [dt1_hat, dt1_sum, dh1_sum, scale * du_hat, scale * du_sum, dh2_sum, dn_hat, dn_sum, dy_sum]
        + qkv_sums
        + [colsum(s.dK[P : P + B, :]), colsum(s.dV[P : P + B, :]), dscale, du_sum],
        axis=0,
    )
    gv_copies = group([(s.gvec, s.gvs.at[d], device) for device in dp_peers], s.gvs.at[0 : N - 1])
    s.gvs[d] = s.gvec[...]
    for k in order[2:]:
        sum_block(c1, k)
    gv_copies.wait_recv()
    total = s.gvs[0]
    for k in range(1, N):
        total = total + s.gvs[k]
    s.gvt[...] = total
    s.gvi[j] = total
    gv_copies = group([(s.gvt, s.gvi.at[j], device) for device in img_peers], s.gvi.at[0 : J - 1])
    sum_img(c2)
    sum_img(c1)
    sum_end(wq, g_q)
    sum_end(wc, g_c)
    sum_end(wo, g_o)
    ds_copies.wait_recv()
    e_cols = jnp.concatenate([s.eall[k, :, e_at] for k in range(N)], axis=0)
    for t in range(2):
        for k in range(J):
            rows = jnp.concatenate([s.dsall[i, k, t : t + 1, :] for i in range(N)], axis=0)
            v = lax.dot_general(
                e_cols, rows, (((0,), (0,)), ((), ())), precision=highest, preferred_element_type=f32
            )
            s.geb[:, t * C + k * B : t * C + (k + 1) * B] = v
    g_emb[...] = s.geb[rows_at(lax.rem(flat, 2) * RE, RE, 8), :]
    gv_copies.wait_recv()
    VW = g.VW
    each_block = B // VW
    pick = lax.broadcasted_iota(jnp.int32, (B, VW), 0) == (
        lax.broadcasted_iota(jnp.int32, (B, VW), 1) + lax.rem(flat, each_block) * VW
    )
    g_v[...] = jnp.dot(
        s.gvi[lax.div(flat, each_block)], jnp.where(pick, 1.0, 0.0), precision=highest,
        preferred_element_type=f32,
    )
    sum_end(c2, gc2)
    sum_end(c1, gc1)
    out_copies.wait_recv()
    in_copies.wait_recv()
    wires.drain()
    assert wires.used[0] <= g.copies[0] and wires.used[1] <= g.copies[1], wires.used


def hand_over(*refs):
    count = len(refs) // 2
    for k in range(count):
        refs[count + k][...] = refs[k][...].astype(refs[count + k].dtype)


def fused(
    image, cond, context, w_conv1, w_conv2, w_embed, w_qkv, w_context, w_out, vectors, cotangent
):
    J, N = lax.axis_size("img"), lax.axis_size("dp")
    local, cols, chans = image.shape[1:]
    g = types.SimpleNamespace(
        P=local * cols * J, Q=local * cols, C=chans, B=chans // J, N=N, J=J, COLS=cols, SIZE=chans // GROUPS,
        T=context.shape[1], X=context.shape[2], E=cond.shape[1], RE=w_embed.shape[0], VW=vectors.shape[1],
        HEAD=HEAD, FACTOR=HEAD ** (-0.5),
        weights=[
            (1, w_conv1.shape[0]), (1, w_conv2.shape[0]), (3, w_qkv.shape[0]), (2, w_context.shape[0]),
            (1, w_out.shape[0]),
        ],
    )
    groups = scratch_plan(g)
    rows = local * cols
    shape = jax.ShapeDtypeStruct
    outs = [
        shape((rows, chans), bf16), shape((rows, chans), bf16), shape(w_conv1.shape, f32), shape(w_conv2.shape, f32),
        shape(w_embed.shape, f32), shape(w_qkv.shape, f32), shape(w_context.shape, f32), shape(w_out.shape, f32),
        shape(vectors.shape, f32),
    ]
    g.copies = (91, 67 + 12 * (N // 2 + 1))
    vmem = pl.BlockSpec(memory_space=pltpu.VMEM)
    result = pl.pallas_call(
        functools.partial(body, g, groups),
        out_shape=outs,
        in_specs=[vmem] * 11,
        out_specs=[vmem] * 9,
        scratch_shapes=[pltpu.VMEM(*spec) for group in groups for spec in group.values()]
        + [pltpu.SemaphoreType.DMA((count,)) for count in g.copies],
        compiler_params=pltpu.CompilerParams(
            collective_id=0, has_side_effects=True, vmem_limit_bytes=60 * 1024 * 1024
        ),
    )(
        image.reshape(rows, chans), cond, context[0], w_conv1, w_conv2, w_embed, w_qkv, w_context, w_out, vectors,
        cotangent.reshape(rows, chans),
    )
    count = len(outs)
    result = pl.pallas_call(
        hand_over, out_shape=outs, in_specs=[vmem] * count, out_specs=[vmem] * count,
    )(*result)
    return (result[0].reshape(image.shape), result[1].reshape(image.shape), *result[2:])


def on_device(
    image, cond, context, w_conv1, w_conv2, w_embed, w_qkv, w_context, w_out, vectors, cotangent
):
    parts = lax.axis_size("img")
    place = lax.axis_index("img")
    images = lax.axis_size("dp")
    rows, cols, chans = image.shape[1] * parts, image.shape[2], image.shape[3]
    pixels = rows * cols
    width = chans // parts
    size = chans // GROUPS
    count = images * parts

    if parts == 4 and width == 128 and images % 2 == 0 and all(
        w.shape[0] % 16 == 0 for w in (w_conv1, w_conv2, w_embed, w_qkv, w_context, w_out)
    ):
        return fused(
            image, cond, context, w_conv1, w_conv2, w_embed, w_qkv, w_context, w_out, vectors, cotangent
        )

    def own(full):
        return lax.dynamic_slice_in_dim(full, place * width, width, full.ndim - 1)

    shards = (w_conv1, w_conv2, w_qkv, w_context, w_embed, w_out)
    lengths = [w.shape[0] * (w.shape[1] // chans) for w in shards]
    packed = jnp.concatenate([columns(w, parts) for w in shards], 1)
    packed = lax.all_to_all(packed, "img", 0, 0, tiled=True)
    packed = lax.all_gather(packed, "dp", axis=0, tiled=True)
    full = []
    start = 0
    for w, length in zip(shards, lengths):
        wide = w.shape[1] // chans
        piece = packed[:, start : start + length].reshape(count, wide, w.shape[0], width)
        full.append(piece.transpose(0, 2, 1, 3).reshape(count * w.shape[0], wide * width))
        start += length
    k1, k2, kq, kc, ke, ko = full
    vec_all = lax.all_gather(vectors, ("dp", "img"), axis=1, tiled=True).astype(f32)
    vec = own(vec_all)

    x_low = lax.all_gather(image[0].reshape(-1, chans), "img", axis=0, tiled=True)
    x_all = x_low.astype(f32)
    normed1_all, inverse1_all = group_norm(x_all, size)
    act1 = jax.nn.silu(normed1_all * vec_all[0] + vec_all[1]).astype(bf16)
    normed1 = own(normed1_all)
    inverse1 = lax.dynamic_slice_in_dim(inverse1_all, place * (GROUPS // parts), GROUPS // parts, 1)
    pre1 = normed1 * vec[0] + vec[1]
    hidden1 = dot(taps_of(act1, rows, cols, False), k1) + vec[2]
    cond_act = jax.nn.silu(cond.astype(f32)).astype(bf16)
    embed = dot(cond_act, ke)[0]
    scale = embed[:width] + vec[14]
    shift = embed[width:] + vec[15]
    normed2, inverse2 = group_norm(hidden1, size)
    affine2 = normed2 * vec[3] + vec[4]
    pre2 = affine2 * (1.0 + scale) + shift
    act2_own = jax.nn.silu(pre2).astype(bf16)
    act2 = lax.all_gather(act2_own, "img", axis=1, tiled=True)
    resid = own(x_all) + dot(taps_of(act2, rows, cols, False), k2) + vec[5]
    normed3, inverse3 = group_norm(resid, size)
    affine3_own = (normed3 * vec[6] + vec[7]).astype(bf16)
    affine3 = lax.all_gather(affine3_own, "img", axis=1, tiled=True)
    qkv = (dot(affine3, kq) + jnp.concatenate([vec[9], vec[10], vec[11]])).astype(bf16)
    ctx = (dot(context[0], kc) + jnp.concatenate([vec[12], vec[13]])).astype(bf16)
    tokens = ctx.shape[0]

    out_full = lax.all_gather(ko, "img", axis=1, tiled=True)
    dy_px = cotangent[0].reshape(-1, chans)
    do_px = lax.dot_general(dy_px, out_full, (((1,), (1,)), ((), ())), preferred_element_type=f32).astype(bf16)
    both = jnp.stack([do_px, dy_px])
    both = lax.all_to_all(both, "img", 2, 1, tiled=True)
    do, dy = both[0], both[1]
    dy_wide = dy.astype(f32)

    keys = jnp.concatenate([ctx[:, :width], qkv[:, width : 2 * width]], 0)
    values = jnp.concatenate([ctx[:, width:], qkv[:, 2 * width :]], 0)
    factor = HEAD ** (-0.5)
    mixed, dq, dk, dv = [], [], [], []
    for h in range(width // HEAD):
        at = slice(h * HEAD, (h + 1) * HEAD)
        q_h, k_h, v_h, do_h = qkv[:, at], keys[:, at], values[:, at], do[:, at]
        scores = dot(k_h, q_h.T) * factor
        top = jnp.max(scores, 0, keepdims=True)
        weights = jnp.exp(scores - top)
        probs = weights / jnp.sum(weights, 0, keepdims=True)
        low = probs.astype(bf16)
        mixed.append(dot(v_h.T, low).T)
        dv.append(dot(low, do_h))
        dp = dot(v_h, do_h.T)
        ds = (probs * (dp - jnp.sum(dp * probs, 0, keepdims=True))).astype(bf16)
        dq.append(dot(k_h.T, ds).T * factor)
        dk.append(dot(ds, q_h) * factor)
    mixed = jnp.concatenate(mixed, 1).astype(bf16)
    dq, dk, dv = (jnp.concatenate(v, 1) for v in (dq, dk, dv))
    mixed_all = lax.all_gather(mixed, "img", axis=1, tiled=True)
    output = (resid + dot(mixed_all, ko) + vec[8]).astype(bf16)

    dqkv = jnp.concatenate([dq, dk[tokens:], dv[tokens:]], 1).astype(bf16)
    dctx = jnp.concatenate([dk[:tokens], dv[:tokens]], 1)
    dn_part = lax.dot_general(dqkv, kq, (((1,), (1,)), ((), ())), preferred_element_type=f32)
    dn = lax.psum_scatter(dn_part.astype(bf16), "img", scatter_dimension=1, tiled=True).astype(f32)
    dy1 = dy_wide + group_back(dn * vec[6], normed3, inverse3, size)
    dh2 = dy1.astype(bf16)

    def turned(kernel):
        return kernel.reshape(9, chans, width).transpose(0, 2, 1).reshape(9 * width, chans)

    def conv_back(dh, kernel, act):
        field = taps_of(dh, rows, cols, True)
        part = dot(field, turned(kernel)).astype(bf16)
        grad = lax.psum_scatter(part, "img", scatter_dimension=1, tiled=True).astype(f32)
        kernel_grad = lax.dot_general(act, field, (((0,), (0,)), ((), ())), preferred_element_type=f32)
        return grad, kernel_grad.reshape(chans, 9, width).transpose(1, 0, 2).reshape(9 * chans, width)

    da2, gk2 = conv_back(dh2, k2, act2)
    du = da2 * silu_slope(pre2)
    dscale = jnp.sum(du * affine2, 0)
    dshift = jnp.sum(du, 0)
    dz = du * (1.0 + scale)
    dh1 = group_back(dz * vec[3], normed2, inverse2, size).astype(bf16)
    da1, gk1 = conv_back(dh1, k1, act1)
    dt1 = da1 * silu_slope(pre1)
    in_grad = (dy1 + group_back(dt1 * vec[0], normed1, inverse1, size)).astype(bf16)

    tops = lax.all_to_all(jnp.stack([output, in_grad]), "img", 1, 2, tiled=True)
    gkq = lax.dot_general(affine3, dqkv, (((0,), (0,)), ((), ())), preferred_element_type=f32)
    gkc = lax.dot_general(context[0], dctx.astype(bf16), (((0,), (0,)), ((), ())), preferred_element_type=f32)
    gko = lax.dot_general(mixed_all, dy, (((0,), (0,)), ((), ())), preferred_element_type=f32)
    gke = cond_act[0].astype(f32)[:, None] * jnp.concatenate([dscale, dshift])[None, :]
    grad_vec = jnp.stack(
        [
            jnp.sum(dt1 * normed1, 0),
            jnp.sum(dt1, 0),
            jnp.sum(dh1.astype(f32), 0),
            jnp.sum(dz * normed2, 0),
            jnp.sum(dz, 0),
            jnp.sum(dh2.astype(f32), 0),
            jnp.sum(dn * normed3, 0),
            jnp.sum(dn, 0),
            jnp.sum(dy_wide, 0),
        ]
        + [jnp.sum(v.astype(f32), 0) for v in jnp.split(dqkv, 3, 1)]
        + [jnp.sum(v, 0) for v in jnp.split(dctx, 2, 1)]
        + [dscale, dshift],
        0,
    )
    grads = (gk1, gk2, gkq, gkc, gke, gko)
    pieces = []
    for w, g in zip(shards, grads):
        wide = w.shape[1] // chans
        piece = g.reshape(count, w.shape[0], wide, width).transpose(0, 2, 1, 3)
        pieces.append(piece.reshape(count, wide * w.shape[0], width))
    packed = jnp.concatenate(pieces, 1).astype(bf16)
    packed = lax.psum_scatter(packed, "dp", scatter_dimension=0, tiled=True).astype(f32)
    packed = lax.all_to_all(packed.astype(bf16), "img", 0, 0, tiled=True).astype(f32)
    outs = []
    start = 0
    for w, length in zip(shards, lengths):
        wide = w.shape[1] // chans
        piece = packed[:, start : start + length].reshape(parts, wide, w.shape[0], width)
        outs.append(piece.transpose(2, 1, 0, 3).reshape(w.shape))
        start += length
    vec_sum = lax.all_gather(lax.psum(grad_vec, "dp"), "img", axis=1, tiled=True)
    each = chans // count
    g_vec = lax.dynamic_slice_in_dim(
        vec_sum, (lax.axis_index("dp") * parts + place) * each, each, 1
    )
    g1, g2, gq, gc, ge, go = outs
    return (tops[0].reshape(image.shape), tops[1].reshape(image.shape), g1, g2, ge, gq, gc, go, g_vec)


def solution(mesh):
    whole = P(("dp", "img"), None)
    field = P("dp", "img", None, None)
    in_specs = (
        field, P("dp", None), P("dp", None, None), whole, whole, whole, whole, whole, whole,
        P(None, ("dp", "img")), field,
    )
    out_specs = (field, field, whole, whole, whole, whole, whole, whole, P(None, ("dp", "img")))
    return jax.shard_map(
        on_device, mesh=mesh, in_specs=in_specs, out_specs=out_specs, check_vma=False
    )
```
